768 devices in a mesh: wide: 192 (over y, x_hi, z), narrow: 4 (over x_lo, core).
Axes of the slice: x: 4 (x_hi: 2, x_lo: 2; x = x_hi * 2 + x_lo), y: 8, z: 12, core: 2. Of those that a mesh axis runs over, the one named last changes fastest.
Arguments:
- load: float32 [49152, 512], P(('wide', 'narrow')), may hold values from -48 to 48
- geom: bfloat16 [7, 49152, 512], P(None, ('wide', 'narrow')), may hold values from -0.15 to 3, as said below
- element_order: int32 [192, 4, 64], P('wide', 'narrow'), may hold values from 0 to 63, each once within a row
Outputs:
- solution: float32 [49152, 512], P(('wide', 'narrow'))
- residual: float32 [49152, 512], P(('wide', 'narrow'))
The draws below stay inside these ranges and needn't reach their ends.
Inputs may be any that keep to these rules, and one draw needn't show every extreme that they name: `geom`: at every point G0, G1, G2 and G6 are positive and |G3|, |G4|, |G5| stay below 0.15. `element_order`: each device's list names each of its 64 block positions exactly once.
All inputs are finite; a program needn't handle non-finite values.
Results may differ from the reference program's by a relative error of at most 0.02.
Values sent between devices are 32-bit elements; how exact they have to be, the bound alone decides.
No kernel may reach another device: no remote copies, remote signals or barrier semaphores. Data moves between devices by JAX's collectives and lax.ppermute only.
A program may use at most 64 MiB of HBM per device.

```python
import math
import jax
import jax.numpy as jnp
import numpy as np
from jax import lax

EZ = 1
EA = 4
ER = 16
CHEB = 3
ITERS = 2
E_DEV = 64
ELEMS = 49152
N_WIDE = 192
N_NARROW = 4


def draw_load(key, part):
    key = jax.random.fold_in(key, 11)
    device = jnp.arange(ELEMS, dtype=jnp.int32) // E_DEV
    wide_index = device // N_NARROW
    narrow_index = device % N_NARROW
    smooth_wide = jax.random.uniform(jax.random.fold_in(key, 4), (N_WIDE,), jnp.float32, minval=0.0, maxval=math.log(4.0))
    smooth_narrow = jax.random.uniform(jax.random.fold_in(key, 5), (N_NARROW,), jnp.float32, minval=0.0, maxval=math.log(4.0))
    rough_wide = jax.random.uniform(jax.random.fold_in(key, 6), (N_WIDE,), jnp.float32, minval=0.0, maxval=math.log(2.0))
    rough_narrow = jax.random.uniform(jax.random.fold_in(key, 7), (N_NARROW,), jnp.float32, minval=0.0, maxval=math.log(2.0))
    rise = 1.0 + 2.0 * wide_index.astype(jnp.float32) / max(N_WIDE - 1, 1)
    smooth_level = 0.4 * jnp.exp(smooth_wide[wide_index] + smooth_narrow[narrow_index])
    rough_level = 0.5 * jnp.exp(rough_wide[wide_index] + rough_narrow[narrow_index]) * rise
    point = jnp.arange(512, dtype=jnp.int32)
    node_i = point // 64
    node_j = point // 8 % 8
    node_k = point % 8
    half_i = jnp.where((node_i == 0) | (node_i == 7), 0.5, 1.0)
    half_j = jnp.where((node_j == 0) | (node_j == 7), 0.5, 1.0)
    half_k = jnp.where((node_k == 0) | (node_k == 7), 0.5, 1.0)
    pattern = (half_i * half_j * half_k).astype(jnp.float32)
    smooth = smooth_level[:, None] * pattern[None, :]
    rough = jnp.clip(jax.random.normal(jax.random.fold_in(key, 3), (ELEMS, 512), jnp.float32), -6.0, 6.0)
    return (smooth + rough_level[:, None] * rough).astype(jnp.float32)


def draw_geom(key, part):
    key = jax.random.fold_in(key, 23)
    shape = (ELEMS, 512)
    diagonal = jnp.exp(jax.random.uniform(jax.random.fold_in(key, 2), (3,) + shape, jnp.float32, minval=math.log(0.5), maxval=math.log(2.0)))
    cross = jax.random.uniform(jax.random.fold_in(key, 3), (3,) + shape, jnp.float32, minval=-0.14, maxval=0.14)
    screen = jnp.exp(jax.random.uniform(jax.random.fold_in(key, 4), (1,) + shape, jnp.float32, minval=math.log(0.25), maxval=math.log(2.5)))
    return jnp.concatenate([diagonal, cross, screen], axis=0).astype(jnp.bfloat16)


def setup_inputs(seed: int = 0) -> dict:
    key_list = jax.random.split(jax.random.key(seed), 4)
    return {
        "load": draw_load(jax.random.fold_in(key_list[3], 71), 0),
        "geom": draw_geom(jax.random.fold_in(key_list[3], 71), 0),
        "element_order": jax.vmap(lambda own: jax.random.permutation(own, E_DEV))(jax.random.split(key_list[2], N_WIDE * N_NARROW)).reshape((N_WIDE, N_NARROW, E_DEV)).astype(jnp.int32),
    }


interval_low = 0.03
interval_high = 1.0


def legendre_seven(point):
    before = 1.0
    current = point
    for degree in range(1, 7):
        after = ((2.0 * degree + 1.0) * point * current - degree * before) / (degree + 1.0)
        before = current
        current = after
    return current


def gll_derivative():
    points = 8
    inner_nodes = [-0.8717401485096066, -0.5917001814331423, -0.2092992179024789, 0.2092992179024789, 0.5917001814331423, 0.8717401485096066]
    nodes = [-1.0] + inner_nodes + [1.0]
    values_at = [legendre_seven(node) for node in nodes]
    matrix = np.zeros((points, points))
    for source in range(points):
        for target in range(points):
            if source != target:
                matrix[source, target] = values_at[source] / (values_at[target] * (nodes[source] - nodes[target]))
    matrix[0, 0] = -(points - 1) * points / 4.0
    matrix[points - 1, points - 1] = (points - 1) * points / 4.0
    return matrix


def gradients(field, derivative):
    pipe_len, cycle_len, radial_len = field.shape
    blocks = field.reshape(pipe_len // 8, 8, cycle_len // 8, 8, radial_len // 8, 8)
    highest = lax.Precision.HIGHEST
    grad_z = jnp.einsum("im,pmqjsk->piqjsk", derivative, blocks, precision=highest)
    grad_a = jnp.einsum("jm,piqmsk->piqjsk", derivative, blocks, precision=highest)
    grad_r = jnp.einsum("km,piqjsm->piqjsk", derivative, blocks, precision=highest)
    return grad_z.reshape(field.shape), grad_a.reshape(field.shape), grad_r.reshape(field.shape)


def divergence(flux_z, flux_a, flux_r, derivative):
    pipe_len, cycle_len, radial_len = flux_z.shape
    shape6 = (pipe_len // 8, 8, cycle_len // 8, 8, radial_len // 8, 8)
    highest = lax.Precision.HIGHEST
    part_z = jnp.einsum("mi,pmqjsk->piqjsk", derivative, flux_z.reshape(shape6), precision=highest)
    part_a = jnp.einsum("mj,piqmsk->piqjsk", derivative, flux_a.reshape(shape6), precision=highest)
    part_r = jnp.einsum("mk,piqjsm->piqjsk", derivative, flux_r.reshape(shape6), precision=highest)
    return (part_z + part_a + part_r).reshape(flux_z.shape)


def element_apply(field, metric, derivative):
    grad_z, grad_a, grad_r = gradients(field, derivative)
    g_zz = metric[0].astype(jnp.float32)
    g_aa = metric[1].astype(jnp.float32)
    g_rr = metric[2].astype(jnp.float32)
    g_za = metric[3].astype(jnp.float32)
    g_zr = metric[4].astype(jnp.float32)
    g_ar = metric[5].astype(jnp.float32)
    flux_z = g_zz * grad_z + g_za * grad_a + g_zr * grad_r
    flux_a = g_za * grad_z + g_aa * grad_a + g_ar * grad_r
    flux_r = g_zr * grad_z + g_ar * grad_a + g_rr * grad_r
    return divergence(flux_z, flux_a, flux_r, derivative) + metric[6].astype(jnp.float32) * field


def element_bound(metric, derivative):
    pipe_len, cycle_len, radial_len = metric.shape[1:]
    absolute = jnp.abs(derivative)
    row_total = jnp.sum(absolute, axis=1)
    q_z = jnp.tile(row_total, pipe_len // 8)[:, None, None]
    q_a = jnp.tile(row_total, cycle_len // 8)[None, :, None]
    q_r = jnp.tile(row_total, radial_len // 8)[None, None, :]
    g_abs = jnp.abs(metric.astype(jnp.float32))
    h_z = g_abs[0] * q_z + g_abs[3] * q_a + g_abs[4] * q_r
    h_a = g_abs[3] * q_z + g_abs[1] * q_a + g_abs[5] * q_r
    h_r = g_abs[4] * q_z + g_abs[5] * q_a + g_abs[2] * q_r
    return divergence(h_z, h_a, h_r, absolute) + g_abs[6]


def pair_sum(padded, axis):
    length = padded.shape[axis] - 2
    core = lax.slice_in_dim(padded, 1, length + 1, axis=axis)
    upper = lax.slice_in_dim(padded, 2, length + 2, axis=axis)
    lower = lax.slice_in_dim(padded, 0, length, axis=axis)
    node = lax.broadcasted_iota(jnp.int32, core.shape, axis) % 8
    return core + jnp.where(node == 7, upper, 0.0) + jnp.where(node == 0, lower, 0.0)


def point_weight(pipe_len, cycle_len, radial_len):
    one = jnp.float32(1.0)
    two = jnp.float32(2.0)
    pipe_node = jnp.arange(pipe_len) % 8
    cycle_node = jnp.arange(cycle_len) % 8
    radial_index = jnp.arange(radial_len)
    radial_node = radial_index % 8
    count_z = jnp.where((pipe_node == 0) | (pipe_node == 7), two, one)
    count_a = jnp.where((cycle_node == 0) | (cycle_node == 7), two, one)
    inside = (radial_index > 0) & (radial_index < radial_len - 1)
    count_r = jnp.where(((radial_node == 0) | (radial_node == 7)) & inside, two, one)
    return one / (count_z[:, None, None] * count_a[None, :, None] * count_r[None, None, :])


def reference(load, geom, element_order):
    derivative = jnp.asarray(gll_derivative(), dtype=jnp.float32)
    device_base = (jnp.arange(N_WIDE * N_NARROW, dtype=jnp.int32) * E_DEV).reshape(N_WIDE, N_NARROW, 1)
    inverse = jnp.argsort(element_order, axis=-1).astype(jnp.int32)
    flat_inverse = (inverse + device_base).reshape(-1)
    flat_order = (element_order.astype(jnp.int32) + device_base).reshape(-1)
    pipe_len = EZ * 8
    cycle_len = N_NARROW * EA * 8
    radial_len = ER * 8

    placed = jnp.take(load, flat_inverse, axis=0)
    load_grid = placed.reshape(N_WIDE, N_NARROW, EZ, EA, ER, 8, 8, 8).transpose(0, 2, 5, 1, 3, 6, 4, 7)
    load_grid = load_grid.reshape(N_WIDE, pipe_len, cycle_len, radial_len)
    placed_geom = jnp.take(geom, flat_inverse, axis=1)
    metric = placed_geom.reshape(7, N_WIDE, N_NARROW, EZ, EA, ER, 8, 8, 8).transpose(1, 0, 3, 6, 2, 4, 7, 5, 8)
    metric = metric.reshape(N_WIDE, 7, pipe_len, cycle_len, radial_len)

    def assemble(blocks):
        whole = blocks.reshape(N_WIDE * pipe_len, cycle_len, radial_len)
        padded = jnp.pad(whole, ((1, 1), (1, 1), (0, 0)), mode="wrap")
        merged = pair_sum(pair_sum(padded, 0), 1)
        radial = jnp.pad(merged, ((0, 0), (0, 0), (1, 1)))
        return pair_sum(radial, 2).reshape(blocks.shape)

    def operator(blocks):
        local = lax.map(lambda pair: element_apply(pair[0], pair[1], derivative), (blocks, metric))
        return assemble(local)

    bound = assemble(lax.map(lambda block: element_bound(block, derivative), metric))
    bound_inverse = 1.0 / bound
    weight = point_weight(pipe_len, cycle_len, radial_len)[None]

    def inner(first_field, second_field):
        return jnp.sum(first_field * second_field * weight)

    center = (interval_high + interval_low) / 2.0
    half_width = (interval_high - interval_low) / 2.0
    sigma_ratio = center / half_width

    def precondition(res):
        rho_now = 1.0 / sigma_ratio
        update = res * bound_inverse / center
        result = update
        for degree_step in range(CHEB - 1):
            rho_next = 1.0 / (2.0 * sigma_ratio - rho_now)
            update = rho_next * rho_now * update + (2.0 * rho_next / half_width) * bound_inverse * (res - operator(result))
            result = result + update
            rho_now = rho_next
        return result

    grid_residual = assemble(load_grid)
    grid_solution = jnp.zeros_like(grid_residual)
    direction = grid_residual
    previous = jnp.float32(1.0)
    for iteration in range(ITERS):
        smoothed = precondition(grid_residual)
        precond_norm = inner(grid_residual, smoothed)
        if iteration == 0:
            direction = smoothed
        else:
            direction = smoothed + (precond_norm / previous) * direction
        image = operator(direction)
        step_size = precond_norm / inner(direction, image)
        grid_solution = grid_solution + step_size * direction
        grid_residual = grid_residual - step_size * image
        previous = precond_norm

    def read_back(blocks):
        rows = blocks.reshape(N_WIDE, EZ, 8, N_NARROW, EA, 8, ER, 8).transpose(0, 3, 1, 4, 6, 2, 5, 7)
        return jnp.take(rows.reshape(ELEMS, 512), flat_order, axis=0)

    return read_back(grid_solution), read_back(grid_residual)
```

```python
import functools

import jax
import jax.numpy as jnp
import ml_dtypes
import numpy as np
from jax import lax
from jax.experimental import pallas as pl
from jax.experimental.pallas import tpu as pltpu
from jax.sharding import PartitionSpec as P

NODES = 8
ROWS = 32
LANES = 128
HALF = 16
INTERVAL_LOW = 0.03
INTERVAL_HIGH = 1.0
FIELD = (NODES, ROWS, LANES)
WIDE = ("outer", "ring")
REST = ("outer", "narrow")


def legendre_seven(point):
    before = 1.0
    current = point
    for degree in range(1, 7):
        after = ((2.0 * degree + 1.0) * point * current - degree * before) / (degree + 1.0)
        before = current
        current = after
    return current


def gll_derivative():
    points = 8
    inner_nodes = [
        -0.8717401485096066,
        -0.5917001814331423,
        -0.2092992179024789,
        0.2092992179024789,
        0.5917001814331423,
        0.8717401485096066,
    ]
    nodes = [-1.0] + inner_nodes + [1.0]
    values_at = [legendre_seven(node) for node in nodes]
    matrix = np.zeros((points, points))
    for source in range(points):
        for target in range(points):
            if source != target:
                matrix[source, target] = values_at[source] / (
                    values_at[target] * (nodes[source] - nodes[target])
                )
    matrix[0, 0] = -(points - 1) * points / 4.0
    matrix[points - 1, points - 1] = (points - 1) * points / 4.0
    return matrix


DERIV = gll_derivative().astype(np.float32)
ABS_DERIV = np.abs(DERIV)
ROW_TOTAL = ABS_DERIV.sum(axis=1)
EYE8 = np.eye(8, dtype=np.float32)


def cycle_matrix(small):
    return np.kron(np.eye(2, dtype=np.float32), np.kron(small, EYE8))


def radial_matrix(small):
    return np.kron(np.eye(16, dtype=np.float32), small)


def split_const(matrix):
    high = matrix.astype(ml_dtypes.bfloat16)
    low = (matrix - high.astype(np.float32)).astype(ml_dtypes.bfloat16)
    return high, low


GRAD = np.concatenate([cycle_matrix(DERIV.T), radial_matrix(DERIV.T)], axis=1)
DIVER = np.concatenate([cycle_matrix(DERIV), radial_matrix(DERIV)], axis=0)
GRAD_HL = np.stack(split_const(GRAD))
DIVER_HL = np.stack(split_const(DIVER))
ABS_HL = np.stack(split_const(np.abs(DIVER)))


def split(value):
    high = value.astype(jnp.bfloat16)
    return high, (value - high.astype(jnp.float32)).astype(jnp.bfloat16)


def dot(left, right):
    return lax.dot_general(
        left, right, (((1,), (0,)), ((), ())), preferred_element_type=jnp.float32
    )


def dot_split(value, matrix_ref):
    high, low = split(value)
    return dot(high, matrix_ref[0]) + (dot(low, matrix_ref[0]) + dot(high, matrix_ref[1]))


def lane_iota(rows):
    return lax.broadcasted_iota(jnp.int32, (rows, LANES), 1)


def row_iota(rows):
    return lax.broadcasted_iota(jnp.int32, (rows, LANES), 0)


def roll(value, shift, axis):
    size = value.shape[axis]
    return pltpu.roll(value, shift % size, axis)


def along_nodes(values, small):
    out = []
    for m in range(NODES):
        total = None
        for i in range(NODES):
            scale = float(small[m][i])
            if scale != 0.0:
                term = values[i] * scale
                total = term if total is None else total + term
        out.append(total)
    return out


def own_assembly(u):
    lane = lane_iota(ROWS)
    k = lane % 8
    er = row_iota(ROWS) % HALF
    up = roll(roll(u, -1, 0), 7, 1)
    down = roll(roll(u, 1, 0), -7, 1)
    u = (
        u
        + jnp.where((k == 7) & (er < HALF - 1), up, 0.0)
        + jnp.where((k == 0) & (er > 0), down, 0.0)
    )
    top, bottom = u[:HALF], u[HALF:]
    lane = lane_iota(HALF)
    j = (lane // 8) % 8
    block = lane // 64
    new_top = (
        top
        + jnp.where(j == 7, roll(bottom, 56, 1), 0.0)
        + jnp.where((j == 0) & (block == 1), roll(bottom, 8, 1), 0.0)
    )
    new_bottom = (
        bottom
        + jnp.where(j == 0, roll(top, -56, 1), 0.0)
        + jnp.where((j == 7) & (block == 0), roll(top, -8, 1), 0.0)
    )
    return new_top, new_bottom


def ends(value):
    lane = lane_iota(HALF)
    return jnp.where(lane < 8, value[:HALF], jnp.where(lane >= 120, value[HALF:], 0.0))


def store_assembled(kv_ref, near_ref, far_ref, pack_ref, even, source, field=0):
    pack = None
    for i in range(NODES):
        top, bottom = own_assembly(source(i))
        value = jnp.concatenate([top, bottom], axis=0)
        kv_ref[i] = value
        if i == 0:
            first = value
        last = value
        piece = ends(value)
        if i:
            piece = roll(piece, 16 * i, 1)
        pack = piece if pack is None else pack + piece
    near_ref[field] = jnp.where(even, last, first)
    far_ref[field] = jnp.where(even, first, last)
    pack_ref[field] = pack


def is_even(place_ref):
    return lax.broadcast_in_dim(place_ref[0], (ROWS, LANES), ()) == 0


def pack_kernel(place_ref, pack_in, near_ref, far_ref, pack_ref):
    even = is_even(place_ref)
    for field in range(pack_ref.shape[0]):
        near, far = near_ref[field], far_ref[field]
        first = ends(jnp.where(even, far, near))
        last = ends(jnp.where(even, near, far))
        pack_ref[field] = pack_in[field] + first + roll(last, 16 * (NODES - 1), 1)


def completed(place_ref, kv, halo, field=0):
    near_ref, far_ref, packs_ref = halo
    even = is_even(place_ref)
    near, far = near_ref[field], far_ref[field]
    count = packs_ref.shape[0]
    here = place_ref[1]
    left = packs_ref[lax.rem(here + count - 1, count), field]
    right = packs_ref[lax.rem(here + 1, count), field]
    lane = lane_iota(HALF)
    side = jnp.where(lane % 16 < 8, roll(left, 8, 1), roll(right, -8, 1))

    def value(i):
        piece = roll(side, -16 * i, 1) if i else side
        u = kv[i] + jnp.concatenate(
            [jnp.where(lane < 8, piece, 0.0), jnp.where(lane >= 120, piece, 0.0)], axis=0
        )
        if i == 0:
            u = u + jnp.where(even, far, near)
        if i == NODES - 1:
            u = u + jnp.where(even, near, far)
        return u

    return value


def apply_element(v_ref, metric_ref, grad_ref, diver_ref, flux_ref, out_ref):
    side = dot_split(v_ref[...].reshape(NODES * ROWS, LANES), grad_ref)
    flux_ref[0] = side[:, :LANES]
    flux_ref[1] = side[:, LANES:]
    for chunk in range(ROWS // 8):
        rows = pl.ds(chunk * 8, 8)
        values = [v_ref[i, rows] for i in range(NODES)]
        grad_z = along_nodes(values, DERIV)
        flux_z = []
        for i in range(NODES):
            at = pl.ds(i * ROWS + chunk * 8, 8)
            g_z, g_a, g_r = grad_z[i], flux_ref[0, at], flux_ref[1, at]
            m = [metric_ref[c, i, rows] for c in range(6)]
            flux_z.append(m[0] * g_z + m[3] * g_a + m[4] * g_r)
            flux_ref[0, at] = m[3] * g_z + m[1] * g_a + m[5] * g_r
            flux_ref[1, at] = m[4] * g_z + m[5] * g_a + m[2] * g_r
        part_z = along_nodes(flux_z, DERIV.T)
        for i in range(NODES):
            out_ref[i, rows] = part_z[i] + metric_ref[6, i, rows] * values[i]
    flux = jnp.concatenate([flux_ref[0], flux_ref[1]], axis=1)
    out_ref[...] += dot_split(flux, diver_ref).reshape(FIELD)


def weight_plane():
    lane, row = lane_iota(ROWS), row_iota(ROWS)
    j, k, er = (lane // 8) % 8, lane % 8, row % HALF
    w_a = jnp.where((j == 0) | (j == 7), 0.5, 1.0)
    shared = ((k == 0) & (er > 0)) | ((k == 7) & (er < HALF - 1))
    return w_a * jnp.where(shared, 0.5, 1.0)


def node_weight(i):
    return 0.5 if i in (0, NODES - 1) else 1.0


def sum_row(sums):
    lane = lane_iota(1)
    row = jnp.zeros((1, LANES), jnp.float32)
    for d, value in enumerate(sums):
        row = jnp.where(lane == d, jnp.sum(value), row)
    return row


SIGMA = ((INTERVAL_HIGH + INTERVAL_LOW) / 2.0) / ((INTERVAL_HIGH - INTERVAL_LOW) / 2.0)
CENTER = (INTERVAL_HIGH + INTERVAL_LOW) / 2.0
HALF_WIDTH = (INTERVAL_HIGH - INTERVAL_LOW) / 2.0
RHO0 = 1.0 / SIGMA
RHO1 = 1.0 / (2.0 * SIGMA - RHO0)
RHO2 = 1.0 / (2.0 * SIGMA - RHO1)


def place_kernel(
    place_ref, order_ref, load_ref, geom_ref, abs_ref,
    metric_ref, load_kv, bound_kv, near_ref, far_ref, pack_ref, flux_ref, work_ref,
):
    pick = jnp.where(
        lax.broadcasted_iota(jnp.int32, (64, 64), 0) == order_ref[...], 1.0, 0.0
    ).astype(jnp.bfloat16)
    low = lane_iota(ROWS) < 64

    def spread(placed, store):
        for b in range(4):
            piece = placed[:, b * LANES : (b + 1) * LANES]
            first, second = piece[:ROWS], piece[ROWS:]
            store(2 * b, jnp.where(low, first, roll(second, 64, 1)))
            store(2 * b + 1, jnp.where(low, roll(first, 64, 1), second))

    for c in range(7):
        def store_metric(i, value, c=c):
            metric_ref[c, i] = value

        spread(dot(pick, geom_ref[c]), store_metric)

    load = load_ref[...]
    high, rest = split(load)
    middle = (load - high.astype(jnp.float32) - rest.astype(jnp.float32)).astype(jnp.bfloat16)

    def store_load(i, value):
        work_ref[i] = value

    spread(dot(pick, high) + (dot(pick, rest) + dot(pick, middle)), store_load)
    store_assembled(load_kv, near_ref, far_ref, pack_ref, is_even(place_ref), lambda i: work_ref[i], 0)

    lane = lane_iota(8)
    q_a = jnp.zeros((8, LANES), jnp.float32)
    q_r = jnp.zeros((8, LANES), jnp.float32)
    for m in range(NODES):
        q_a = jnp.where((lane // 8) % 8 == m, float(ROW_TOTAL[m]), q_a)
        q_r = jnp.where(lane % 8 == m, float(ROW_TOTAL[m]), q_r)
    for chunk in range(ROWS // 8):
        rows = pl.ds(chunk * 8, 8)
        h_z = []
        for i in range(NODES):
            at = pl.ds(i * ROWS + chunk * 8, 8)
            q_z = float(ROW_TOTAL[i])
            g = [jnp.abs(metric_ref[c, i, rows]) for c in range(6)]
            h_z.append(g[0] * q_z + g[3] * q_a + g[4] * q_r)
            flux_ref[0, at] = g[3] * q_z + g[1] * q_a + g[5] * q_r
            flux_ref[1, at] = g[4] * q_z + g[5] * q_a + g[2] * q_r
        part_z = along_nodes(h_z, ABS_DERIV.T)
        for i in range(NODES):
            work_ref[i, rows] = part_z[i] + jnp.abs(metric_ref[6, i, rows])
    flux = jnp.concatenate([flux_ref[0], flux_ref[1]], axis=1)
    work_ref[...] += dot_split(flux, abs_ref).reshape(FIELD)
    store_assembled(bound_kv, near_ref, far_ref, pack_ref, is_even(place_ref), lambda i: work_ref[i], 1)


def start_kernel(
    place_ref, load_kv, bound_kv, h0, h1, h2,
    metric_ref, grad_ref, diver_ref,
    residual_ref, inverse_ref, update_ref, kv_ref, near_ref, far_ref, pack_ref, flux_ref, work_ref,
):
    residual = completed(place_ref, load_kv, (h0, h1, h2), 0)
    bound = completed(place_ref, bound_kv, (h0, h1, h2), 1)
    for i in range(NODES):
        r = residual(i)
        inverse = 1.0 / bound(i)
        residual_ref[i] = r
        inverse_ref[i] = inverse
        update_ref[i] = r * inverse * (1.0 / CENTER)
    apply_element(update_ref, metric_ref, grad_ref, diver_ref, flux_ref, work_ref)
    store_assembled(kv_ref, near_ref, far_ref, pack_ref, is_even(place_ref), lambda i: work_ref[i])


def second_kernel(
    place_ref, kv_in, h0, h1, h2, source_ref, inverse_ref, update_in,
    metric_ref, grad_ref, diver_ref,
    update_ref, result_ref, kv_ref, near_ref, far_ref, pack_ref, flux_ref, work_ref,
):
    image = completed(place_ref, kv_in, (h0, h1, h2))
    for i in range(NODES):
        old = update_in[i]
        update = (RHO1 * RHO0) * old + (2.0 * RHO1 / HALF_WIDTH) * inverse_ref[i] * (
            source_ref[i] - image(i)
        )
        update_ref[i] = update
        result_ref[i] = old + update
    apply_element(result_ref, metric_ref, grad_ref, diver_ref, flux_ref, work_ref)
    store_assembled(kv_ref, near_ref, far_ref, pack_ref, is_even(place_ref), lambda i: work_ref[i])


def third_kernel(
    place_ref, kv_in, h0, h1, h2, source_ref, inverse_ref, update_in, result_in,
    metric_ref, grad_ref, diver_ref,
    result_ref, kv_ref, near_ref, far_ref, pack_ref, sums_ref, flux_ref, work_ref,
):
    image = completed(place_ref, kv_in, (h0, h1, h2))
    plane = weight_plane()
    rz = jnp.zeros((ROWS, LANES), jnp.float32)
    for i in range(NODES):
        source = source_ref[i]
        update = (RHO2 * RHO1) * update_in[i] + (2.0 * RHO2 / HALF_WIDTH) * inverse_ref[i] * (
            source - image(i)
        )
        result = result_in[i] + update
        result_ref[i] = result
        rz = rz + source * result * node_weight(i)
    apply_element(result_ref, metric_ref, grad_ref, diver_ref, flux_ref, work_ref)
    energy = jnp.zeros((ROWS, LANES), jnp.float32)
    for i in range(NODES):
        energy = energy + result_ref[i] * work_ref[i]
    sums_ref[...] = sum_row([rz * plane, energy])
    store_assembled(kv_ref, near_ref, far_ref, pack_ref, is_even(place_ref), lambda i: work_ref[i])


def fourth_kernel(
    place_ref, kv_in, h0, h1, h2, inverse_ref, metric_ref, grad_ref, diver_ref,
    image_ref, update_ref, kv_ref, near_ref, far_ref, pack_ref, flux_ref, work_ref,
):
    image = completed(place_ref, kv_in, (h0, h1, h2))
    for i in range(NODES):
        value = image(i)
        image_ref[i] = value
        update_ref[i] = value * inverse_ref[i] * (1.0 / CENTER)
    apply_element(update_ref, metric_ref, grad_ref, diver_ref, flux_ref, work_ref)
    store_assembled(kv_ref, near_ref, far_ref, pack_ref, is_even(place_ref), lambda i: work_ref[i])


def sixth_kernel(
    place_ref, kv_in, h0, h1, h2, source_ref, inverse_ref, update_in, result_in,
    residual_ref, first_ref, early_ref, metric_ref, grad_ref, diver_ref,
    result_ref, kv_ref, near_ref, far_ref, pack_ref, sums_ref, flux_ref, work_ref,
):
    image = completed(place_ref, kv_in, (h0, h1, h2))
    plane = weight_plane()
    r_y = jnp.zeros((ROWS, LANES), jnp.float32)
    w_y = jnp.zeros((ROWS, LANES), jnp.float32)
    for i in range(NODES):
        source = source_ref[i]
        update = (RHO2 * RHO1) * update_in[i] + (2.0 * RHO2 / HALF_WIDTH) * inverse_ref[i] * (
            source - image(i)
        )
        result = result_in[i] + update
        result_ref[i] = result
        r_y = r_y + residual_ref[i] * result * node_weight(i)
        w_y = w_y + source * result * node_weight(i)
    apply_element(result_ref, metric_ref, grad_ref, diver_ref, flux_ref, work_ref)
    z_ky = jnp.zeros((ROWS, LANES), jnp.float32)
    y_ky = jnp.zeros((ROWS, LANES), jnp.float32)
    for i in range(NODES):
        z_ky = z_ky + first_ref[i] * work_ref[i]
        y_ky = y_ky + result_ref[i] * work_ref[i]
    zero = jnp.zeros((1, LANES), jnp.float32)
    late = sum_row([zero, zero, r_y * plane, w_y * plane, z_ky, y_ky])
    sums_ref[...] = jnp.broadcast_to(early_ref[...] + late, sums_ref.shape)
    store_assembled(kv_ref, near_ref, far_ref, pack_ref, is_even(place_ref), lambda i: work_ref[i])


def last_kernel(
    place_ref, kv_in, h0, h1, h2, sums_ref, order_ref,
    residual_ref, first_ref, image_ref, second_ref,
    solution_ref, residual_out, spread_ref,
):
    sums = jnp.sum(sums_ref[...], axis=0, keepdims=True)
    lane = lane_iota(1)

    def total(d):
        return jnp.sum(jnp.where(lane == d, sums, 0.0), axis=1, keepdims=True)

    rz0, zw, ry, wy, zq, yq = (total(d) for d in range(6))
    alpha0 = rz0 / zw
    rz1 = rz0 - alpha0 * (zw + ry) + alpha0 * alpha0 * wy
    beta = rz1 / rz0
    share = 1.0 + beta
    energy = share * share * zw - 2.0 * share * alpha0 * zq + alpha0 * alpha0 * yq
    alpha1 = rz1 / energy
    first_scale = alpha0 + alpha1 * share
    second_scale = alpha1 * alpha0
    image = completed(place_ref, kv_in, (h0, h1, h2))
    low = lane_iota(ROWS) < 64
    for b in range(4):
        pair = []
        for i in (2 * b, 2 * b + 1):
            x = first_scale * first_ref[i] - second_scale * second_ref[i]
            r = residual_ref[i] - first_scale * image_ref[i] + second_scale * image(i)
            pair.append((x, r))
        for f in range(2):
            even, odd = pair[0][f], pair[1][f]
            lanes = pl.ds(b * LANES, LANES)
            spread_ref[f, :ROWS, lanes] = jnp.where(low, even, roll(odd, 64, 1))
            spread_ref[f, ROWS:, lanes] = jnp.where(low, roll(even, 64, 1), odd)
    pick = jnp.where(
        lax.broadcasted_iota(jnp.int32, (64, 64), 1) == order_ref[...], 1.0, 0.0
    ).astype(jnp.bfloat16)
    for f, out in ((0, solution_ref), (1, residual_out)):
        value = spread_ref[f]
        high, middle = split(value)
        rest = (value - high.astype(jnp.float32) - middle.astype(jnp.float32)).astype(jnp.bfloat16)
        out[...] = dot(pick, high) + (dot(pick, middle) + dot(pick, rest))


VMEM_LIMIT = 24 * 1024 * 1024
F32 = jnp.float32


def call(kernel, place, outs, scratch, *operands):
    vmem = pl.BlockSpec(memory_space=pltpu.VMEM)
    return pl.pallas_call(
        kernel,
        out_shape=[jax.ShapeDtypeStruct(s, F32) for s in outs],
        in_specs=[pl.BlockSpec(memory_space=pltpu.SMEM)] + [vmem] * len(operands),
        out_specs=[vmem] * len(outs),
        scratch_shapes=[pltpu.VMEM(s, F32) for s in scratch],
        compiler_params=pltpu.CompilerParams(vmem_limit_bytes=VMEM_LIMIT),
    )(place, *operands)


FLUX = (2, NODES * ROWS, LANES)


def faces(fields=1):
    return [(fields, ROWS, LANES), (fields, ROWS, LANES), (fields, HALF, LANES)]


def exchange(place, near, far, pack):
    count = lax.axis_size(WIDE)
    near = lax.ppermute(near, WIDE, [(w, w ^ 1) for w in range(count)])
    far = lax.ppermute(
        far, WIDE, [(w, (w + 1 if w % 2 else w - 1) % count) for w in range(count)]
    )
    (pack,) = call(pack_kernel, place, [pack.shape], [], pack, near, far)
    return near, far, lax.all_gather(pack, "narrow")


def local(load, geom, element_order):
    place = jnp.stack([lax.axis_index(WIDE) % 2, lax.axis_index("narrow")]).astype(jnp.int32)
    order = element_order.reshape(1, 64)
    grad = jnp.asarray(GRAD_HL)
    diver = jnp.asarray(DIVER_HL)
    metric, load_kv, bound_kv, *face = call(
        place_kernel, place,
        [(7,) + FIELD, FIELD, FIELD] + faces(2),
        [FLUX, FIELD],
        order, load, geom, jnp.asarray(ABS_HL),
    )
    halo = exchange(place, *face)
    residual, inverse, update, kv, *face = call(
        start_kernel, place,
        [FIELD, FIELD, FIELD, FIELD] + faces(),
        [FLUX, FIELD],
        load_kv, bound_kv, *halo, metric, grad, diver,
    )
    halo = exchange(place, *face)
    update, result, kv, *face = call(
        second_kernel, place,
        [FIELD, FIELD, FIELD] + faces(),
        [FLUX, FIELD],
        kv, *halo, residual, inverse, update, metric, grad, diver,
    )
    halo = exchange(place, *face)
    first, kv, *face, early = call(
        third_kernel, place,
        [FIELD, FIELD] + faces() + [(1, LANES)],
        [FLUX, FIELD],
        kv, *halo, residual, inverse, update, result, metric, grad, diver,
    )
    halo = exchange(place, *face)
    image, update, kv, *face = call(
        fourth_kernel, place,
        [FIELD, FIELD, FIELD] + faces(),
        [FLUX, FIELD],
        kv, *halo, inverse, metric, grad, diver,
    )
    halo = exchange(place, *face)
    update, result, kv, *face = call(
        second_kernel, place,
        [FIELD, FIELD, FIELD] + faces(),
        [FLUX, FIELD],
        kv, *halo, image, inverse, update, metric, grad, diver,
    )
    halo = exchange(place, *face)
    second, kv, *face, sums = call(
        sixth_kernel, place,
        [FIELD, FIELD] + faces() + [(lax.axis_size(REST), LANES)],
        [FLUX, FIELD],
        kv, *halo, image, inverse, update, result,
        residual, first, early, metric, grad, diver,
    )
    halo = exchange(place, *face)
    sums = lax.all_to_all(sums, REST, 0, 0)
    sums = jnp.broadcast_to(
        jnp.sum(sums, axis=0, keepdims=True), (lax.axis_size("ring"), LANES)
    )
    sums = lax.all_to_all(sums, "ring", 0, 0)
    return tuple(
        call(
            last_kernel, place,
            [(64, 512), (64, 512)],
            [(2, 64, 512)],
            kv, *halo, sums, element_order.reshape(64, 1), residual, first, image, second,
        )
    )


def solution(mesh):
    wide, narrow = mesh.devices.shape
    ring = 12 if wide % 12 == 0 else 2
    fine = jax.sharding.Mesh(
        mesh.devices.reshape(wide // ring, ring, narrow), ("outer", "ring", "narrow")
    )
    rows = ("outer", "ring", "narrow")
    return jax.shard_map(
        local,
        mesh=fine,
        in_specs=(P(rows, None), P(None, rows, None), P(WIDE, "narrow", None)),
        out_specs=(P(rows, None), P(rows, None)),
        check_vma=False,
    )
```

```python
import functools

import jax
import jax.numpy as jnp
import ml_dtypes
import numpy as np
from jax import lax
from jax.experimental import pallas as pl
from jax.experimental.pallas import tpu as pltpu
from jax.sharding import PartitionSpec as P

NODES = 8
ROWS = 32
LANES = 128
HALF = 16
INTERVAL_LOW = 0.03
INTERVAL_HIGH = 1.0
FIELD = (NODES, ROWS, LANES)
WIDE = ("outer", "ring")
REST = ("outer", "narrow")


def legendre_seven(point):
    before = 1.0
    current = point
    for degree in range(1, 7):
        after = ((2.0 * degree + 1.0) * point * current - degree * before) / (degree + 1.0)
        before = current
        current = after
    return current


def gll_derivative():
    points = 8
    inner_nodes = [
        -0.8717401485096066,
        -0.5917001814331423,
        -0.2092992179024789,
        0.2092992179024789,
        0.5917001814331423,
        0.8717401485096066,
    ]
    nodes = [-1.0] + inner_nodes + [1.0]
    values_at = [legendre_seven(node) for node in nodes]
    matrix = np.zeros((points, points))
    for source in range(points):
        for target in range(points):
            if source != target:
                matrix[source, target] = values_at[source] / (
                    values_at[target] * (nodes[source] - nodes[target])
                )
    matrix[0, 0] = -(points - 1) * points / 4.0
    matrix[points - 1, points - 1] = (points - 1) * points / 4.0
    return matrix


DERIV = gll_derivative().astype(np.float32)
ABS_DERIV = np.abs(DERIV)
ROW_TOTAL = ABS_DERIV.sum(axis=1)
EYE8 = np.eye(8, dtype=np.float32)


def cycle_matrix(small):
    return np.kron(np.eye(2, dtype=np.float32), np.kron(small, EYE8))


def radial_matrix(small):
    return np.kron(np.eye(16, dtype=np.float32), small)


def split_const(matrix):
    high = matrix.astype(ml_dtypes.bfloat16)
    low = (matrix - high.astype(np.float32)).astype(ml_dtypes.bfloat16)
    return high, low


GRAD = np.concatenate([cycle_matrix(DERIV.T), radial_matrix(DERIV.T)], axis=1)
DIVER = np.concatenate([cycle_matrix(DERIV), radial_matrix(DERIV)], axis=0)
GRAD_HL = np.stack(split_const(GRAD))
DIVER_HL = np.stack(split_const(DIVER))
ABS_HL = np.stack(split_const(np.abs(DIVER)))


def split(value):
    high = value.astype(jnp.bfloat16)
    return high, (value - high.astype(jnp.float32)).astype(jnp.bfloat16)


def dot(left, right):
    return lax.dot_general(
        left, right, (((1,), (0,)), ((), ())), preferred_element_type=jnp.float32
    )


def dot_split(value, matrix_ref):
    high, low = split(value)
    return dot(high, matrix_ref[0]) + (dot(low, matrix_ref[0]) + dot(high, matrix_ref[1]))


def lane_iota(rows):
    return lax.broadcasted_iota(jnp.int32, (rows, LANES), 1)


def row_iota(rows):
    return lax.broadcasted_iota(jnp.int32, (rows, LANES), 0)


def roll(value, shift, axis):
    size = value.shape[axis]
    return pltpu.roll(value, shift % size, axis)


def along_nodes(values, small):
    out = []
    for m in range(NODES):
        total = None
        for i in range(NODES):
            scale = float(small[m][i])
            if scale != 0.0:
                term = values[i] * scale
                total = term if total is None else total + term
        out.append(total)
    return out


def own_assembly(u):
    lane = lane_iota(ROWS)
    k = lane % 8
    er = row_iota(ROWS) % HALF
    up = roll(roll(u, -1, 0), 7, 1)
    down = roll(roll(u, 1, 0), -7, 1)
    u = (
        u
        + jnp.where((k == 7) & (er < HALF - 1), up, 0.0)
        + jnp.where((k == 0) & (er > 0), down, 0.0)
    )
    top, bottom = u[:HALF], u[HALF:]
    lane = lane_iota(HALF)
    j = (lane // 8) % 8
    block = lane // 64
    new_top = (
        top
        + jnp.where(j == 7, roll(bottom, 56, 1), 0.0)
        + jnp.where((j == 0) & (block == 1), roll(bottom, 8, 1), 0.0)
    )
    new_bottom = (
        bottom
        + jnp.where(j == 0, roll(top, -56, 1), 0.0)
        + jnp.where((j == 7) & (block == 0), roll(top, -8, 1), 0.0)
    )
    return new_top, new_bottom


def ends(value):
    lane = lane_iota(HALF)
    return jnp.where(lane < 8, value[:HALF], jnp.where(lane >= 120, value[HALF:], 0.0))


def store_assembled(kv_ref, near_ref, far_ref, pack_ref, even, source, field=0):
    pack = None
    for i in range(NODES):
        top, bottom = own_assembly(source(i))
        value = jnp.concatenate([top, bottom], axis=0)
        kv_ref[i] = value
        if i == 0:
            first = value
        last = value
        piece = ends(value)
        if i:
            piece = roll(piece, 16 * i, 1)
        pack = piece if pack is None else pack + piece
    near_ref[field] = jnp.where(even, last, first)
    far_ref[field] = jnp.where(even, first, last)
    pack_ref[field] = pack


def is_even(place_ref):
    return lax.broadcast_in_dim(place_ref[0], (ROWS, LANES), ()) == 0


def pack_kernel(place_ref, pack_in, far_ref, near_ref, pack_ref):
    even = is_even(place_ref)
    for field in range(pack_ref.shape[0]):
        near, far = near_ref[field], far_ref[field]
        first = ends(jnp.where(even, far, near))
        last = ends(jnp.where(even, near, far))
        pack_ref[field] = pack_in[field] + first + roll(last, 16 * (NODES - 1), 1)


def completed(place_ref, kv, halo, field=0):
    far_ref, near_ref, packs_ref = halo
    even = is_even(place_ref)
    near, far = near_ref[field], far_ref[field]
    count = packs_ref.shape[0]
    here = place_ref[1]
    left = packs_ref[lax.rem(here + count - 1, count), field]
    right = packs_ref[lax.rem(here + 1, count), field]
    lane = lane_iota(HALF)
    side = jnp.where(lane % 16 < 8, roll(left, 8, 1), roll(right, -8, 1))

    def value(i):
        piece = roll(side, -16 * i, 1) if i else side
        u = kv[i] + jnp.concatenate(
            [jnp.where(lane < 8, piece, 0.0), jnp.where(lane >= 120, piece, 0.0)], axis=0
        )
        if i == 0:
            u = u + jnp.where(even, far, near)
        if i == NODES - 1:
            u = u + jnp.where(even, near, far)
        return u

    return value


def apply_element(v_ref, metric_ref, grad_ref, diver_ref, flux_ref, out_ref):
    side = dot_split(v_ref[...].reshape(NODES * ROWS, LANES), grad_ref)
    flux_ref[0] = side[:, :LANES]
    flux_ref[1] = side[:, LANES:]
    for chunk in range(ROWS // 8):
        rows = pl.ds(chunk * 8, 8)
        values = [v_ref[i, rows] for i in range(NODES)]
        grad_z = along_nodes(values, DERIV)
        flux_z = []
        for i in range(NODES):
            at = pl.ds(i * ROWS + chunk * 8, 8)
            g_z, g_a, g_r = grad_z[i], flux_ref[0, at], flux_ref[1, at]
            m = [metric_ref[c, i, rows] for c in range(6)]
            flux_z.append(m[0] * g_z + m[3] * g_a + m[4] * g_r)
            flux_ref[0, at] = m[3] * g_z + m[1] * g_a + m[5] * g_r
            flux_ref[1, at] = m[4] * g_z + m[5] * g_a + m[2] * g_r
        part_z = along_nodes(flux_z, DERIV.T)
        for i in range(NODES):
            out_ref[i, rows] = part_z[i] + metric_ref[6, i, rows] * values[i]
    flux = jnp.concatenate([flux_ref[0], flux_ref[1]], axis=1)
    out_ref[...] += dot_split(flux, diver_ref).reshape(FIELD)


def weight_plane():
    lane, row = lane_iota(ROWS), row_iota(ROWS)
    j, k, er = (lane // 8) % 8, lane % 8, row % HALF
    w_a = jnp.where((j == 0) | (j == 7), 0.5, 1.0)
    shared = ((k == 0) & (er > 0)) | ((k == 7) & (er < HALF - 1))
    return w_a * jnp.where(shared, 0.5, 1.0)


def node_weight(i):
    return 0.5 if i in (0, NODES - 1) else 1.0


def sum_row(sums):
    lane = lane_iota(1)
    row = jnp.zeros((1, LANES), jnp.float32)
    for d, value in enumerate(sums):
        row = jnp.where(lane == d, jnp.sum(value), row)
    return row


SIGMA = ((INTERVAL_HIGH + INTERVAL_LOW) / 2.0) / ((INTERVAL_HIGH - INTERVAL_LOW) / 2.0)
CENTER = (INTERVAL_HIGH + INTERVAL_LOW) / 2.0
HALF_WIDTH = (INTERVAL_HIGH - INTERVAL_LOW) / 2.0
RHO0 = 1.0 / SIGMA
RHO1 = 1.0 / (2.0 * SIGMA - RHO0)
RHO2 = 1.0 / (2.0 * SIGMA - RHO1)


def place_kernel(
    place_ref, order_ref, load_ref, geom_ref, abs_ref,
    metric_ref, load_kv, bound_kv, near_ref, far_ref, pack_ref, flux_ref, work_ref,
):
    pick = jnp.where(
        lax.broadcasted_iota(jnp.int32, (64, 64), 0) == order_ref[...], 1.0, 0.0
    ).astype(jnp.bfloat16)
    low = lane_iota(ROWS) < 64

    def spread(placed, store):
        for b in range(4):
            piece = placed[:, b * LANES : (b + 1) * LANES]
            first, second = piece[:ROWS], piece[ROWS:]
            store(2 * b, jnp.where(low, first, roll(second, 64, 1)))
            store(2 * b + 1, jnp.where(low, roll(first, 64, 1), second))

    for c in range(7):
        def store_metric(i, value, c=c):
            metric_ref[c, i] = value

        spread(dot(pick, geom_ref[c]), store_metric)

    load = load_ref[...]
    high, rest = split(load)
    middle = (load - high.astype(jnp.float32) - rest.astype(jnp.float32)).astype(jnp.bfloat16)

    def store_load(i, value):
        work_ref[i] = value

    spread(dot(pick, high) + (dot(pick, rest) + dot(pick, middle)), store_load)
    store_assembled(load_kv, near_ref, far_ref, pack_ref, is_even(place_ref), lambda i: work_ref[i], 0)

    lane = lane_iota(8)
    q_a = jnp.zeros((8, LANES), jnp.float32)
    q_r = jnp.zeros((8, LANES), jnp.float32)
    for m in range(NODES):
        q_a = jnp.where((lane // 8) % 8 == m, float(ROW_TOTAL[m]), q_a)
        q_r = jnp.where(lane % 8 == m, float(ROW_TOTAL[m]), q_r)
    for chunk in range(ROWS // 8):
        rows = pl.ds(chunk * 8, 8)
        h_z = []
        for i in range(NODES):
            at = pl.ds(i * ROWS + chunk * 8, 8)
            q_z = float(ROW_TOTAL[i])
            g = [jnp.abs(metric_ref[c, i, rows]) for c in range(6)]
            h_z.append(g[0] * q_z + g[3] * q_a + g[4] * q_r)
            flux_ref[0, at] = g[3] * q_z + g[1] * q_a + g[5] * q_r
            flux_ref[1, at] = g[4] * q_z + g[5] * q_a + g[2] * q_r
        part_z = along_nodes(h_z, ABS_DERIV.T)
        for i in range(NODES):
            work_ref[i, rows] = part_z[i] + jnp.abs(metric_ref[6, i, rows])
    flux = jnp.concatenate([flux_ref[0], flux_ref[1]], axis=1)
    work_ref[...] += dot_split(flux, abs_ref).reshape(FIELD)
    store_assembled(bound_kv, near_ref, far_ref, pack_ref, is_even(place_ref), lambda i: work_ref[i], 1)


def start_kernel(
    place_ref, load_kv, bound_kv, h0, h1, h2,
    metric_ref, grad_ref, diver_ref,
    residual_ref, inverse_ref, update_ref, kv_ref, near_ref, far_ref, pack_ref, flux_ref, work_ref,
):
    residual = completed(place_ref, load_kv, (h0, h1, h2), 0)
    bound = completed(place_ref, bound_kv, (h0, h1, h2), 1)
    for i in range(NODES):
        r = residual(i)
        inverse = 1.0 / bound(i)
        residual_ref[i] = r
        inverse_ref[i] = inverse
        update_ref[i] = r * inverse * (1.0 / CENTER)
    apply_element(update_ref, metric_ref, grad_ref, diver_ref, flux_ref, work_ref)
    store_assembled(kv_ref, near_ref, far_ref, pack_ref, is_even(place_ref), lambda i: work_ref[i])


def second_kernel(
    place_ref, kv_in, h0, h1, h2, source_ref, inverse_ref, update_in,
    metric_ref, grad_ref, diver_ref,
    update_ref, result_ref, kv_ref, near_ref, far_ref, pack_ref, flux_ref, work_ref,
):
    image = completed(place_ref, kv_in, (h0, h1, h2))
    for i in range(NODES):
        old = update_in[i]
        update = (RHO1 * RHO0) * old + (2.0 * RHO1 / HALF_WIDTH) * inverse_ref[i] * (
            source_ref[i] - image(i)
        )
        update_ref[i] = update
        result_ref[i] = old + update
    apply_element(result_ref, metric_ref, grad_ref, diver_ref, flux_ref, work_ref)
    store_assembled(kv_ref, near_ref, far_ref, pack_ref, is_even(place_ref), lambda i: work_ref[i])


def third_kernel(
    place_ref, kv_in, h0, h1, h2, source_ref, inverse_ref, update_in, result_in,
    metric_ref, grad_ref, diver_ref,
    result_ref, kv_ref, near_ref, far_ref, pack_ref, sums_ref, flux_ref, work_ref,
):
    image = completed(place_ref, kv_in, (h0, h1, h2))
    plane = weight_plane()
    rz = jnp.zeros((ROWS, LANES), jnp.float32)
    for i in range(NODES):
        source = source_ref[i]
        update = (RHO2 * RHO1) * update_in[i] + (2.0 * RHO2 / HALF_WIDTH) * inverse_ref[i] * (
            source - image(i)
        )
        result = result_in[i] + update
        result_ref[i] = result
        rz = rz + source * result * node_weight(i)
    apply_element(result_ref, metric_ref, grad_ref, diver_ref, flux_ref, work_ref)
    energy = jnp.zeros((ROWS, LANES), jnp.float32)
    for i in range(NODES):
        energy = energy + result_ref[i] * work_ref[i]
    sums_ref[...] = sum_row([rz * plane, energy])
    store_assembled(kv_ref, near_ref, far_ref, pack_ref, is_even(place_ref), lambda i: work_ref[i])


def fourth_kernel(
    place_ref, kv_in, h0, h1, h2, inverse_ref, metric_ref, grad_ref, diver_ref,
    image_ref, update_ref, kv_ref, near_ref, far_ref, pack_ref, flux_ref, work_ref,
):
    image = completed(place_ref, kv_in, (h0, h1, h2))
    for i in range(NODES):
        value = image(i)
        image_ref[i] = value
        update_ref[i] = value * inverse_ref[i] * (1.0 / CENTER)
    apply_element(update_ref, metric_ref, grad_ref, diver_ref, flux_ref, work_ref)
    store_assembled(kv_ref, near_ref, far_ref, pack_ref, is_even(place_ref), lambda i: work_ref[i])


def sixth_kernel(
    place_ref, kv_in, h0, h1, h2, source_ref, inverse_ref, update_in, result_in,
    residual_ref, first_ref, early_ref, metric_ref, grad_ref, diver_ref,
    result_ref, kv_ref, near_ref, far_ref, pack_ref, sums_ref, flux_ref, work_ref,
):
    image = completed(place_ref, kv_in, (h0, h1, h2))
    plane = weight_plane()
    r_y = jnp.zeros((ROWS, LANES), jnp.float32)
    w_y = jnp.zeros((ROWS, LANES), jnp.float32)
    for i in range(NODES):
        source = source_ref[i]
        update = (RHO2 * RHO1) * update_in[i] + (2.0 * RHO2 / HALF_WIDTH) * inverse_ref[i] * (
            source - image(i)
        )
        result = result_in[i] + update
        result_ref[i] = result
        r_y = r_y + residual_ref[i] * result * node_weight(i)
        w_y = w_y + source * result * node_weight(i)
    apply_element(result_ref, metric_ref, grad_ref, diver_ref, flux_ref, work_ref)
    z_ky = jnp.zeros((ROWS, LANES), jnp.float32)
    y_ky = jnp.zeros((ROWS, LANES), jnp.float32)
    for i in range(NODES):
        z_ky = z_ky + first_ref[i] * work_ref[i]
        y_ky = y_ky + result_ref[i] * work_ref[i]
    zero = jnp.zeros((1, LANES), jnp.float32)
    late = sum_row([zero, zero, r_y * plane, w_y * plane, z_ky, y_ky])
    sums_ref[...] = jnp.broadcast_to(early_ref[...] + late, sums_ref.shape)
    store_assembled(kv_ref, near_ref, far_ref, pack_ref, is_even(place_ref), lambda i: work_ref[i])


def last_kernel(
    place_ref, kv_in, h0, h1, h2, sums_ref, order_ref,
    residual_ref, first_ref, image_ref, second_ref,
    solution_ref, residual_out, spread_ref,
):
    sums = jnp.sum(sums_ref[...], axis=0, keepdims=True)
    lane = lane_iota(1)

    def total(d):
        return jnp.sum(jnp.where(lane == d, sums, 0.0), axis=1, keepdims=True)

    rz0, zw, ry, wy, zq, yq = (total(d) for d in range(6))
    alpha0 = rz0 / zw
    rz1 = rz0 - alpha0 * (zw + ry) + alpha0 * alpha0 * wy
    beta = rz1 / rz0
    share = 1.0 + beta
    energy = share * share * zw - 2.0 * share * alpha0 * zq + alpha0 * alpha0 * yq
    alpha1 = rz1 / energy
    first_scale = alpha0 + alpha1 * share
    second_scale = alpha1 * alpha0
    image = completed(place_ref, kv_in, (h0, h1, h2))
    low = lane_iota(ROWS) < 64
    for b in range(4):
        pair = []
        for i in (2 * b, 2 * b + 1):
            x = first_scale * first_ref[i] - second_scale * second_ref[i]
            r = residual_ref[i] - first_scale * image_ref[i] + second_scale * image(i)
            pair.append((x, r))
        for f in range(2):
            even, odd = pair[0][f], pair[1][f]
            lanes = pl.ds(b * LANES, LANES)
            spread_ref[f, :ROWS, lanes] = jnp.where(low, even, roll(odd, 64, 1))
            spread_ref[f, ROWS:, lanes] = jnp.where(low, roll(even, 64, 1), odd)
    pick = jnp.where(
        lax.broadcasted_iota(jnp.int32, (64, 64), 1) == order_ref[...], 1.0, 0.0
    ).astype(jnp.bfloat16)
    for f, out in ((0, solution_ref), (1, residual_out)):
        value = spread_ref[f]
        high, middle = split(value)
        rest = (value - high.astype(jnp.float32) - middle.astype(jnp.float32)).astype(jnp.bfloat16)
        out[...] = dot(pick, high) + (dot(pick, middle) + dot(pick, rest))


VMEM_LIMIT = 24 * 1024 * 1024
F32 = jnp.float32


def call(kernel, place, outs, scratch, *operands):
    vmem = pl.BlockSpec(memory_space=pltpu.VMEM)
    return pl.pallas_call(
        kernel,
        out_shape=[jax.ShapeDtypeStruct(s, F32) for s in outs],
        in_specs=[pl.BlockSpec(memory_space=pltpu.SMEM)] + [vmem] * len(operands),
        out_specs=[vmem] * len(outs),
        scratch_shapes=[pltpu.VMEM(s, F32) for s in scratch],
        compiler_params=pltpu.CompilerParams(vmem_limit_bytes=VMEM_LIMIT),
    )(place, *operands)


FLUX = (2, NODES * ROWS, LANES)


def faces(fields=1):
    return [(fields, ROWS, LANES), (fields, ROWS, LANES), (fields, HALF, LANES)]


def exchange(place, near, far, pack):
    count = lax.axis_size(WIDE)
    far = lax.ppermute(
        far, WIDE, [(w, (w + 1 if w % 2 else w - 1) % count) for w in range(count)]
    )
    near = lax.ppermute(near, WIDE, [(w, w ^ 1) for w in range(count)])
    (pack,) = call(pack_kernel, place, [pack.shape], [], pack, far, near)
    return far, near, lax.all_gather(pack, "narrow")


def local(load, geom, element_order):
    place = jnp.stack([lax.axis_index(WIDE) % 2, lax.axis_index("narrow")]).astype(jnp.int32)
    order = element_order.reshape(1, 64)
    grad = jnp.asarray(GRAD_HL)
    diver = jnp.asarray(DIVER_HL)
    metric, load_kv, bound_kv, *face = call(
        place_kernel, place,
        [(7,) + FIELD, FIELD, FIELD] + faces(2),
        [FLUX, FIELD],
        order, load, geom, jnp.asarray(ABS_HL),
    )
    halo = exchange(place, *face)
    residual, inverse, update, kv, *face = call(
        start_kernel, place,
        [FIELD, FIELD, FIELD, FIELD] + faces(),
        [FLUX, FIELD],
        load_kv, bound_kv, *halo, metric, grad, diver,
    )
    halo = exchange(place, *face)
    update, result, kv, *face = call(
        second_kernel, place,
        [FIELD, FIELD, FIELD] + faces(),
        [FLUX, FIELD],
        kv, *halo, residual, inverse, update, metric, grad, diver,
    )
    halo = exchange(place, *face)
    first, kv, *face, early = call(
        third_kernel, place,
        [FIELD, FIELD] + faces() + [(1, LANES)],
        [FLUX, FIELD],
        kv, *halo, residual, inverse, update, result, metric, grad, diver,
    )
    halo = exchange(place, *face)
    image, update, kv, *face = call(
        fourth_kernel, place,
        [FIELD, FIELD, FIELD] + faces(),
        [FLUX, FIELD],
        kv, *halo, inverse, metric, grad, diver,
    )
    halo = exchange(place, *face)
    update, result, kv, *face = call(
        second_kernel, place,
        [FIELD, FIELD, FIELD] + faces(),
        [FLUX, FIELD],
        kv, *halo, image, inverse, update, metric, grad, diver,
    )
    halo = exchange(place, *face)
    second, kv, *face, sums = call(
        sixth_kernel, place,
        [FIELD, FIELD] + faces() + [(lax.axis_size(REST), LANES)],
        [FLUX, FIELD],
        kv, *halo, image, inverse, update, result,
        residual, first, early, metric, grad, diver,
    )
    halo = exchange(place, *face)
    sums = lax.all_to_all(sums, REST, 0, 0)
    sums = jnp.broadcast_to(
        jnp.sum(sums, axis=0, keepdims=True), (lax.axis_size("ring"), LANES)
    )
    sums = lax.all_to_all(sums, "ring", 0, 0)
    return tuple(
        call(
            last_kernel, place,
            [(64, 512), (64, 512)],
            [(2, 64, 512)],
            kv, *halo, sums, element_order.reshape(64, 1), residual, first, image, second,
        )
    )


def solution(mesh):
    wide, narrow = mesh.devices.shape
    ring = 12 if wide % 12 == 0 else 2
    fine = jax.sharding.Mesh(
        mesh.devices.reshape(wide // ring, ring, narrow), ("outer", "ring", "narrow")
    )
    rows = ("outer", "ring", "narrow")
    return jax.shard_map(
        local,
        mesh=fine,
        in_specs=(P(rows, None), P(None, rows, None), P(WIDE, "narrow", None)),
        out_specs=(P(rows, None), P(rows, None)),
        check_vma=False,
    )
```

```python
import functools

import jax
import jax.numpy as jnp
import ml_dtypes
import numpy as np
from jax import lax
from jax.experimental import pallas as pl
from jax.experimental.pallas import tpu as pltpu
from jax.sharding import PartitionSpec as P

NODES = 8
ROWS = 32
LANES = 128
HALF = 16
GROWS = ROWS + HALF
INTERVAL_LOW = 0.03
INTERVAL_HIGH = 1.0
FIELD = (NODES, ROWS, LANES)
GHOST = (NODES, HALF, LANES)
BIG = (NODES, GROWS, LANES)
WIDE = ("outer", "ring")
REST = ("outer", "narrow")


def legendre_seven(point):
    before = 1.0
    current = point
    for degree in range(1, 7):
        after = ((2.0 * degree + 1.0) * point * current - degree * before) / (degree + 1.0)
        before = current
        current = after
    return current


def gll_derivative():
    points = 8
    inner_nodes = [
        -0.8717401485096066,
        -0.5917001814331423,
        -0.2092992179024789,
        0.2092992179024789,
        0.5917001814331423,
        0.8717401485096066,
    ]
    nodes = [-1.0] + inner_nodes + [1.0]
    values_at = [legendre_seven(node) for node in nodes]
    matrix = np.zeros((points, points))
    for source in range(points):
        for target in range(points):
            if source != target:
                matrix[source, target] = values_at[source] / (
                    values_at[target] * (nodes[source] - nodes[target])
                )
    matrix[0, 0] = -(points - 1) * points / 4.0
    matrix[points - 1, points - 1] = (points - 1) * points / 4.0
    return matrix


DERIV = gll_derivative().astype(np.float32)
ABS_DERIV = np.abs(DERIV)
ROW_TOTAL = ABS_DERIV.sum(axis=1)
EYE8 = np.eye(8, dtype=np.float32)


def cycle_matrix(small):
    return np.kron(np.eye(2, dtype=np.float32), np.kron(small, EYE8))


def radial_matrix(small):
    return np.kron(np.eye(16, dtype=np.float32), small)


def split_const(matrix):
    high = matrix.astype(ml_dtypes.bfloat16)
    low = (matrix - high.astype(np.float32)).astype(ml_dtypes.bfloat16)
    return high, low


GRAD = np.concatenate([cycle_matrix(DERIV.T), radial_matrix(DERIV.T)], axis=1)
DIVER = np.concatenate([cycle_matrix(DERIV), radial_matrix(DERIV)], axis=0)
GRAD_HL = np.stack(split_const(GRAD))
DIVER_HL = np.stack(split_const(DIVER))
ABS_HL = np.stack(split_const(np.abs(DIVER)))


def split(value):
    high = value.astype(jnp.bfloat16)
    return high, (value - high.astype(jnp.float32)).astype(jnp.bfloat16)


def dot(left, right):
    return lax.dot_general(
        left, right, (((1,), (0,)), ((), ())), preferred_element_type=jnp.float32
    )


def dot_split(value, matrix_ref):
    high, low = split(value)
    return dot(high, matrix_ref[0]) + (dot(low, matrix_ref[0]) + dot(high, matrix_ref[1]))


def lane_iota(rows):
    return lax.broadcasted_iota(jnp.int32, (rows, LANES), 1)


def row_iota(rows):
    return lax.broadcasted_iota(jnp.int32, (rows, LANES), 0)


def roll(value, shift, axis):
    size = value.shape[axis]
    return pltpu.roll(value, shift % size, axis)


def along_nodes(values, small):
    half = NODES // 2
    even = [values[i] + values[NODES - 1 - i] for i in range(half)]
    odd = [values[i] - values[NODES - 1 - i] for i in range(half)]
    out = [None] * NODES
    for m in range(half):
        from_even, from_odd = None, None
        for i in range(half):
            near, far = float(small[m][i]), float(small[m][NODES - 1 - i])
            one = even[i] * (0.5 * (near + far))
            two = odd[i] * (0.5 * (near - far))
            from_even = one if from_even is None else from_even + one
            from_odd = two if from_odd is None else from_odd + two
        out[m] = from_odd + from_even
        out[NODES - 1 - m] = from_odd - from_even
    return out


def along_nodes_plain(values, small):
    out = []
    for m in range(NODES):
        total = None
        for i in range(NODES):
            term = values[i] * float(small[m][i])
            total = term if total is None else total + term
        out.append(total)
    return out


def edge(value):
    return jnp.where(lane_iota(HALF) < 64, value[:HALF], value[HALF:])


def packed_edges(even, odd):
    low = lane_iota(HALF) < 64
    return jnp.where(low, even, roll(odd, 64, 1)), jnp.where(low, roll(even, 64, 1), odd)


def store_edges(lo_ref, hi_ref, c, values):
    for b in range(NODES // 2):
        lo_ref[c, b], hi_ref[c, b] = packed_edges(values[2 * b], values[2 * b + 1])


def ghost_columns(left_ref, right_ref, c):
    low = lane_iota(HALF) < 64
    out = []
    for b in range(NODES // 2):
        left, right = left_ref[c, b], right_ref[c, b]
        out.append(jnp.where(low, left, roll(right, 64, 1)))
        out.append(jnp.where(low, roll(left, 64, 1), right))
    return out


def facing(left, right):
    return roll(jnp.where(lane_iota(HALF) < 64, right, left), 64, 1)


def own_assembly(u):
    count = u.shape[0]
    k = lane_iota(count) % 8
    er = row_iota(count) % HALF
    up = roll(roll(u, -1, 0), 7, 1)
    down = roll(roll(u, 1, 0), -7, 1)
    u = (
        u
        + jnp.where((k == 7) & (er < HALF - 1), up, 0.0)
        + jnp.where((k == 0) & (er > 0), down, 0.0)
    )
    top, bottom = u[:HALF], u[HALF:ROWS]
    lane = lane_iota(HALF)
    j = (lane // 8) % 8
    block = lane // 64
    new_top = (
        top
        + jnp.where(j == 7, roll(bottom, 56, 1), 0.0)
        + jnp.where((j == 0) & (block == 1), roll(bottom, 8, 1), 0.0)
    )
    new_bottom = (
        bottom
        + jnp.where(j == 0, roll(top, -56, 1), 0.0)
        + jnp.where((j == 7) & (block == 0), roll(top, -8, 1), 0.0)
    )
    if count == GROWS:
        ghost = u[ROWS:]
        new_top = new_top + jnp.where(lane < 8, roll(ghost, -56, 1), 0.0)
        new_bottom = new_bottom + jnp.where(lane >= 120, roll(ghost, 56, 1), 0.0)
    return jnp.concatenate([new_top, new_bottom], axis=0)


def ends(value):
    lane = lane_iota(HALF)
    return jnp.where(lane < 8, value[:HALF], jnp.where(lane >= 120, value[HALF:], 0.0))


def store_assembled(kv_ref, far_ref, near_ref, even, source, field=0, pack_ref=None):
    pack = None
    for i in range(NODES):
        value = own_assembly(source(i))
        kv_ref[i] = value
        if i == 0:
            first = value
        last = value
        if pack_ref is not None:
            piece = ends(value)
            if i:
                piece = roll(piece, 16 * i, 1)
            pack = piece if pack is None else pack + piece
    near_ref[field] = jnp.where(even, last, first)
    far_ref[field] = jnp.where(even, first, last)
    if pack_ref is not None:
        pack_ref[field] = pack


def is_even(place_ref):
    return lax.broadcast_in_dim(place_ref[0], (ROWS, LANES), ()) == 0


def pack_kernel(place_ref, pack_in, far_ref, near_ref, pack_ref):
    even = is_even(place_ref)
    for field in range(pack_ref.shape[0]):
        near, far = near_ref[field], far_ref[field]
        first = jnp.where(even, far, near)
        last = jnp.where(even, near, far)
        pack_ref[field, :HALF] = (
            pack_in[field] + ends(first) + roll(ends(last), 16 * (NODES - 1), 1)
        )
        if pack_ref.shape[1] > HALF:
            pack_ref[field, HALF:ROWS] = edge(first)
            pack_ref[field, ROWS:] = edge(last)


def beside(place_ref, packs_ref):
    count = packs_ref.shape[0]
    here = place_ref[1]
    return lax.rem(here + count - 1, count), lax.rem(here + 1, count)


def completed(place_ref, kv, halo, field=0):
    far_ref, near_ref = halo[:2]
    even = is_even(place_ref)
    near, far = near_ref[field], far_ref[field]
    lane = lane_iota(HALF)
    if len(halo) > 2:
        left, right = beside(place_ref, halo[2])
        side = jnp.where(
            lane % 16 < 8,
            roll(halo[2][left, field, :HALF], 8, 1),
            roll(halo[2][right, field, :HALF], -8, 1),
        )

    def value(i):
        u = kv[i]
        if len(halo) > 2:
            piece = roll(side, -16 * i, 1) if i else side
            u = u + jnp.concatenate(
                [jnp.where(lane < 8, piece, 0.0), jnp.where(lane >= 120, piece, 0.0)], axis=0
            )
        if i == 0:
            u = u + jnp.where(even, far, near)
        if i == NODES - 1:
            u = u + jnp.where(even, near, far)
        return u

    return value


def ghost_sums(place_ref, packs_ref, field=0):
    left, right = beside(place_ref, packs_ref)
    lane = lane_iota(HALF)
    own = packs_ref[place_ref[1], field, :HALF]
    lines = jnp.where(lane % 16 < 8, own, roll(own, 16, 1))
    inner = (lane >= 56) & (lane < 72)

    def value(i):
        u = jnp.where(inner, roll(lines, 56 - 16 * i, 1), 0.0)
        if i in (0, NODES - 1):
            rows = slice(HALF, ROWS) if i == 0 else slice(ROWS, GROWS)
            u = u + facing(packs_ref[left, field, rows], packs_ref[right, field, rows])
        return u

    return value


def apply_element(v_ref, metric_ref, ghost_ref, grad_ref, diver_ref, flux_ref, out_ref):
    count = v_ref.shape[1]
    side = dot_split(v_ref[...].reshape(NODES * count, LANES), grad_ref)
    flux_ref[0] = side[:, :LANES]
    flux_ref[1] = side[:, LANES:]
    for chunk in range(count // 8):
        rows = pl.ds(chunk * 8, 8)
        if chunk < ROWS // 8:
            geometry, there = metric_ref, rows
        else:
            geometry, there = ghost_ref, pl.ds(chunk * 8 - ROWS, 8)
        values = [v_ref[i, rows] for i in range(NODES)]
        grad_z = along_nodes(values, DERIV)
        flux_z = []
        for i in range(NODES):
            at = pl.ds(i * count + chunk * 8, 8)
            g_z, g_a, g_r = grad_z[i], flux_ref[0, at], flux_ref[1, at]
            m = [geometry[c, i, there] for c in range(6)]
            flux_z.append(m[0] * g_z + m[3] * g_a + m[4] * g_r)
            flux_ref[0, at] = m[3] * g_z + m[1] * g_a + m[5] * g_r
            flux_ref[1, at] = m[4] * g_z + m[5] * g_a + m[2] * g_r
        part_z = along_nodes(flux_z, DERIV.T)
        for i in range(NODES):
            out_ref[i, rows] = part_z[i] + geometry[6, i, there] * values[i]
    flux = jnp.concatenate([flux_ref[0], flux_ref[1]], axis=1)
    out_ref[...] += dot_split(flux, diver_ref).reshape(out_ref.shape)


def weight_plane():
    lane, row = lane_iota(ROWS), row_iota(ROWS)
    j, k, er = (lane // 8) % 8, lane % 8, row % HALF
    w_a = jnp.where((j == 0) | (j == 7), 0.5, 1.0)
    shared = ((k == 0) & (er > 0)) | ((k == 7) & (er < HALF - 1))
    return w_a * jnp.where(shared, 0.5, 1.0)


def node_weight(i):
    return 0.5 if i in (0, NODES - 1) else 1.0


def sum_row(sums):
    lane = lane_iota(1)
    row = jnp.zeros((1, LANES), jnp.float32)
    for d, value in enumerate(sums):
        row = jnp.where(lane == d, jnp.sum(value), row)
    return row


SIGMA = ((INTERVAL_HIGH + INTERVAL_LOW) / 2.0) / ((INTERVAL_HIGH - INTERVAL_LOW) / 2.0)
CENTER = (INTERVAL_HIGH + INTERVAL_LOW) / 2.0
HALF_WIDTH = (INTERVAL_HIGH - INTERVAL_LOW) / 2.0
RHO0 = 1.0 / SIGMA
RHO1 = 1.0 / (2.0 * SIGMA - RHO0)
RHO2 = 1.0 / (2.0 * SIGMA - RHO1)


STEP1 = 2.0 * RHO1 / HALF_WIDTH
STEP2 = 2.0 * RHO2 / HALF_WIDTH


def place_kernel(
    place_ref, order_hbm, load_hbm, geom_hbm, abs_hbm,
    metric_ref, load_kv, bound_kv, far_ref, near_ref, pack_ref, lo_ref, hi_ref,
    flux_ref, work_ref, order_ref, load_ref, geom_ref, abs_ref, sems,
):
    copies = [
        pltpu.make_async_copy(source, target, sems.at[c])
        for c, (source, target) in enumerate(
            [(order_hbm, order_ref), (load_hbm, load_ref), (geom_hbm, geom_ref), (abs_hbm, abs_ref)]
        )
    ]
    for copy in copies:
        copy.start()
    copies[0].wait()
    copies[1].wait()
    pick = jnp.where(
        lax.broadcasted_iota(jnp.int32, (64, 64), 0) == order_ref[...], 1.0, 0.0
    ).astype(jnp.bfloat16)
    low = lane_iota(ROWS) < 64

    def spread(placed, store):
        for b in range(4):
            piece = placed[:, b * LANES : (b + 1) * LANES]
            first, second = piece[:ROWS], piece[ROWS:]
            store(2 * b, jnp.where(low, first, roll(second, 64, 1)))
            store(2 * b + 1, jnp.where(low, roll(first, 64, 1), second))

    load = load_ref[...]
    high, rest = split(load)
    middle = (load - high.astype(jnp.float32) - rest.astype(jnp.float32)).astype(jnp.bfloat16)

    def store_load(i, value):
        work_ref[i] = value

    spread(dot(pick, high) + (dot(pick, rest) + dot(pick, middle)), store_load)
    even = is_even(place_ref)
    store_assembled(
        load_kv, far_ref, near_ref, even, lambda i: work_ref[i], 0, pack_ref
    )
    store_edges(lo_ref, hi_ref, 7, [edge(load_kv[i]) for i in range(NODES)])

    copies[2].wait()
    for c in range(7):

        def store_metric(i, value, c=c):
            metric_ref[c, i] = value

        spread(dot(pick, geom_ref[c]), store_metric)
        store_edges(lo_ref, hi_ref, c, [edge(metric_ref[c, i]) for i in range(NODES)])

    lane = lane_iota(8)
    q_a = jnp.zeros((8, LANES), jnp.float32)
    q_r = jnp.zeros((8, LANES), jnp.float32)
    for m in range(NODES):
        q_a = jnp.where((lane // 8) % 8 == m, float(ROW_TOTAL[m]), q_a)
        q_r = jnp.where(lane % 8 == m, float(ROW_TOTAL[m]), q_r)
    for chunk in range(ROWS // 8):
        rows = pl.ds(chunk * 8, 8)
        h_z = []
        for i in range(NODES):
            at = pl.ds(i * ROWS + chunk * 8, 8)
            q_z = float(ROW_TOTAL[i])
            g = [jnp.abs(metric_ref[c, i, rows]) for c in range(6)]
            h_z.append(g[0] * q_z + g[3] * q_a + g[4] * q_r)
            flux_ref[0, at] = g[3] * q_z + g[1] * q_a + g[5] * q_r
            flux_ref[1, at] = g[4] * q_z + g[5] * q_a + g[2] * q_r
        part_z = along_nodes_plain(h_z, ABS_DERIV.T)
        for i in range(NODES):
            work_ref[i, rows] = part_z[i] + jnp.abs(metric_ref[6, i, rows])
    flux = jnp.concatenate([flux_ref[0], flux_ref[1]], axis=1)
    copies[3].wait()
    work_ref[...] += dot_split(flux, abs_ref).reshape(FIELD)
    store_assembled(
        bound_kv, far_ref, near_ref, even, lambda i: work_ref[i], 1, pack_ref
    )
    store_edges(lo_ref, hi_ref, 8, [edge(bound_kv[i]) for i in range(NODES)])


def first_kernel(
    place_ref, load_kv, bound_kv, h0, h1, h2, left_ref, right_ref, metric_ref, grad_ref, diver_ref,
    residual_ref, inverse_ref, update_ref, ghost_inverse, ghost_metric, kv_ref, far_ref, near_ref,
    v_ref, flux_ref, work_ref,
):
    residual = completed(place_ref, load_kv, (h0, h1, h2), 0)
    bound = completed(place_ref, bound_kv, (h0, h1, h2), 1)
    for i in range(NODES):
        r = residual(i)
        inverse = 1.0 / bound(i)
        update = r * inverse * (1.0 / CENTER)
        residual_ref[i] = r
        inverse_ref[i] = inverse
        update_ref[i] = update
        v_ref[i, :ROWS] = update
    residual, residual_sums = ghost_columns(left_ref, right_ref, 7), ghost_sums(place_ref, h2, 0)
    bound, bound_sums = ghost_columns(left_ref, right_ref, 8), ghost_sums(place_ref, h2, 1)
    for i in range(NODES):
        inverse = 1.0 / (bound[i] + bound_sums(i))
        ghost_inverse[i] = inverse
        v_ref[i, ROWS:] = (residual[i] + residual_sums(i)) * inverse * (1.0 / CENTER)
    for c in range(7):
        for i, value in enumerate(ghost_columns(left_ref, right_ref, c)):
            ghost_metric[c, i] = value
    apply_element(v_ref, metric_ref, ghost_metric, grad_ref, diver_ref, flux_ref, work_ref)
    store_assembled(kv_ref, far_ref, near_ref, is_even(place_ref), lambda i: work_ref[i])


def second_kernel(
    place_ref, kv_in, h0, h1, source_ref, inverse_ref, update_in, metric_ref, grad_ref, diver_ref,
    start_ref, kv_ref, far_ref, near_ref, pack_ref, lo_ref, hi_ref, v_ref, flux_ref, work_ref,
):
    image = completed(place_ref, kv_in, (h0, h1))
    for i in range(NODES):
        old = update_in[i]
        inverse = inverse_ref[i]
        source = source_ref[i]
        update = (RHO1 * RHO0) * old + STEP1 * inverse * (source - image(i))
        result = old + update
        v_ref[i] = result
        start_ref[i] = result + (RHO2 * RHO1) * update + STEP2 * inverse * source
    apply_element(v_ref, metric_ref, None, grad_ref, diver_ref, flux_ref, work_ref)
    store_assembled(
        kv_ref, far_ref, near_ref, is_even(place_ref), lambda i: work_ref[i], 0, pack_ref
    )
    store_edges(
        lo_ref, hi_ref, 0,
        [edge(start_ref[i] - STEP2 * inverse_ref[i] * kv_ref[i]) for i in range(NODES)],
    )


def third_kernel(
    place_ref, kv_in, h0, h1, h2, left_ref, right_ref, source_ref, inverse_ref, start_ref,
    ghost_inverse, ghost_metric, metric_ref, grad_ref, diver_ref,
    result_ref, kv_ref, far_ref, near_ref, sums_ref, v_ref, flux_ref, work_ref,
):
    image = completed(place_ref, kv_in, (h0, h1, h2))
    plane = weight_plane()
    rz = jnp.zeros((ROWS, LANES), jnp.float32)
    for i in range(NODES):
        result = start_ref[i] - STEP2 * inverse_ref[i] * image(i)
        result_ref[i] = result
        v_ref[i, :ROWS] = result
        rz = rz + source_ref[i] * result * node_weight(i)
    start, sums = ghost_columns(left_ref, right_ref, 0), ghost_sums(place_ref, h2)
    for i in range(NODES):
        v_ref[i, ROWS:] = start[i] - STEP2 * ghost_inverse[i] * sums(i)
    apply_element(v_ref, metric_ref, ghost_metric, grad_ref, diver_ref, flux_ref, work_ref)
    energy = jnp.zeros((ROWS, LANES), jnp.float32)
    for i in range(NODES):
        energy = energy + result_ref[i] * work_ref[i, :ROWS]
    sums_ref[...] = sum_row([rz * plane, energy])
    store_assembled(kv_ref, far_ref, near_ref, is_even(place_ref), lambda i: work_ref[i])


def fourth_kernel(
    place_ref, kv_in, h0, h1, inverse_ref, metric_ref, grad_ref, diver_ref,
    image_ref, update_ref, kv_ref, far_ref, near_ref, pack_ref, lo_ref, hi_ref, flux_ref, work_ref,
):
    image = completed(place_ref, kv_in, (h0, h1))
    for i in range(NODES):
        value = image(i)
        image_ref[i] = value
        update_ref[i] = value * inverse_ref[i] * (1.0 / CENTER)
    apply_element(update_ref, metric_ref, None, grad_ref, diver_ref, flux_ref, work_ref)
    store_assembled(
        kv_ref, far_ref, near_ref, is_even(place_ref), lambda i: work_ref[i], 0, pack_ref
    )
    scale = 1.0 + RHO1 * RHO0 + STEP1 * CENTER
    store_edges(
        lo_ref, hi_ref, 0,
        [edge(scale * update_ref[i] - STEP1 * inverse_ref[i] * kv_ref[i]) for i in range(NODES)],
    )


def fifth_kernel(
    place_ref, kv_in, h0, h1, h2, left_ref, right_ref, source_ref, inverse_ref, update_in,
    ghost_inverse, ghost_metric, metric_ref, grad_ref, diver_ref,
    start_ref, kv_ref, far_ref, near_ref, v_ref, flux_ref, work_ref,
):
    image = completed(place_ref, kv_in, (h0, h1, h2))
    for i in range(NODES):
        old = update_in[i]
        inverse = inverse_ref[i]
        source = source_ref[i]
        update = (RHO1 * RHO0) * old + STEP1 * inverse * (source - image(i))
        result = old + update
        v_ref[i, :ROWS] = result
        start_ref[i] = result + (RHO2 * RHO1) * update + STEP2 * inverse * source
    start, sums = ghost_columns(left_ref, right_ref, 0), ghost_sums(place_ref, h2)
    for i in range(NODES):
        v_ref[i, ROWS:] = start[i] - STEP1 * ghost_inverse[i] * sums(i)
    apply_element(v_ref, metric_ref, ghost_metric, grad_ref, diver_ref, flux_ref, work_ref)
    store_assembled(kv_ref, far_ref, near_ref, is_even(place_ref), lambda i: work_ref[i])


def sixth_kernel(
    place_ref, kv_in, h0, h1, source_ref, inverse_ref, start_ref, residual_ref, first_ref, early_ref,
    metric_ref, grad_ref, diver_ref,
    result_ref, kv_ref, far_ref, near_ref, pack_ref, sums_ref, flux_ref, work_ref,
):
    image = completed(place_ref, kv_in, (h0, h1))
    plane = weight_plane()
    r_y = jnp.zeros((ROWS, LANES), jnp.float32)
    w_y = jnp.zeros((ROWS, LANES), jnp.float32)
    for i in range(NODES):
        result = start_ref[i] - STEP2 * inverse_ref[i] * image(i)
        result_ref[i] = result
        r_y = r_y + residual_ref[i] * result * node_weight(i)
        w_y = w_y + source_ref[i] * result * node_weight(i)
    apply_element(result_ref, metric_ref, None, grad_ref, diver_ref, flux_ref, work_ref)
    z_ky = jnp.zeros((ROWS, LANES), jnp.float32)
    y_ky = jnp.zeros((ROWS, LANES), jnp.float32)
    for i in range(NODES):
        z_ky = z_ky + first_ref[i] * work_ref[i]
        y_ky = y_ky + result_ref[i] * work_ref[i]
    zero = jnp.zeros((1, LANES), jnp.float32)
    late = sum_row([zero, zero, r_y * plane, w_y * plane, z_ky, y_ky])
    sums_ref[...] = jnp.broadcast_to(early_ref[...] + late, sums_ref.shape)
    store_assembled(
        kv_ref, far_ref, near_ref, is_even(place_ref), lambda i: work_ref[i], 0, pack_ref
    )


def last_kernel(
    place_ref, kv_in, h0, h1, h2, sums_ref, order_ref,
    residual_ref, first_ref, image_ref, second_ref,
    solution_ref, residual_out, spread_ref,
):
    sums = jnp.sum(sums_ref[...], axis=0, keepdims=True)
    lane = lane_iota(1)

    def total(d):
        return jnp.sum(jnp.where(lane == d, sums, 0.0), axis=1, keepdims=True)

    rz0, zw, ry, wy, zq, yq = (total(d) for d in range(6))
    alpha0 = rz0 / zw
    rz1 = rz0 - alpha0 * (zw + ry) + alpha0 * alpha0 * wy
    beta = rz1 / rz0
    share = 1.0 + beta
    energy = share * share * zw - 2.0 * share * alpha0 * zq + alpha0 * alpha0 * yq
    alpha1 = rz1 / energy
    first_scale = alpha0 + alpha1 * share
    second_scale = alpha1 * alpha0
    image = completed(place_ref, kv_in, (h0, h1, h2))
    low = lane_iota(ROWS) < 64
    for b in range(4):
        pair = []
        for i in (2 * b, 2 * b + 1):
            x = first_scale * first_ref[i] - second_scale * second_ref[i]
            r = residual_ref[i] - first_scale * image_ref[i] + second_scale * image(i)
            pair.append((x, r))
        for f in range(2):
            even, odd = pair[0][f], pair[1][f]
            lanes = pl.ds(b * LANES, LANES)
            spread_ref[f, :ROWS, lanes] = jnp.where(low, even, roll(odd, 64, 1))
            spread_ref[f, ROWS:, lanes] = jnp.where(low, roll(even, 64, 1), odd)
    pick = jnp.where(
        lax.broadcasted_iota(jnp.int32, (64, 64), 1) == order_ref[...], 1.0, 0.0
    ).astype(jnp.bfloat16)
    for f, out in ((0, solution_ref), (1, residual_out)):
        value = spread_ref[f]
        high, middle = split(value)
        rest = (value - high.astype(jnp.float32) - middle.astype(jnp.float32)).astype(jnp.bfloat16)
        out[...] = dot(pick, high) + (dot(pick, middle) + dot(pick, rest))


VMEM_LIMIT = 24 * 1024 * 1024
F32 = jnp.float32


def call(kernel, place, outs, scratch, *operands, space=pltpu.VMEM):
    vmem = pl.BlockSpec(memory_space=pltpu.VMEM)
    return pl.pallas_call(
        kernel,
        out_shape=[jax.ShapeDtypeStruct(s, F32) for s in outs],
        in_specs=[pl.BlockSpec(memory_space=pltpu.SMEM)]
        + [pl.BlockSpec(memory_space=space)] * len(operands),
        out_specs=[vmem] * len(outs),
        scratch_shapes=[pltpu.VMEM(s, F32) if isinstance(s, tuple) else s for s in scratch],
        compiler_params=pltpu.CompilerParams(vmem_limit_bytes=VMEM_LIMIT),
    )(place, *operands)


FLUX = (2, NODES * ROWS, LANES)
BIG_FLUX = (2, NODES * GROWS, LANES)


def faces(fields=1):
    return [(fields, ROWS, LANES), (fields, ROWS, LANES)]


def packs(fields=1):
    return [(fields, HALF, LANES)]


def swap_wide(far, near):
    count = lax.axis_size(WIDE)
    far = lax.ppermute(
        far, WIDE, [(w, (w + 1 if w % 2 else w - 1) % count) for w in range(count)]
    )
    near = lax.ppermute(near, WIDE, [(w, w ^ 1) for w in range(count)])
    return far, near


def swap_all(place, far, near, pack, rows):
    far, near = swap_wide(far, near)
    (pack,) = call(pack_kernel, place, [(pack.shape[0], rows, LANES)], [], pack, far, near)
    return far, near, lax.all_gather(pack, "narrow")


def edges(fields=1):
    return [(fields, NODES // 2, HALF, LANES)] * 2


def swap_edges(lo, hi):
    count = lax.axis_size("narrow")
    left = lax.ppermute(hi, "narrow", [(n, (n + 1) % count) for n in range(count)])
    right = lax.ppermute(lo, "narrow", [(n, (n - 1) % count) for n in range(count)])
    return left, right


def local(load, geom, element_order):
    place = jnp.stack([lax.axis_index(WIDE) % 2, lax.axis_index("narrow")]).astype(jnp.int32)
    grad = jnp.asarray(GRAD_HL)
    diver = jnp.asarray(DIVER_HL)
    metric, load_kv, bound_kv, *face, lo, hi = call(
        place_kernel, place,
        [(7,) + FIELD, FIELD, FIELD] + faces(2) + packs(2) + edges(9),
        [
            FLUX, FIELD,
            pltpu.VMEM((1, 64), jnp.int32), pltpu.VMEM(load.shape, load.dtype),
            pltpu.VMEM(geom.shape, geom.dtype), pltpu.VMEM(ABS_HL.shape, jnp.bfloat16),
            pltpu.SemaphoreType.DMA((4,)),
        ],
        *(pltpu.with_memory_space_constraint(x, pltpu.HBM) for x in (element_order.reshape(1, 64), load, geom, jnp.asarray(ABS_HL))),
        space=pltpu.HBM,
    )
    sides = swap_edges(lo, hi)
    halo = swap_all(place, *face, GROWS)
    residual, inverse, update, ghost_inverse, ghost_metric, kv, *face = call(
        first_kernel, place,
        [FIELD, FIELD, FIELD, GHOST, (7,) + GHOST, FIELD] + faces(),
        [BIG, BIG_FLUX, BIG],
        load_kv, bound_kv, *halo, *sides, metric, grad, diver,
    )
    halo = swap_wide(*face)
    start, kv, *face, lo, hi = call(
        second_kernel, place,
        [FIELD, FIELD] + faces() + packs() + edges(),
        [FIELD, FLUX, FIELD],
        kv, *halo, residual, inverse, update, metric, grad, diver,
    )
    sides = swap_edges(lo, hi)
    halo = swap_all(place, *face, GROWS)
    first, kv, *face, early = call(
        third_kernel, place,
        [FIELD, FIELD] + faces() + [(1, LANES)],
        [BIG, BIG_FLUX, BIG],
        kv, *halo, *sides, residual, inverse, start, ghost_inverse, ghost_metric, metric, grad, diver,
    )
    halo = swap_wide(*face)
    image, update, kv, *face, lo, hi = call(
        fourth_kernel, place,
        [FIELD, FIELD, FIELD] + faces() + packs() + edges(),
        [FLUX, FIELD],
        kv, *halo, inverse, metric, grad, diver,
    )
    sides = swap_edges(lo, hi)
    halo = swap_all(place, *face, GROWS)
    start, kv, *face = call(
        fifth_kernel, place,
        [FIELD, FIELD] + faces(),
        [BIG, BIG_FLUX, BIG],
        kv, *halo, *sides, image, inverse, update, ghost_inverse, ghost_metric, metric, grad, diver,
    )
    halo = swap_wide(*face)
    second, kv, *face, sums = call(
        sixth_kernel, place,
        [FIELD, FIELD] + faces() + packs() + [(lax.axis_size(REST), LANES)],
        [FLUX, FIELD],
        kv, *halo, image, inverse, start, residual, first, early, metric, grad, diver,
    )
    halo = swap_all(place, *face, HALF)
    sums = lax.all_to_all(sums, REST, 0, 0)
    sums = jnp.broadcast_to(
        jnp.sum(sums, axis=0, keepdims=True), (lax.axis_size("ring"), LANES)
    )
    sums = lax.all_to_all(sums, "ring", 0, 0)
    return tuple(
        call(
            last_kernel, place,
            [(64, 512), (64, 512)],
            [(2, 64, 512)],
            kv, *halo, sums, element_order.reshape(64, 1), residual, first, image, second,
        )
    )


def solution(mesh):
    wide, narrow = mesh.devices.shape
    ring = 12 if wide % 12 == 0 else 2
    fine = jax.sharding.Mesh(
        mesh.devices.reshape(wide // ring, ring, narrow), ("outer", "ring", "narrow")
    )
    rows = ("outer", "ring", "narrow")
    return jax.shard_map(
        local,
        mesh=fine,
        in_specs=(P(rows, None), P(None, rows, None), P(WIDE, "narrow", None)),
        out_specs=(P(rows, None), P(rows, None)),
        check_vma=False,
    )
```

```python
import functools

import jax
import jax.numpy as jnp
import ml_dtypes
import numpy as np
from jax import lax
from jax.experimental import pallas as pl
from jax.experimental.pallas import tpu as pltpu
from jax.sharding import PartitionSpec as P

NODES = 8
ROWS = 32
LANES = 128
HALF = 16
GROWS = ROWS + HALF
INTERVAL_LOW = 0.03
INTERVAL_HIGH = 1.0
FIELD = (NODES, ROWS, LANES)
GHOST = (NODES, HALF, LANES)
BIG = (NODES, GROWS, LANES)
WIDE = ("outer", "ring")
REST = ("outer", "narrow")


def legendre_seven(point):
    before = 1.0
    current = point
    for degree in range(1, 7):
        after = ((2.0 * degree + 1.0) * point * current - degree * before) / (degree + 1.0)
        before = current
        current = after
    return current


def gll_derivative():
    points = 8
    inner_nodes = [
        -0.8717401485096066,
        -0.5917001814331423,
        -0.2092992179024789,
        0.2092992179024789,
        0.5917001814331423,
        0.8717401485096066,
    ]
    nodes = [-1.0] + inner_nodes + [1.0]
    values_at = [legendre_seven(node) for node in nodes]
    matrix = np.zeros((points, points))
    for source in range(points):
        for target in range(points):
            if source != target:
                matrix[source, target] = values_at[source] / (
                    values_at[target] * (nodes[source] - nodes[target])
                )
    matrix[0, 0] = -(points - 1) * points / 4.0
    matrix[points - 1, points - 1] = (points - 1) * points / 4.0
    return matrix


DERIV = gll_derivative().astype(np.float32)
ABS_DERIV = np.abs(DERIV)
ROW_TOTAL = ABS_DERIV.sum(axis=1)
EYE8 = np.eye(8, dtype=np.float32)


def cycle_matrix(small):
    return np.kron(np.eye(2, dtype=np.float32), np.kron(small, EYE8))


def radial_matrix(small):
    return np.kron(np.eye(16, dtype=np.float32), small)


def split_const(matrix):
    high = matrix.astype(ml_dtypes.bfloat16)
    low = (matrix - high.astype(np.float32)).astype(ml_dtypes.bfloat16)
    return high, low


GRAD = np.concatenate([cycle_matrix(DERIV.T), radial_matrix(DERIV.T)], axis=1)
DIVER = np.concatenate([cycle_matrix(DERIV), radial_matrix(DERIV)], axis=0)
GRAD_PARTS = split_const(GRAD)
GRAD_HL = np.concatenate([GRAD_PARTS[0], GRAD_PARTS[0], GRAD_PARTS[1]], axis=0)
DIVER_HL = np.concatenate(split_const(DIVER), axis=1)
ABS_HL = np.stack(split_const(np.abs(DIVER)))


def split(value):
    high = value.astype(jnp.bfloat16)
    return high, (value - high.astype(jnp.float32)).astype(jnp.bfloat16)


def dot(left, right):
    return lax.dot_general(
        left, right, (((1,), (0,)), ((), ())), preferred_element_type=jnp.float32
    )


def dot_split(value, matrix_ref):
    high, low = split(value)
    return dot(high, matrix_ref[0]) + (dot(low, matrix_ref[0]) + dot(high, matrix_ref[1]))


def dot_grad(value, grad_ref):
    high, low = split(value)
    both = jnp.concatenate([high, low], axis=1)
    return dot(both, grad_ref[: 2 * LANES]) + dot(high, grad_ref[2 * LANES :])


def dot_diver(value, diver_ref):
    high, low = split(value)
    both = dot(high, diver_ref[...])
    return both[:, :LANES] + (both[:, LANES:] + dot(low, diver_ref[:, :LANES]))


def lane_iota(rows):
    return lax.broadcasted_iota(jnp.int32, (rows, LANES), 1)


def row_iota(rows):
    return lax.broadcasted_iota(jnp.int32, (rows, LANES), 0)


def roll(value, shift, axis):
    size = value.shape[axis]
    return pltpu.roll(value, shift % size, axis)


def along_nodes(values, small):
    half = NODES // 2
    even = [values[i] + values[NODES - 1 - i] for i in range(half)]
    odd = [values[i] - values[NODES - 1 - i] for i in range(half)]
    out = [None] * NODES
    for m in range(half):
        from_even, from_odd = None, None
        for i in range(half):
            near, far = float(small[m][i]), float(small[m][NODES - 1 - i])
            one = even[i] * (0.5 * (near + far))
            two = odd[i] * (0.5 * (near - far))
            from_even = one if from_even is None else from_even + one
            from_odd = two if from_odd is None else from_odd + two
        out[m] = from_odd + from_even
        out[NODES - 1 - m] = from_odd - from_even
    return out


def along_nodes_plain(values, small):
    out = []
    for m in range(NODES):
        total = None
        for i in range(NODES):
            term = values[i] * float(small[m][i])
            total = term if total is None else total + term
        out.append(total)
    return out


def edge(value):
    return jnp.where(lane_iota(HALF) < 64, value[:HALF], value[HALF:])


def packed_edges(even, odd):
    low = lane_iota(HALF) < 64
    return jnp.where(low, even, roll(odd, 64, 1)), jnp.where(low, roll(even, 64, 1), odd)


def store_edges(lo_ref, hi_ref, c, values):
    for b in range(NODES // 2):
        lo_ref[c, b], hi_ref[c, b] = packed_edges(values[2 * b], values[2 * b + 1])


def ghost_columns(left_ref, right_ref, c):
    low = lane_iota(HALF) < 64
    out = []
    for b in range(NODES // 2):
        left, right = left_ref[c, b], right_ref[c, b]
        out.append(jnp.where(low, left, roll(right, 64, 1)))
        out.append(jnp.where(low, roll(left, 64, 1), right))
    return out


def facing(left, right):
    return roll(jnp.where(lane_iota(HALF) < 64, right, left), 64, 1)


def own_assembly(u):
    count = u.shape[0]
    k = lane_iota(count) % 8
    er = row_iota(count) % HALF
    up = roll(roll(u, -1, 0), 7, 1)
    down = roll(roll(u, 1, 0), -7, 1)
    u = (
        u
        + jnp.where((k == 7) & (er < HALF - 1), up, 0.0)
        + jnp.where((k == 0) & (er > 0), down, 0.0)
    )
    top, bottom = u[:HALF], u[HALF:ROWS]
    lane = lane_iota(HALF)
    j = (lane // 8) % 8
    block = lane // 64
    new_top = (
        top
        + jnp.where(j == 7, roll(bottom, 56, 1), 0.0)
        + jnp.where((j == 0) & (block == 1), roll(bottom, 8, 1), 0.0)
    )
    new_bottom = (
        bottom
        + jnp.where(j == 0, roll(top, -56, 1), 0.0)
        + jnp.where((j == 7) & (block == 0), roll(top, -8, 1), 0.0)
    )
    if count == GROWS:
        ghost = u[ROWS:]
        new_top = new_top + jnp.where(lane < 8, roll(ghost, -56, 1), 0.0)
        new_bottom = new_bottom + jnp.where(lane >= 120, roll(ghost, 56, 1), 0.0)
    return jnp.concatenate([new_top, new_bottom], axis=0)


def ends(value):
    lane = lane_iota(HALF)
    return jnp.where(lane < 8, value[:HALF], jnp.where(lane >= 120, value[HALF:], 0.0))


def store_assembled(kv_ref, far_ref, near_ref, even, source, field=0, pack_ref=None):
    pack = None
    for i in range(NODES):
        value = own_assembly(source(i))
        kv_ref[i] = value
        if i == 0:
            first = value
        last = value
        if pack_ref is not None:
            piece = ends(value)
            if i:
                piece = roll(piece, 16 * i, 1)
            pack = piece if pack is None else pack + piece
    near_ref[field] = jnp.where(even, last, first)
    far_ref[field] = jnp.where(even, first, last)
    if pack_ref is not None:
        pack_ref[field] = pack


def is_even():
    return lax.broadcast_in_dim(lax.rem(lax.axis_index("ring"), 2), (ROWS, LANES), ()) == 0


def pack_kernel(pack_in, far_ref, near_ref, pack_ref):
    even = is_even()
    for field in range(pack_ref.shape[0]):
        near, far = near_ref[field], far_ref[field]
        first = jnp.where(even, far, near)
        last = jnp.where(even, near, far)
        pack_ref[field, :HALF] = (
            pack_in[field] + ends(first) + roll(ends(last), 16 * (NODES - 1), 1)
        )
        if pack_ref.shape[1] > HALF:
            pack_ref[field, HALF:ROWS] = edge(first)
            pack_ref[field, ROWS:] = edge(last)


def beside(packs_ref):
    count = packs_ref.shape[0]
    here = lax.axis_index("narrow")
    return lax.rem(here + count - 1, count), lax.rem(here + 1, count)


def completed(kv, halo, field=0):
    far_ref, near_ref = halo[:2]
    even = is_even()
    near, far = near_ref[field], far_ref[field]
    lane = lane_iota(HALF)
    if len(halo) > 2:
        left, right = beside(halo[2])
        side = jnp.where(
            lane % 16 < 8,
            roll(halo[2][left, field, :HALF], 8, 1),
            roll(halo[2][right, field, :HALF], -8, 1),
        )

    def value(i):
        u = kv[i]
        if len(halo) > 2:
            piece = roll(side, -16 * i, 1) if i else side
            u = u + jnp.concatenate(
                [jnp.where(lane < 8, piece, 0.0), jnp.where(lane >= 120, piece, 0.0)], axis=0
            )
        if i == 0:
            u = u + jnp.where(even, far, near)
        if i == NODES - 1:
            u = u + jnp.where(even, near, far)
        return u

    return value


def ghost_sums(packs_ref, field=0):
    left, right = beside(packs_ref)
    lane = lane_iota(HALF)
    own = packs_ref[lax.axis_index("narrow"), field, :HALF]
    lines = jnp.where(lane % 16 < 8, own, roll(own, 16, 1))
    inner = (lane >= 56) & (lane < 72)

    def value(i):
        u = jnp.where(inner, roll(lines, 56 - 16 * i, 1), 0.0)
        if i in (0, NODES - 1):
            rows = slice(HALF, ROWS) if i == 0 else slice(ROWS, GROWS)
            u = u + facing(packs_ref[left, field, rows], packs_ref[right, field, rows])
        return u

    return value


def apply_element(v_ref, metric_ref, ghost_ref, grad_ref, diver_ref, flux_ref, out_ref):
    count = v_ref.shape[1]
    side = dot_grad(v_ref[...].reshape(NODES * count, LANES), grad_ref)
    flux_ref[0] = side[:, :LANES]
    flux_ref[1] = side[:, LANES:]
    for chunk in range(count // 8):
        rows = pl.ds(chunk * 8, 8)
        if chunk < ROWS // 8:
            geometry, there = metric_ref, rows
        else:
            geometry, there = ghost_ref, pl.ds(chunk * 8 - ROWS, 8)
        values = [v_ref[i, rows] for i in range(NODES)]
        grad_z = along_nodes(values, DERIV)
        flux_z = []
        for i in range(NODES):
            at = pl.ds(i * count + chunk * 8, 8)
            g_z, g_a, g_r = grad_z[i], flux_ref[0, at], flux_ref[1, at]
            m = [geometry[c, i, there] for c in range(6)]
            flux_z.append(m[0] * g_z + m[3] * g_a + m[4] * g_r)
            flux_ref[0, at] = m[3] * g_z + m[1] * g_a + m[5] * g_r
            flux_ref[1, at] = m[4] * g_z + m[5] * g_a + m[2] * g_r
        part_z = along_nodes(flux_z, DERIV.T)
        for i in range(NODES):
            out_ref[i, rows] = part_z[i] + geometry[6, i, there] * values[i]
    flux = jnp.concatenate([flux_ref[0], flux_ref[1]], axis=1)
    out_ref[...] += dot_diver(flux, diver_ref).reshape(out_ref.shape)


def weight_plane():
    lane, row = lane_iota(ROWS), row_iota(ROWS)
    j, k, er = (lane // 8) % 8, lane % 8, row % HALF
    w_a = jnp.where((j == 0) | (j == 7), 0.5, 1.0)
    shared = ((k == 0) & (er > 0)) | ((k == 7) & (er < HALF - 1))
    return w_a * jnp.where(shared, 0.5, 1.0)


def node_weight(i):
    return 0.5 if i in (0, NODES - 1) else 1.0


def sum_row(sums):
    lane = lane_iota(1)
    row = jnp.zeros((1, LANES), jnp.float32)
    for d, value in enumerate(sums):
        row = jnp.where(lane == d, jnp.sum(value), row)
    return row


SIGMA = ((INTERVAL_HIGH + INTERVAL_LOW) / 2.0) / ((INTERVAL_HIGH - INTERVAL_LOW) / 2.0)
CENTER = (INTERVAL_HIGH + INTERVAL_LOW) / 2.0
HALF_WIDTH = (INTERVAL_HIGH - INTERVAL_LOW) / 2.0
RHO0 = 1.0 / SIGMA
RHO1 = 1.0 / (2.0 * SIGMA - RHO0)
RHO2 = 1.0 / (2.0 * SIGMA - RHO1)


STEP1 = 2.0 * RHO1 / HALF_WIDTH
STEP2 = 2.0 * RHO2 / HALF_WIDTH


def place_kernel(
    order_hbm, load_hbm, geom_hbm, abs_hbm,
    metric_ref, load_kv, bound_kv, far_ref, near_ref, pack_ref, lo_ref, hi_ref,
    flux_ref, work_ref, order_ref, load_ref, geom_ref, abs_ref, sems,
):
    copies = [
        pltpu.make_async_copy(source, target, sems.at[c])
        for c, (source, target) in enumerate(
            [(order_hbm, order_ref), (load_hbm, load_ref), (geom_hbm, geom_ref), (abs_hbm, abs_ref)]
        )
    ]
    for copy in copies:
        copy.start()
    copies[0].wait()
    copies[1].wait()
    pick = jnp.where(
        lax.broadcasted_iota(jnp.int32, (64, 64), 0) == order_ref[...], 1.0, 0.0
    ).astype(jnp.bfloat16)
    low = lane_iota(ROWS) < 64

    def spread(placed, store):
        for b in range(4):
            piece = placed[:, b * LANES : (b + 1) * LANES]
            first, second = piece[:ROWS], piece[ROWS:]
            store(2 * b, jnp.where(low, first, roll(second, 64, 1)))
            store(2 * b + 1, jnp.where(low, roll(first, 64, 1), second))

    load = load_ref[...]
    high, rest = split(load)
    middle = (load - high.astype(jnp.float32) - rest.astype(jnp.float32)).astype(jnp.bfloat16)

    def store_load(i, value):
        work_ref[i] = value

    spread(dot(pick, high) + (dot(pick, rest) + dot(pick, middle)), store_load)
    even = is_even()
    store_assembled(
        load_kv, far_ref, near_ref, even, lambda i: work_ref[i], 0, pack_ref
    )
    store_edges(lo_ref, hi_ref, 7, [edge(load_kv[i]) for i in range(NODES)])

    copies[2].wait()
    for c in range(7):

        def store_metric(i, value, c=c):
            metric_ref[c, i] = value

        spread(dot(pick, geom_ref[c]), store_metric)
        store_edges(lo_ref, hi_ref, c, [edge(metric_ref[c, i]) for i in range(NODES)])

    lane = lane_iota(8)
    q_a = jnp.zeros((8, LANES), jnp.float32)
    q_r = jnp.zeros((8, LANES), jnp.float32)
    for m in range(NODES):
        q_a = jnp.where((lane // 8) % 8 == m, float(ROW_TOTAL[m]), q_a)
        q_r = jnp.where(lane % 8 == m, float(ROW_TOTAL[m]), q_r)
    for chunk in range(ROWS // 8):
        rows = pl.ds(chunk * 8, 8)
        h_z = []
        for i in range(NODES):
            at = pl.ds(i * ROWS + chunk * 8, 8)
            q_z = float(ROW_TOTAL[i])
            g = [jnp.abs(metric_ref[c, i, rows]) for c in range(6)]
            h_z.append(g[0] * q_z + g[3] * q_a + g[4] * q_r)
            flux_ref[0, at] = g[3] * q_z + g[1] * q_a + g[5] * q_r
            flux_ref[1, at] = g[4] * q_z + g[5] * q_a + g[2] * q_r
        part_z = along_nodes_plain(h_z, ABS_DERIV.T)
        for i in range(NODES):
            work_ref[i, rows] = part_z[i] + jnp.abs(metric_ref[6, i, rows])
    flux = jnp.concatenate([flux_ref[0], flux_ref[1]], axis=1)
    copies[3].wait()
    work_ref[...] += dot_split(flux, abs_ref).reshape(FIELD)
    store_assembled(
        bound_kv, far_ref, near_ref, even, lambda i: work_ref[i], 1, pack_ref
    )
    store_edges(lo_ref, hi_ref, 8, [edge(bound_kv[i]) for i in range(NODES)])


def first_kernel(
    load_kv, bound_kv, h0, h1, h2, left_ref, right_ref, metric_ref, grad_ref, diver_ref,
    residual_ref, inverse_ref, update_ref, ghost_inverse, ghost_metric, kv_ref, far_ref, near_ref,
    v_ref, flux_ref, work_ref,
):
    residual = completed(load_kv, (h0, h1, h2), 0)
    bound = completed(bound_kv, (h0, h1, h2), 1)
    for i in range(NODES):
        r = residual(i)
        inverse = 1.0 / bound(i)
        update = r * inverse * (1.0 / CENTER)
        residual_ref[i] = r
        inverse_ref[i] = inverse
        update_ref[i] = update
        v_ref[i, :ROWS] = update
    residual, residual_sums = ghost_columns(left_ref, right_ref, 7), ghost_sums(h2, 0)
    bound, bound_sums = ghost_columns(left_ref, right_ref, 8), ghost_sums(h2, 1)
    for i in range(NODES):
        inverse = 1.0 / (bound[i] + bound_sums(i))
        ghost_inverse[i] = inverse
        v_ref[i, ROWS:] = (residual[i] + residual_sums(i)) * inverse * (1.0 / CENTER)
    for c in range(7):
        for i, value in enumerate(ghost_columns(left_ref, right_ref, c)):
            ghost_metric[c, i] = value
    apply_element(v_ref, metric_ref, ghost_metric, grad_ref, diver_ref, flux_ref, work_ref)
    store_assembled(kv_ref, far_ref, near_ref, is_even(), lambda i: work_ref[i])


def second_kernel(
    kv_in, h0, h1, source_ref, inverse_ref, update_in, metric_ref, grad_ref, diver_ref,
    start_ref, kv_ref, far_ref, near_ref, pack_ref, lo_ref, hi_ref, v_ref, flux_ref, work_ref,
):
    image = completed(kv_in, (h0, h1))
    for i in range(NODES):
        old = update_in[i]
        inverse = inverse_ref[i]
        source = source_ref[i]
        update = (RHO1 * RHO0) * old + STEP1 * inverse * (source - image(i))
        result = old + update
        v_ref[i] = result
        start_ref[i] = result + (RHO2 * RHO1) * update + STEP2 * inverse * source
    apply_element(v_ref, metric_ref, None, grad_ref, diver_ref, flux_ref, work_ref)
    store_assembled(
        kv_ref, far_ref, near_ref, is_even(), lambda i: work_ref[i], 0, pack_ref
    )
    store_edges(
        lo_ref, hi_ref, 0,
        [edge(start_ref[i] - STEP2 * inverse_ref[i] * kv_ref[i]) for i in range(NODES)],
    )


def third_kernel(
    kv_in, h0, h1, h2, left_ref, right_ref, source_ref, inverse_ref, start_ref,
    ghost_inverse, ghost_metric, metric_ref, grad_ref, diver_ref,
    result_ref, kv_ref, far_ref, near_ref, sums_ref, v_ref, flux_ref, work_ref,
):
    image = completed(kv_in, (h0, h1, h2))
    plane = weight_plane()
    rz = jnp.zeros((ROWS, LANES), jnp.float32)
    for i in range(NODES):
        result = start_ref[i] - STEP2 * inverse_ref[i] * image(i)
        result_ref[i] = result
        v_ref[i, :ROWS] = result
        rz = rz + source_ref[i] * result * node_weight(i)
    start, sums = ghost_columns(left_ref, right_ref, 0), ghost_sums(h2)
    for i in range(NODES):
        v_ref[i, ROWS:] = start[i] - STEP2 * ghost_inverse[i] * sums(i)
    apply_element(v_ref, metric_ref, ghost_metric, grad_ref, diver_ref, flux_ref, work_ref)
    energy = jnp.zeros((ROWS, LANES), jnp.float32)
    for i in range(NODES):
        energy = energy + result_ref[i] * work_ref[i, :ROWS]
    sums_ref[...] = sum_row([rz * plane, energy])
    store_assembled(kv_ref, far_ref, near_ref, is_even(), lambda i: work_ref[i])


def fourth_kernel(
    kv_in, h0, h1, inverse_ref, metric_ref, grad_ref, diver_ref,
    image_ref, update_ref, kv_ref, far_ref, near_ref, pack_ref, lo_ref, hi_ref, flux_ref, work_ref,
):
    image = completed(kv_in, (h0, h1))
    for i in range(NODES):
        value = image(i)
        image_ref[i] = value
        update_ref[i] = value * inverse_ref[i] * (1.0 / CENTER)
    apply_element(update_ref, metric_ref, None, grad_ref, diver_ref, flux_ref, work_ref)
    store_assembled(
        kv_ref, far_ref, near_ref, is_even(), lambda i: work_ref[i], 0, pack_ref
    )
    scale = 1.0 + RHO1 * RHO0 + STEP1 * CENTER
    store_edges(
        lo_ref, hi_ref, 0,
        [edge(scale * update_ref[i] - STEP1 * inverse_ref[i] * kv_ref[i]) for i in range(NODES)],
    )


def fifth_kernel(
    kv_in, h0, h1, h2, left_ref, right_ref, source_ref, inverse_ref, update_in,
    ghost_inverse, ghost_metric, metric_ref, grad_ref, diver_ref,
    start_ref, kv_ref, far_ref, near_ref, v_ref, flux_ref, work_ref,
):
    image = completed(kv_in, (h0, h1, h2))
    for i in range(NODES):
        old = update_in[i]
        inverse = inverse_ref[i]
        source = source_ref[i]
        update = (RHO1 * RHO0) * old + STEP1 * inverse * (source - image(i))
        result = old + update
        v_ref[i, :ROWS] = result
        start_ref[i] = result + (RHO2 * RHO1) * update + STEP2 * inverse * source
    start, sums = ghost_columns(left_ref, right_ref, 0), ghost_sums(h2)
    for i in range(NODES):
        v_ref[i, ROWS:] = start[i] - STEP1 * ghost_inverse[i] * sums(i)
    apply_element(v_ref, metric_ref, ghost_metric, grad_ref, diver_ref, flux_ref, work_ref)
    store_assembled(kv_ref, far_ref, near_ref, is_even(), lambda i: work_ref[i])


def sixth_kernel(
    kv_in, h0, h1, source_ref, inverse_ref, start_ref, residual_ref, first_ref, early_ref,
    metric_ref, grad_ref, diver_ref,
    result_ref, kv_ref, far_ref, near_ref, pack_ref, sums_ref, flux_ref, work_ref,
):
    image = completed(kv_in, (h0, h1))
    plane = weight_plane()
    r_y = jnp.zeros((ROWS, LANES), jnp.float32)
    w_y = jnp.zeros((ROWS, LANES), jnp.float32)
    for i in range(NODES):
        result = start_ref[i] - STEP2 * inverse_ref[i] * image(i)
        result_ref[i] = result
        r_y = r_y + residual_ref[i] * result * node_weight(i)
        w_y = w_y + source_ref[i] * result * node_weight(i)
    apply_element(result_ref, metric_ref, None, grad_ref, diver_ref, flux_ref, work_ref)
    z_ky = jnp.zeros((ROWS, LANES), jnp.float32)
    y_ky = jnp.zeros((ROWS, LANES), jnp.float32)
    for i in range(NODES):
        z_ky = z_ky + first_ref[i] * work_ref[i]
        y_ky = y_ky + result_ref[i] * work_ref[i]
    zero = jnp.zeros((1, LANES), jnp.float32)
    late = sum_row([zero, zero, r_y * plane, w_y * plane, z_ky, y_ky])
    sums_ref[...] = jnp.broadcast_to(early_ref[...] + late, sums_ref.shape)
    store_assembled(
        kv_ref, far_ref, near_ref, is_even(), lambda i: work_ref[i], 0, pack_ref
    )


def spread_kernel(
    kv_in, h0, h1, h2, order_ref, residual_ref, first_ref, image_ref, second_ref, out_ref, spread_ref
):
    image = completed(kv_in, (h0, h1, h2))
    low = lane_iota(ROWS) < 64
    pick = jnp.where(
        lax.broadcasted_iota(jnp.int32, (64, 64), 1) == order_ref[...], 1.0, 0.0
    ).astype(jnp.bfloat16)
    fields = [lambda i, ref=ref: ref[i] for ref in (first_ref, second_ref, residual_ref, image_ref)]
    for f, field in enumerate(fields + [image]):
        for b in range(NODES // 2):
            even, odd = field(2 * b), field(2 * b + 1)
            lanes = pl.ds(b * LANES, LANES)
            spread_ref[:ROWS, lanes] = jnp.where(low, even, roll(odd, 64, 1))
            spread_ref[ROWS:, lanes] = jnp.where(low, roll(even, 64, 1), odd)
        value = spread_ref[...]
        high, middle = split(value)
        rest = (value - high.astype(jnp.float32) - middle.astype(jnp.float32)).astype(jnp.bfloat16)
        out_ref[f] = dot(pick, high) + (dot(pick, middle) + dot(pick, rest))


def last_kernel(sums_ref, spread_ref, solution_ref, residual_ref):
    sums = jnp.sum(sums_ref[...], axis=0, keepdims=True)
    lane = lane_iota(1)

    def total(d):
        return jnp.sum(jnp.where(lane == d, sums, 0.0), axis=1, keepdims=True)

    rz0, zw, ry, wy, zq, yq = (total(d) for d in range(6))
    alpha0 = rz0 / zw
    rz1 = rz0 - alpha0 * (zw + ry) + alpha0 * alpha0 * wy
    beta = rz1 / rz0
    share = 1.0 + beta
    energy = share * share * zw - 2.0 * share * alpha0 * zq + alpha0 * alpha0 * yq
    alpha1 = rz1 / energy
    first_scale = alpha0 + alpha1 * share
    second_scale = alpha1 * alpha0
    solution_ref[...] = first_scale * spread_ref[0] - second_scale * spread_ref[1]
    residual_ref[...] = (
        spread_ref[2] - first_scale * spread_ref[3] + second_scale * spread_ref[4]
    )


VMEM_LIMIT = 24 * 1024 * 1024
F32 = jnp.float32


def call(kernel, outs, scratch, *operands, space=pltpu.VMEM, cost=None):
    vmem = pl.BlockSpec(memory_space=pltpu.VMEM)
    return pl.pallas_call(
        kernel,
        out_shape=[jax.ShapeDtypeStruct(s, F32) for s in outs],
        in_specs=[pl.BlockSpec(memory_space=space)] * len(operands),
        out_specs=[vmem] * len(outs),
        scratch_shapes=[pltpu.VMEM(s, F32) if isinstance(s, tuple) else s for s in scratch],
        cost_estimate=cost,
        compiler_params=pltpu.CompilerParams(vmem_limit_bytes=VMEM_LIMIT),
    )(*operands)


FLUX = (2, NODES * ROWS, LANES)
COST = pl.CostEstimate(flops=10**11, transcendentals=0, bytes_accessed=10**8)
BIG_FLUX = (2, NODES * GROWS, LANES)


def faces(fields=1):
    return [(fields, ROWS, LANES), (fields, ROWS, LANES)]


def packs(fields=1):
    return [(fields, HALF, LANES)]


def swap_wide(far, near):
    count = lax.axis_size(WIDE)
    far = lax.ppermute(
        far, WIDE, [(w, (w + 1 if w % 2 else w - 1) % count) for w in range(count)]
    )
    near = lax.ppermute(near, WIDE, [(w, w ^ 1) for w in range(count)])
    return far, near


def swap_all(far, near, pack, rows):
    far, near = swap_wide(far, near)
    (pack,) = call(pack_kernel, [(pack.shape[0], rows, LANES)], [], pack, far, near, cost=COST)
    return far, near, lax.all_gather(pack, "narrow")


def edges(fields=1):
    return [(fields, NODES // 2, HALF, LANES)] * 2


def swap_edges(lo, hi):
    count = lax.axis_size("narrow")
    left = lax.ppermute(hi, "narrow", [(n, (n + 1) % count) for n in range(count)])
    right = lax.ppermute(lo, "narrow", [(n, (n - 1) % count) for n in range(count)])
    return left, right


def local(load, geom, element_order):
    grad = jnp.asarray(GRAD_HL)
    diver = jnp.asarray(DIVER_HL)
    metric, load_kv, bound_kv, *face, lo, hi = call(
        place_kernel,
        [(7,) + FIELD, FIELD, FIELD] + faces(2) + packs(2) + edges(9),
        [
            FLUX, FIELD,
            pltpu.VMEM((1, 64), jnp.int32), pltpu.VMEM(load.shape, load.dtype),
            pltpu.VMEM(geom.shape, geom.dtype), pltpu.VMEM(ABS_HL.shape, jnp.bfloat16),
            pltpu.SemaphoreType.DMA((4,)),
        ],
        *(pltpu.with_memory_space_constraint(x, pltpu.HBM) for x in (element_order.reshape(1, 64), load, geom, jnp.asarray(ABS_HL))),
        space=pltpu.HBM,
    )
    sides = swap_edges(lo, hi)
    halo = swap_all(*face, GROWS)
    residual, inverse, update, ghost_inverse, ghost_metric, kv, *face = call(
        first_kernel,
        [FIELD, FIELD, FIELD, GHOST, (7,) + GHOST, FIELD] + faces(),
        [BIG, BIG_FLUX, BIG],
        load_kv, bound_kv, *halo, *sides, metric, grad, diver,
    )
    halo = swap_wide(*face)
    start, kv, *face, lo, hi = call(
        second_kernel,
        [FIELD, FIELD] + faces() + packs() + edges(),
        [FIELD, FLUX, FIELD],
        kv, *halo, residual, inverse, update, metric, grad, diver,
    )
    sides = swap_edges(lo, hi)
    halo = swap_all(*face, GROWS)
    first, kv, *face, early = call(
        third_kernel,
        [FIELD, FIELD] + faces() + [(1, LANES)],
        [BIG, BIG_FLUX, BIG],
        kv, *halo, *sides, residual, inverse, start, ghost_inverse, ghost_metric, metric, grad, diver,
    )
    halo = swap_wide(*face)
    image, update, kv, *face, lo, hi = call(
        fourth_kernel,
        [FIELD, FIELD, FIELD] + faces() + packs() + edges(),
        [FLUX, FIELD],
        kv, *halo, inverse, metric, grad, diver,
    )
    sides = swap_edges(lo, hi)
    halo = swap_all(*face, GROWS)
    start, kv, *face = call(
        fifth_kernel,
        [FIELD, FIELD] + faces(),
        [BIG, BIG_FLUX, BIG],
        kv, *halo, *sides, image, inverse, update, ghost_inverse, ghost_metric, metric, grad, diver,
    )
    halo = swap_wide(*face)
    second, kv, *face, sums = call(
        sixth_kernel,
        [FIELD, FIELD] + faces() + packs() + [(lax.axis_size(REST), LANES)],
        [FLUX, FIELD],
        kv, *halo, image, inverse, start, residual, first, early, metric, grad, diver,
    )
    halo = swap_all(*face, HALF)
    sums = lax.all_to_all(sums, REST, 0, 0)
    sums = jnp.broadcast_to(
        jnp.sum(sums, axis=0, keepdims=True), (lax.axis_size("ring"), LANES)
    )
    sums = lax.all_to_all(sums, "ring", 0, 0)
    (spread,) = call(
        spread_kernel,
        [(5, 64, 512)],
        [(64, 512)],
        kv, *halo, element_order.reshape(64, 1), residual, first, image, second,
    )
    return tuple(call(last_kernel, [(64, 512), (64, 512)], [], sums, spread))


def solution(mesh):
    wide, narrow = mesh.devices.shape
    ring = 12 if wide % 12 == 0 else 2
    fine = jax.sharding.Mesh(
        mesh.devices.reshape(wide // ring, ring, narrow), ("outer", "ring", "narrow")
    )
    rows = ("outer", "ring", "narrow")
    return jax.shard_map(
        local,
        mesh=fine,
        in_specs=(P(rows, None), P(None, rows, None), P(WIDE, "narrow", None)),
        out_specs=(P(rows, None), P(rows, None)),
        check_vma=False,
    )
```

```python
import functools

import jax
import jax.numpy as jnp
import ml_dtypes
import numpy as np
from jax import lax
from jax.experimental import pallas as pl
from jax.experimental.pallas import tpu as pltpu
from jax.sharding import PartitionSpec as P

NODES = 8
ROWS = 32
LANES = 128
HALF = 16
GROWS = ROWS + HALF
INTERVAL_LOW = 0.03
INTERVAL_HIGH = 1.0
FIELD = (NODES, ROWS, LANES)
GHOST = (NODES, HALF, LANES)
BIG = (NODES, GROWS, LANES)
WIDE = ("outer", "ring")
REST = ("outer", "narrow")


def legendre_seven(point):
    before = 1.0
    current = point
    for degree in range(1, 7):
        after = ((2.0 * degree + 1.0) * point * current - degree * before) / (degree + 1.0)
        before = current
        current = after
    return current


def gll_derivative():
    points = 8
    inner_nodes = [
        -0.8717401485096066,
        -0.5917001814331423,
        -0.2092992179024789,
        0.2092992179024789,
        0.5917001814331423,
        0.8717401485096066,
    ]
    nodes = [-1.0] + inner_nodes + [1.0]
    values_at = [legendre_seven(node) for node in nodes]
    matrix = np.zeros((points, points))
    for source in range(points):
        for target in range(points):
            if source != target:
                matrix[source, target] = values_at[source] / (
                    values_at[target] * (nodes[source] - nodes[target])
                )
    matrix[0, 0] = -(points - 1) * points / 4.0
    matrix[points - 1, points - 1] = (points - 1) * points / 4.0
    return matrix


DERIV = gll_derivative().astype(np.float32)
ABS_DERIV = np.abs(DERIV)
ROW_TOTAL = ABS_DERIV.sum(axis=1)
EYE8 = np.eye(8, dtype=np.float32)


def cycle_matrix(small):
    return np.kron(np.eye(2, dtype=np.float32), np.kron(small, EYE8))


def radial_matrix(small):
    return np.kron(np.eye(16, dtype=np.float32), small)


def split_const(matrix):
    high = matrix.astype(ml_dtypes.bfloat16)
    low = (matrix - high.astype(np.float32)).astype(ml_dtypes.bfloat16)
    return high, low


GRAD = np.concatenate([cycle_matrix(DERIV.T), radial_matrix(DERIV.T)], axis=1)
DIVER = np.concatenate([cycle_matrix(DERIV), radial_matrix(DERIV)], axis=0)
GRAD_PARTS = split_const(GRAD)
GRAD_HL = np.concatenate([GRAD_PARTS[0], GRAD_PARTS[0], GRAD_PARTS[1]], axis=0)
DIVER_HL = np.concatenate(split_const(DIVER), axis=1)
ABS_HL = np.stack(split_const(np.abs(DIVER)))


def split(value):
    high = value.astype(jnp.bfloat16)
    return high, (value - high.astype(jnp.float32)).astype(jnp.bfloat16)


def dot(left, right):
    return lax.dot_general(
        left, right, (((1,), (0,)), ((), ())), preferred_element_type=jnp.float32
    )


def dot_split(value, matrix_ref):
    high, low = split(value)
    return dot(high, matrix_ref[0]) + (dot(low, matrix_ref[0]) + dot(high, matrix_ref[1]))


def dot_grad(value, grad_ref):
    high, low = split(value)
    both = jnp.concatenate([high, low], axis=1)
    return dot(both, grad_ref[: 2 * LANES]) + dot(high, grad_ref[2 * LANES :])


def dot_diver(value, diver_ref):
    high, low = split(value)
    both = dot(high, diver_ref[...])
    return both[:, :LANES] + (both[:, LANES:] + dot(low, diver_ref[:, :LANES]))


def lane_iota(rows):
    return lax.broadcasted_iota(jnp.int32, (rows, LANES), 1)


def row_iota(rows):
    return lax.broadcasted_iota(jnp.int32, (rows, LANES), 0)


def roll(value, shift, axis):
    size = value.shape[axis]
    return pltpu.roll(value, shift % size, axis)


def along_nodes(values, small):
    half = NODES // 2
    even = [values[i] + values[NODES - 1 - i] for i in range(half)]
    odd = [values[i] - values[NODES - 1 - i] for i in range(half)]
    out = [None] * NODES
    for m in range(half):
        from_even, from_odd = None, None
        for i in range(half):
            near, far = float(small[m][i]), float(small[m][NODES - 1 - i])
            one = even[i] * (0.5 * (near + far))
            two = odd[i] * (0.5 * (near - far))
            from_even = one if from_even is None else from_even + one
            from_odd = two if from_odd is None else from_odd + two
        out[m] = from_odd + from_even
        out[NODES - 1 - m] = from_odd - from_even
    return out


def along_nodes_plain(values, small):
    out = []
    for m in range(NODES):
        total = None
        for i in range(NODES):
            term = values[i] * float(small[m][i])
            total = term if total is None else total + term
        out.append(total)
    return out


def edge(value):
    return jnp.where(lane_iota(HALF) < 64, value[:HALF], value[HALF:])


def packed_edges(even, odd):
    low = lane_iota(HALF) < 64
    return jnp.where(low, even, roll(odd, 64, 1)), jnp.where(low, roll(even, 64, 1), odd)


def store_edges(lo_ref, hi_ref, lo_at, hi_at, values):
    for b in range(NODES // 2):
        lo_ref[lo_at, b], hi_ref[hi_at, b] = packed_edges(values[2 * b], values[2 * b + 1])


def ghost_columns(lefts, rights):
    low = lane_iota(HALF) < 64
    out = []
    for b in range(NODES // 2):
        left, right = lefts[b], rights[b]
        out.append(jnp.where(low, left, roll(right, 64, 1)))
        out.append(jnp.where(low, roll(left, 64, 1), right))
    return out


def gathered_ghost(packs_ref):
    left, right = beside(packs_ref)
    half = range(NODES // 2)
    return ghost_columns(
        [packs_ref[left, 0, HALF * (5 + b) : HALF * (6 + b)] for b in half],
        [packs_ref[right, 0, HALF * (1 + b) : HALF * (2 + b)] for b in half],
    )


def facing(left, right):
    return roll(jnp.where(lane_iota(HALF) < 64, right, left), 64, 1)


def own_assembly(u):
    count = u.shape[0]
    k = lane_iota(count) % 8
    er = row_iota(count) % HALF
    up = roll(roll(u, -1, 0), 7, 1)
    down = roll(roll(u, 1, 0), -7, 1)
    u = (
        u
        + jnp.where((k == 7) & (er < HALF - 1), up, 0.0)
        + jnp.where((k == 0) & (er > 0), down, 0.0)
    )
    top, bottom = u[:HALF], u[HALF:ROWS]
    lane = lane_iota(HALF)
    j = (lane // 8) % 8
    block = lane // 64
    new_top = (
        top
        + jnp.where(j == 7, roll(bottom, 56, 1), 0.0)
        + jnp.where((j == 0) & (block == 1), roll(bottom, 8, 1), 0.0)
    )
    new_bottom = (
        bottom
        + jnp.where(j == 0, roll(top, -56, 1), 0.0)
        + jnp.where((j == 7) & (block == 0), roll(top, -8, 1), 0.0)
    )
    if count == GROWS:
        ghost = u[ROWS:]
        new_top = new_top + jnp.where(lane < 8, roll(ghost, -56, 1), 0.0)
        new_bottom = new_bottom + jnp.where(lane >= 120, roll(ghost, 56, 1), 0.0)
    return jnp.concatenate([new_top, new_bottom], axis=0)


def ends(value):
    lane = lane_iota(HALF)
    return jnp.where(lane < 8, value[:HALF], jnp.where(lane >= 120, value[HALF:], 0.0))


def store_assembled(kv_ref, far_ref, near_ref, even, source, field=0, pack_ref=None):
    pack = None
    for i in range(NODES):
        value = own_assembly(source(i))
        kv_ref[i] = value
        if i == 0:
            first = value
        last = value
        if pack_ref is not None:
            piece = ends(value)
            if i:
                piece = roll(piece, 16 * i, 1)
            pack = piece if pack is None else pack + piece
    near_ref[field] = jnp.where(even, last, first)
    far_ref[field] = jnp.where(even, first, last)
    if pack_ref is not None:
        pack_ref[field] = pack


def is_even():
    return lax.broadcast_in_dim(lax.rem(lax.axis_index("ring"), 2), (ROWS, LANES), ()) == 0


def near_face(near_ref, field, even):
    if near_ref.ndim == 4:
        return jnp.where(even, near_ref[1, field], near_ref[0, field])
    return near_ref[field]


def pack_kernel(pack_in, far_ref, near_ref, pack_ref):
    even = is_even()
    for field in range(pack_ref.shape[0]):
        near, far = near_face(near_ref, field, even), far_ref[field]
        first = jnp.where(even, far, near)
        last = jnp.where(even, near, far)
        pack_ref[field, :HALF] = (
            pack_in[field] + ends(first) + roll(ends(last), 16 * (NODES - 1), 1)
        )
        if pack_ref.shape[1] > HALF:
            pack_ref[field, HALF:ROWS] = edge(first)
            pack_ref[field, ROWS:] = edge(last)


def pack_edges_kernel(step, pack_in, edges_in, inverse_ref, far_ref, near_ref, pack_ref):
    even = is_even()
    near, far = near_ref[0], far_ref[0]
    first = jnp.where(even, far, near)
    last = jnp.where(even, near, far)
    pack_ref[0, :HALF] = pack_in[0] + ends(first) + roll(ends(last), 16 * (NODES - 1), 1)
    zero = jnp.zeros((HALF, LANES), jnp.float32)
    for b in range(NODES // 2):
        lo, hi = edges_in[0, b], edges_in[1, b]
        if b == 0:
            add = packed_edges(edge(-step * inverse_ref[0] * first), zero)
            lo, hi = lo + add[0], hi + add[1]
        if b == NODES // 2 - 1:
            add = packed_edges(zero, edge(-step * inverse_ref[NODES - 1] * last))
            lo, hi = lo + add[0], hi + add[1]
        pack_ref[0, HALF * (1 + b) : HALF * (2 + b)] = lo
        pack_ref[0, HALF * (5 + b) : HALF * (6 + b)] = hi


def beside(packs_ref):
    count = packs_ref.shape[0]
    here = lax.axis_index("narrow")
    return lax.rem(here + count - 1, count), lax.rem(here + 1, count)


def completed(kv, halo, field=0):
    far_ref, near_ref = halo[:2]
    even = is_even()
    near, far = near_face(near_ref, field, even), far_ref[field]
    lane = lane_iota(HALF)
    if len(halo) > 2:
        left, right = beside(halo[2])
        side = jnp.where(
            lane % 16 < 8,
            roll(halo[2][left, field, :HALF], 8, 1),
            roll(halo[2][right, field, :HALF], -8, 1),
        )

    def value(i):
        u = kv[i]
        if len(halo) > 2:
            piece = roll(side, -16 * i, 1) if i else side
            u = u + jnp.concatenate(
                [jnp.where(lane < 8, piece, 0.0), jnp.where(lane >= 120, piece, 0.0)], axis=0
            )
        if i == 0:
            u = u + jnp.where(even, far, near)
        if i == NODES - 1:
            u = u + jnp.where(even, near, far)
        return u

    return value


def ghost_sums(packs_ref, field=0, wide_too=False):
    left, right = beside(packs_ref)
    lane = lane_iota(HALF)
    own = packs_ref[lax.axis_index("narrow"), field, :HALF]
    lines = jnp.where(lane % 16 < 8, own, roll(own, 16, 1))
    inner = (lane >= 56) & (lane < 72)

    def value(i):
        u = jnp.where(inner, roll(lines, 56 - 16 * i, 1), 0.0)
        if wide_too and i in (0, NODES - 1):
            rows = slice(HALF, ROWS) if i == 0 else slice(ROWS, GROWS)
            u = u + facing(packs_ref[left, field, rows], packs_ref[right, field, rows])
        return u

    return value


def apply_element(v_ref, metric_ref, ghost_ref, grad_ref, diver_ref, flux_ref, out_ref):
    count = v_ref.shape[1]
    side = dot_grad(v_ref[...].reshape(NODES * count, LANES), grad_ref)
    flux_ref[0] = side[:, :LANES]
    flux_ref[1] = side[:, LANES:]
    for chunk in range(count // 8):
        rows = pl.ds(chunk * 8, 8)
        if chunk < ROWS // 8:
            geometry, there = metric_ref, rows
        else:
            geometry, there = ghost_ref, pl.ds(chunk * 8 - ROWS, 8)
        values = [v_ref[i, rows] for i in range(NODES)]
        grad_z = along_nodes(values, DERIV)
        flux_z = []
        for i in range(NODES):
            at = pl.ds(i * count + chunk * 8, 8)
            g_z, g_a, g_r = grad_z[i], flux_ref[0, at], flux_ref[1, at]
            m = [geometry[c, i, there] for c in range(6)]
            flux_z.append(m[0] * g_z + m[3] * g_a + m[4] * g_r)
            flux_ref[0, at] = m[3] * g_z + m[1] * g_a + m[5] * g_r
            flux_ref[1, at] = m[4] * g_z + m[5] * g_a + m[2] * g_r
        part_z = along_nodes(flux_z, DERIV.T)
        for i in range(NODES):
            out_ref[i, rows] = part_z[i] + geometry[6, i, there] * values[i]
    flux = jnp.concatenate([flux_ref[0], flux_ref[1]], axis=1)
    out_ref[...] += dot_diver(flux, diver_ref).reshape(out_ref.shape)


def weight_plane():
    lane, row = lane_iota(ROWS), row_iota(ROWS)
    j, k, er = (lane // 8) % 8, lane % 8, row % HALF
    w_a = jnp.where((j == 0) | (j == 7), 0.5, 1.0)
    shared = ((k == 0) & (er > 0)) | ((k == 7) & (er < HALF - 1))
    return w_a * jnp.where(shared, 0.5, 1.0)


def node_weight(i):
    return 0.5 if i in (0, NODES - 1) else 1.0


def sum_row(sums):
    lane = lane_iota(1)
    row = jnp.zeros((1, LANES), jnp.float32)
    for d, value in enumerate(sums):
        row = jnp.where(lane == d, jnp.sum(value), row)
    return row


SIGMA = ((INTERVAL_HIGH + INTERVAL_LOW) / 2.0) / ((INTERVAL_HIGH - INTERVAL_LOW) / 2.0)
CENTER = (INTERVAL_HIGH + INTERVAL_LOW) / 2.0
HALF_WIDTH = (INTERVAL_HIGH - INTERVAL_LOW) / 2.0
RHO0 = 1.0 / SIGMA
RHO1 = 1.0 / (2.0 * SIGMA - RHO0)
RHO2 = 1.0 / (2.0 * SIGMA - RHO1)


STEP1 = 2.0 * RHO1 / HALF_WIDTH
STEP2 = 2.0 * RHO2 / HALF_WIDTH


def place_kernel(
    order_hbm, load_hbm, geom_hbm, abs_hbm,
    metric_ref, load_kv, bound_kv, far_ref, near_ref, pack_ref, lo_ref, hi_ref,
    flux_ref, work_ref, order_ref, load_ref, geom_ref, abs_ref, sems,
):
    copies = [
        pltpu.make_async_copy(source, target, sems.at[c])
        for c, (source, target) in enumerate(
            [(order_hbm, order_ref), (load_hbm, load_ref), (geom_hbm, geom_ref), (abs_hbm, abs_ref)]
        )
    ]
    for copy in copies:
        copy.start()
    copies[0].wait()
    copies[1].wait()
    pick = jnp.where(
        lax.broadcasted_iota(jnp.int32, (64, 64), 0) == order_ref[...], 1.0, 0.0
    ).astype(jnp.bfloat16)
    low = lane_iota(ROWS) < 64

    def spread(placed, store):
        for b in range(4):
            piece = placed[:, b * LANES : (b + 1) * LANES]
            first, second = piece[:ROWS], piece[ROWS:]
            store(2 * b, jnp.where(low, first, roll(second, 64, 1)))
            store(2 * b + 1, jnp.where(low, roll(first, 64, 1), second))

    load = load_ref[...]
    high, rest = split(load)
    middle = (load - high.astype(jnp.float32) - rest.astype(jnp.float32)).astype(jnp.bfloat16)

    def store_load(i, value):
        work_ref[i] = value

    spread(dot(pick, high) + (dot(pick, rest) + dot(pick, middle)), store_load)
    even = is_even()
    store_assembled(
        load_kv, far_ref, near_ref, even, lambda i: work_ref[i], 0, pack_ref
    )
    store_edges(lo_ref, hi_ref, 7, 7, [edge(load_kv[i]) for i in range(NODES)])

    copies[2].wait()
    for c in range(7):

        def store_metric(i, value, c=c):
            metric_ref[c, i] = value

        spread(dot(pick, geom_ref[c]), store_metric)
        store_edges(lo_ref, hi_ref, c, c, [edge(metric_ref[c, i]) for i in range(NODES)])

    lane = lane_iota(8)
    q_a = jnp.zeros((8, LANES), jnp.float32)
    q_r = jnp.zeros((8, LANES), jnp.float32)
    for m in range(NODES):
        q_a = jnp.where((lane // 8) % 8 == m, float(ROW_TOTAL[m]), q_a)
        q_r = jnp.where(lane % 8 == m, float(ROW_TOTAL[m]), q_r)
    for chunk in range(ROWS // 8):
        rows = pl.ds(chunk * 8, 8)
        h_z = []
        for i in range(NODES):
            at = pl.ds(i * ROWS + chunk * 8, 8)
            q_z = float(ROW_TOTAL[i])
            g = [jnp.abs(metric_ref[c, i, rows]) for c in range(6)]
            h_z.append(g[0] * q_z + g[3] * q_a + g[4] * q_r)
            flux_ref[0, at] = g[3] * q_z + g[1] * q_a + g[5] * q_r
            flux_ref[1, at] = g[4] * q_z + g[5] * q_a + g[2] * q_r
        part_z = along_nodes_plain(h_z, ABS_DERIV.T)
        for i in range(NODES):
            work_ref[i, rows] = part_z[i] + jnp.abs(metric_ref[6, i, rows])
    flux = jnp.concatenate([flux_ref[0], flux_ref[1]], axis=1)
    copies[3].wait()
    work_ref[...] += dot_split(flux, abs_ref).reshape(FIELD)
    store_assembled(
        bound_kv, far_ref, near_ref, even, lambda i: work_ref[i], 1, pack_ref
    )
    store_edges(lo_ref, hi_ref, 8, 8, [edge(bound_kv[i]) for i in range(NODES)])


def first_kernel(
    load_kv, bound_kv, h0, h1, h2, left_ref, right_ref, metric_ref, grad_ref, diver_ref,
    residual_ref, inverse_ref, update_ref, ghost_inverse, ghost_metric, kv_ref, far_ref, near_ref,
    v_ref, flux_ref, work_ref,
):
    residual = completed(load_kv, (h0, h1, h2), 0)
    bound = completed(bound_kv, (h0, h1, h2), 1)
    for i in range(NODES):
        r = residual(i)
        inverse = 1.0 / bound(i)
        update = r * inverse * (1.0 / CENTER)
        residual_ref[i] = r
        inverse_ref[i] = inverse
        update_ref[i] = update
        v_ref[i, :ROWS] = update
    residual, residual_sums = ghost_columns(left_ref[7], right_ref[7]), ghost_sums(h2, 0, True)
    bound, bound_sums = ghost_columns(left_ref[8], right_ref[8]), ghost_sums(h2, 1, True)
    for i in range(NODES):
        inverse = 1.0 / (bound[i] + bound_sums(i))
        ghost_inverse[i] = inverse
        v_ref[i, ROWS:] = (residual[i] + residual_sums(i)) * inverse * (1.0 / CENTER)
    for c in range(7):
        for i, value in enumerate(ghost_columns(left_ref[c], right_ref[c])):
            ghost_metric[c, i] = value
    apply_element(v_ref, metric_ref, ghost_metric, grad_ref, diver_ref, flux_ref, work_ref)
    store_assembled(kv_ref, far_ref, near_ref, is_even(), lambda i: work_ref[i])


def second_kernel(
    kv_in, h0, h1, source_ref, inverse_ref, update_in, metric_ref, grad_ref, diver_ref,
    start_ref, kv_ref, far_ref, near_ref, pack_ref, edges_ref, v_ref, flux_ref, work_ref,
):
    image = completed(kv_in, (h0, h1))
    for i in range(NODES):
        old = update_in[i]
        inverse = inverse_ref[i]
        source = source_ref[i]
        update = (RHO1 * RHO0) * old + STEP1 * inverse * (source - image(i))
        result = old + update
        v_ref[i] = result
        start_ref[i] = result + (RHO2 * RHO1) * update + STEP2 * inverse * source
    apply_element(v_ref, metric_ref, None, grad_ref, diver_ref, flux_ref, work_ref)
    store_assembled(
        kv_ref, far_ref, near_ref, is_even(), lambda i: work_ref[i], 0, pack_ref
    )
    store_edges(
        edges_ref, edges_ref, 0, 1,
        [edge(start_ref[i] - STEP2 * inverse_ref[i] * kv_ref[i]) for i in range(NODES)],
    )


def third_kernel(
    kv_in, h0, h1, h2, source_ref, inverse_ref, start_ref,
    ghost_inverse, ghost_metric, metric_ref, grad_ref, diver_ref,
    result_ref, kv_ref, far_ref, near_ref, sums_ref, v_ref, flux_ref, work_ref,
):
    image = completed(kv_in, (h0, h1, h2))
    plane = weight_plane()
    rz = jnp.zeros((ROWS, LANES), jnp.float32)
    for i in range(NODES):
        result = start_ref[i] - STEP2 * inverse_ref[i] * image(i)
        result_ref[i] = result
        v_ref[i, :ROWS] = result
        rz = rz + source_ref[i] * result * node_weight(i)
    start, sums = gathered_ghost(h2), ghost_sums(h2)
    for i in range(NODES):
        v_ref[i, ROWS:] = start[i] - STEP2 * ghost_inverse[i] * sums(i)
    apply_element(v_ref, metric_ref, ghost_metric, grad_ref, diver_ref, flux_ref, work_ref)
    energy = jnp.zeros((ROWS, LANES), jnp.float32)
    for i in range(NODES):
        energy = energy + result_ref[i] * work_ref[i, :ROWS]
    sums_ref[...] = sum_row([rz * plane, energy])
    store_assembled(kv_ref, far_ref, near_ref, is_even(), lambda i: work_ref[i])


def fourth_kernel(
    kv_in, h0, h1, inverse_ref, metric_ref, grad_ref, diver_ref,
    image_ref, update_ref, kv_ref, far_ref, near_ref, pack_ref, edges_ref, flux_ref, work_ref,
):
    image = completed(kv_in, (h0, h1))
    for i in range(NODES):
        value = image(i)
        image_ref[i] = value
        update_ref[i] = value * inverse_ref[i] * (1.0 / CENTER)
    apply_element(update_ref, metric_ref, None, grad_ref, diver_ref, flux_ref, work_ref)
    store_assembled(
        kv_ref, far_ref, near_ref, is_even(), lambda i: work_ref[i], 0, pack_ref
    )
    scale = 1.0 + RHO1 * RHO0 + STEP1 * CENTER
    store_edges(
        edges_ref, edges_ref, 0, 1,
        [edge(scale * update_ref[i] - STEP1 * inverse_ref[i] * kv_ref[i]) for i in range(NODES)],
    )


def fifth_kernel(
    kv_in, h0, h1, h2, source_ref, inverse_ref, update_in,
    ghost_inverse, ghost_metric, metric_ref, grad_ref, diver_ref,
    start_ref, kv_ref, far_ref, near_ref, v_ref, flux_ref, work_ref,
):
    image = completed(kv_in, (h0, h1, h2))
    for i in range(NODES):
        old = update_in[i]
        inverse = inverse_ref[i]
        source = source_ref[i]
        update = (RHO1 * RHO0) * old + STEP1 * inverse * (source - image(i))
        result = old + update
        v_ref[i, :ROWS] = result
        start_ref[i] = result + (RHO2 * RHO1) * update + STEP2 * inverse * source
    start, sums = gathered_ghost(h2), ghost_sums(h2)
    for i in range(NODES):
        v_ref[i, ROWS:] = start[i] - STEP1 * ghost_inverse[i] * sums(i)
    apply_element(v_ref, metric_ref, ghost_metric, grad_ref, diver_ref, flux_ref, work_ref)
    store_assembled(kv_ref, far_ref, near_ref, is_even(), lambda i: work_ref[i])


def sixth_kernel(
    kv_in, h0, h1, source_ref, inverse_ref, start_ref, residual_ref, first_ref, early_ref,
    metric_ref, grad_ref, diver_ref,
    result_ref, kv_ref, far_ref, near_ref, pack_ref, sums_ref, flux_ref, work_ref,
):
    image = completed(kv_in, (h0, h1))
    plane = weight_plane()
    r_y = jnp.zeros((ROWS, LANES), jnp.float32)
    w_y = jnp.zeros((ROWS, LANES), jnp.float32)
    for i in range(NODES):
        result = start_ref[i] - STEP2 * inverse_ref[i] * image(i)
        result_ref[i] = result
        r_y = r_y + residual_ref[i] * result * node_weight(i)
        w_y = w_y + source_ref[i] * result * node_weight(i)
    apply_element(result_ref, metric_ref, None, grad_ref, diver_ref, flux_ref, work_ref)
    z_ky = jnp.zeros((ROWS, LANES), jnp.float32)
    y_ky = jnp.zeros((ROWS, LANES), jnp.float32)
    for i in range(NODES):
        z_ky = z_ky + first_ref[i] * work_ref[i]
        y_ky = y_ky + result_ref[i] * work_ref[i]
    zero = jnp.zeros((1, LANES), jnp.float32)
    late = sum_row([zero, zero, r_y * plane, w_y * plane, z_ky, y_ky])
    sums_ref[...] = jnp.broadcast_to(early_ref[...] + late, sums_ref.shape)
    store_assembled(
        kv_ref, far_ref, near_ref, is_even(), lambda i: work_ref[i], 0, pack_ref
    )


def spread_kernel(
    kv_in, h0, h1, h2, order_ref, residual_ref, first_ref, image_ref, second_ref, out_ref, spread_ref
):
    image = completed(kv_in, (h0, h1, h2))
    low = lane_iota(ROWS) < 64
    pick = jnp.where(
        lax.broadcasted_iota(jnp.int32, (64, 64), 1) == order_ref[...], 1.0, 0.0
    ).astype(jnp.bfloat16)
    fields = [lambda i, ref=ref: ref[i] for ref in (first_ref, second_ref, residual_ref, image_ref)]
    for f, field in enumerate(fields + [image]):
        for b in range(NODES // 2):
            even, odd = field(2 * b), field(2 * b + 1)
            lanes = pl.ds(b * LANES, LANES)
            spread_ref[:ROWS, lanes] = jnp.where(low, even, roll(odd, 64, 1))
            spread_ref[ROWS:, lanes] = jnp.where(low, roll(even, 64, 1), odd)
        value = spread_ref[...]
        high, middle = split(value)
        rest = (value - high.astype(jnp.float32) - middle.astype(jnp.float32)).astype(jnp.bfloat16)
        out_ref[f] = dot(pick, high) + (dot(pick, middle) + dot(pick, rest))


def last_kernel(sums_ref, spread_ref, solution_ref, residual_ref):
    sums = jnp.sum(sums_ref[...], axis=0, keepdims=True)
    lane = lane_iota(1)

    def total(d):
        return jnp.sum(jnp.where(lane == d, sums, 0.0), axis=1, keepdims=True)

    rz0, zw, ry, wy, zq, yq = (total(d) for d in range(6))
    alpha0 = rz0 / zw
    rz1 = rz0 - alpha0 * (zw + ry) + alpha0 * alpha0 * wy
    beta = rz1 / rz0
    share = 1.0 + beta
    energy = share * share * zw - 2.0 * share * alpha0 * zq + alpha0 * alpha0 * yq
    alpha1 = rz1 / energy
    first_scale = alpha0 + alpha1 * share
    second_scale = alpha1 * alpha0
    solution_ref[...] = first_scale * spread_ref[0] - second_scale * spread_ref[1]
    residual_ref[...] = (
        spread_ref[2] - first_scale * spread_ref[3] + second_scale * spread_ref[4]
    )


VMEM_LIMIT = 24 * 1024 * 1024
F32 = jnp.float32


def call(kernel, outs, scratch, *operands, space=pltpu.VMEM, cost=None):
    vmem = pl.BlockSpec(memory_space=pltpu.VMEM)
    return pl.pallas_call(
        kernel,
        out_shape=[jax.ShapeDtypeStruct(s, F32) for s in outs],
        in_specs=[pl.BlockSpec(memory_space=space)] * len(operands),
        out_specs=[vmem] * len(outs),
        scratch_shapes=[pltpu.VMEM(s, F32) if isinstance(s, tuple) else s for s in scratch],
        cost_estimate=cost,
        compiler_params=pltpu.CompilerParams(vmem_limit_bytes=VMEM_LIMIT),
    )(*operands)


FLUX = (2, NODES * ROWS, LANES)
COST = pl.CostEstimate(flops=10**11, transcendentals=0, bytes_accessed=10**8)
BIG_FLUX = (2, NODES * GROWS, LANES)


def faces(fields=1):
    return [(fields, ROWS, LANES), (fields, ROWS, LANES)]


def packs(fields=1):
    return [(fields, HALF, LANES)]


def swap_far(far):
    count = lax.axis_size(WIDE)
    return lax.ppermute(
        far, WIDE, [(w, (w + 1 if w % 2 else w - 1) % count) for w in range(count)]
    )


def swap_wide(far, near):
    count = lax.axis_size(WIDE)
    return swap_far(far), lax.ppermute(near, WIDE, [(w, w ^ 1) for w in range(count)])


def swap_all(far, near, pack, rows):
    far, near = swap_wide(far, near)
    (pack,) = call(pack_kernel, [(pack.shape[0], rows, LANES)], [], pack, far, near, cost=COST)
    return far, near, lax.all_gather(pack, "narrow")


def edges(fields):
    return (fields, NODES // 2, HALF, LANES)


def swap_edged(step, inverse, far, near, pack, edges_out):
    far, near = swap_wide(far, near)
    (pack,) = call(
        functools.partial(pack_edges_kernel, step),
        [(1, HALF * (1 + NODES), LANES)],
        [],
        pack, edges_out, inverse, far, near,
    )
    return far, near, lax.all_gather(pack, "narrow")


def swap_edges(lo, hi):
    count = lax.axis_size("narrow")
    left = lax.ppermute(hi, "narrow", [(n, (n + 1) % count) for n in range(count)])
    right = lax.ppermute(lo, "narrow", [(n, (n - 1) % count) for n in range(count)])
    return left, right


def local(load, geom, element_order):
    grad = jnp.asarray(GRAD_HL)
    diver = jnp.asarray(DIVER_HL)
    metric, load_kv, bound_kv, *face, lo, hi = call(
        place_kernel,
        [(7,) + FIELD, FIELD, FIELD] + faces(2) + packs(2) + [edges(9)] * 2,
        [
            FLUX, FIELD,
            pltpu.VMEM((1, 64), jnp.int32), pltpu.VMEM(load.shape, load.dtype),
            pltpu.VMEM(geom.shape, geom.dtype), pltpu.VMEM(ABS_HL.shape, jnp.bfloat16),
            pltpu.SemaphoreType.DMA((4,)),
        ],
        *(pltpu.with_memory_space_constraint(x, pltpu.HBM) for x in (element_order.reshape(1, 64), load, geom, jnp.asarray(ABS_HL))),
        space=pltpu.HBM,
    )
    sides = swap_edges(lo, hi)
    halo = swap_all(*face, GROWS)
    residual, inverse, update, ghost_inverse, ghost_metric, kv, *face = call(
        first_kernel,
        [FIELD, FIELD, FIELD, GHOST, (7,) + GHOST, FIELD] + faces(),
        [BIG, BIG_FLUX, BIG],
        load_kv, bound_kv, *halo, *sides, metric, grad, diver,
    )
    halo = swap_wide(*face)
    start, kv, *face = call(
        second_kernel,
        [FIELD, FIELD] + faces() + packs() + [edges(2)],
        [FIELD, FLUX, FIELD],
        kv, *halo, residual, inverse, update, metric, grad, diver,
    )
    halo = swap_edged(STEP2, inverse, *face)
    first, kv, *face, early = call(
        third_kernel,
        [FIELD, FIELD] + faces() + [(1, LANES)],
        [BIG, BIG_FLUX, BIG],
        kv, *halo, residual, inverse, start, ghost_inverse, ghost_metric, metric, grad, diver,
    )
    halo = swap_wide(*face)
    image, update, kv, *face = call(
        fourth_kernel,
        [FIELD, FIELD, FIELD] + faces() + packs() + [edges(2)],
        [FLUX, FIELD],
        kv, *halo, inverse, metric, grad, diver,
    )
    halo = swap_edged(STEP1, inverse, *face)
    start, kv, *face = call(
        fifth_kernel,
        [FIELD, FIELD] + faces(),
        [BIG, BIG_FLUX, BIG],
        kv, *halo, image, inverse, update, ghost_inverse, ghost_metric, metric, grad, diver,
    )
    halo = swap_wide(*face)
    second, kv, *face, sums = call(
        sixth_kernel,
        [FIELD, FIELD] + faces() + packs() + [(lax.axis_size(REST), LANES)],
        [FLUX, FIELD],
        kv, *halo, image, inverse, start, residual, first, early, metric, grad, diver,
    )
    far, near, pack = face
    far = swap_far(far)
    ring = lax.axis_size("ring")
    sums = lax.all_to_all(sums, REST, 0, 0)
    sums = jnp.broadcast_to(jnp.sum(sums, axis=0, keepdims=True), (ring, LANES))
    near, sums = lax.optimization_barrier((near, sums))
    sums = lax.all_to_all(sums, "ring", 0, 0)
    near = lax.all_gather(
        near, "ring", axis_index_groups=[[v, v + 1] for v in range(0, ring, 2)]
    )
    (pack,) = call(pack_kernel, [pack.shape], [], pack, far, near)
    halo = far, near, lax.all_gather(pack, "narrow")
    (spread,) = call(
        spread_kernel,
        [(5, 64, 512)],
        [(64, 512)],
        kv, *halo, element_order.reshape(64, 1), residual, first, image, second,
    )
    return tuple(call(last_kernel, [(64, 512), (64, 512)], [], sums, spread))


def solution(mesh):
    wide, narrow = mesh.devices.shape
    ring = 12 if wide % 12 == 0 else 2
    fine = jax.sharding.Mesh(
        mesh.devices.reshape(wide // ring, ring, narrow), ("outer", "ring", "narrow")
    )
    rows = ("outer", "ring", "narrow")
    return jax.shard_map(
        local,
        mesh=fine,
        in_specs=(P(rows, None), P(None, rows, None), P(WIDE, "narrow", None)),
        out_specs=(P(rows, None), P(rows, None)),
        check_vma=False,
    )
```

```python
import functools

import jax
import jax.numpy as jnp
import ml_dtypes
import numpy as np
from jax import lax
from jax.experimental import pallas as pl
from jax.experimental.pallas import tpu as pltpu
from jax.sharding import PartitionSpec as P

NODES = 8
ROWS = 32
LANES = 128
HALF = 16
GROWS = ROWS + HALF
INTERVAL_LOW = 0.03
INTERVAL_HIGH = 1.0
FIELD = (NODES, ROWS, LANES)
GHOST = (NODES, HALF, LANES)
BIG = (NODES, GROWS, LANES)
WIDE = ("outer", "ring")
REST = ("outer", "narrow")


def legendre_seven(point):
    before = 1.0
    current = point
    for degree in range(1, 7):
        after = ((2.0 * degree + 1.0) * point * current - degree * before) / (degree + 1.0)
        before = current
        current = after
    return current


def gll_derivative():
    points = 8
    inner_nodes = [
        -0.8717401485096066,
        -0.5917001814331423,
        -0.2092992179024789,
        0.2092992179024789,
        0.5917001814331423,
        0.8717401485096066,
    ]
    nodes = [-1.0] + inner_nodes + [1.0]
    values_at = [legendre_seven(node) for node in nodes]
    matrix = np.zeros((points, points))
    for source in range(points):
        for target in range(points):
            if source != target:
                matrix[source, target] = values_at[source] / (
                    values_at[target] * (nodes[source] - nodes[target])
                )
    matrix[0, 0] = -(points - 1) * points / 4.0
    matrix[points - 1, points - 1] = (points - 1) * points / 4.0
    return matrix


DERIV = gll_derivative().astype(np.float32)
ABS_DERIV = np.abs(DERIV)
ROW_TOTAL = ABS_DERIV.sum(axis=1)
EYE8 = np.eye(8, dtype=np.float32)


def cycle_matrix(small):
    return np.kron(np.eye(2, dtype=np.float32), np.kron(small, EYE8))


def radial_matrix(small):
    return np.kron(np.eye(16, dtype=np.float32), small)


def split_const(matrix):
    high = matrix.astype(ml_dtypes.bfloat16)
    low = (matrix - high.astype(np.float32)).astype(ml_dtypes.bfloat16)
    return high, low


GRAD = np.concatenate([cycle_matrix(DERIV.T), radial_matrix(DERIV.T)], axis=1)
DIVER = np.concatenate([cycle_matrix(DERIV), radial_matrix(DERIV)], axis=0)
GRAD_PARTS = split_const(GRAD)
GRAD_HL = np.concatenate([GRAD_PARTS[0], GRAD_PARTS[0], GRAD_PARTS[1]], axis=0)
DIVER_HL = np.concatenate(split_const(DIVER), axis=1)
ABS_HL = np.stack(split_const(np.abs(DIVER)))


def split(value):
    high = value.astype(jnp.bfloat16)
    return high, (value - high.astype(jnp.float32)).astype(jnp.bfloat16)


def dot(left, right):
    return lax.dot_general(
        left, right, (((1,), (0,)), ((), ())), preferred_element_type=jnp.float32
    )


def dot_split(value, matrix_ref):
    high, low = split(value)
    return dot(high, matrix_ref[0]) + (dot(low, matrix_ref[0]) + dot(high, matrix_ref[1]))


def dot_grad(value, grad_ref):
    high, low = split(value)
    both = jnp.concatenate([high, low], axis=1)
    return dot(both, grad_ref[: 2 * LANES]) + dot(high, grad_ref[2 * LANES :])


def dot_diver(value, diver_ref):
    high, low = split(value)
    both = dot(high, diver_ref[...])
    return both[:, :LANES] + (both[:, LANES:] + dot(low, diver_ref[:, :LANES]))


def lane_iota(rows):
    return lax.broadcasted_iota(jnp.int32, (rows, LANES), 1)


def row_iota(rows):
    return lax.broadcasted_iota(jnp.int32, (rows, LANES), 0)


def roll(value, shift, axis):
    size = value.shape[axis]
    return pltpu.roll(value, shift % size, axis)


def along_nodes(values, small):
    half = NODES // 2
    even = [values[i] + values[NODES - 1 - i] for i in range(half)]
    odd = [values[i] - values[NODES - 1 - i] for i in range(half)]
    out = [None] * NODES
    for m in range(half):
        from_even, from_odd = None, None
        for i in range(half):
            near, far = float(small[m][i]), float(small[m][NODES - 1 - i])
            one = even[i] * (0.5 * (near + far))
            two = odd[i] * (0.5 * (near - far))
            from_even = one if from_even is None else from_even + one
            from_odd = two if from_odd is None else from_odd + two
        out[m] = from_odd + from_even
        out[NODES - 1 - m] = from_odd - from_even
    return out


def along_nodes_plain(values, small):
    out = []
    for m in range(NODES):
        total = None
        for i in range(NODES):
            term = values[i] * float(small[m][i])
            total = term if total is None else total + term
        out.append(total)
    return out


def edge(value):
    return jnp.where(lane_iota(HALF) < 64, value[:HALF], value[HALF:])


def packed_edges(even, odd):
    low = lane_iota(HALF) < 64
    return jnp.where(low, even, roll(odd, 64, 1)), jnp.where(low, roll(even, 64, 1), odd)


def store_edges(lo_ref, hi_ref, lo_at, hi_at, values):
    for b in range(NODES // 2):
        lo_ref[lo_at, b], hi_ref[hi_at, b] = packed_edges(values[2 * b], values[2 * b + 1])


def ghost_columns(lefts, rights):
    low = lane_iota(HALF) < 64
    out = []
    for b in range(NODES // 2):
        left, right = lefts[b], rights[b]
        out.append(jnp.where(low, left, roll(right, 64, 1)))
        out.append(jnp.where(low, roll(left, 64, 1), right))
    return out


def gathered_ghost(packs_ref):
    left, right = beside(packs_ref)
    half = range(NODES // 2)
    return ghost_columns(
        [packs_ref[left, 0, HALF * (5 + b) : HALF * (6 + b)] for b in half],
        [packs_ref[right, 0, HALF * (1 + b) : HALF * (2 + b)] for b in half],
    )


def facing(left, right):
    return roll(jnp.where(lane_iota(HALF) < 64, right, left), 64, 1)


def own_assembly(u):
    count = u.shape[0]
    k = lane_iota(count) % 8
    er = row_iota(count) % HALF
    up = roll(roll(u, -1, 0), 7, 1)
    down = roll(roll(u, 1, 0), -7, 1)
    u = (
        u
        + jnp.where((k == 7) & (er < HALF - 1), up, 0.0)
        + jnp.where((k == 0) & (er > 0), down, 0.0)
    )
    top, bottom = u[:HALF], u[HALF:ROWS]
    lane = lane_iota(HALF)
    j = (lane // 8) % 8
    block = lane // 64
    new_top = (
        top
        + jnp.where(j == 7, roll(bottom, 56, 1), 0.0)
        + jnp.where((j == 0) & (block == 1), roll(bottom, 8, 1), 0.0)
    )
    new_bottom = (
        bottom
        + jnp.where(j == 0, roll(top, -56, 1), 0.0)
        + jnp.where((j == 7) & (block == 0), roll(top, -8, 1), 0.0)
    )
    if count == GROWS:
        ghost = u[ROWS:]
        new_top = new_top + jnp.where(lane < 8, roll(ghost, -56, 1), 0.0)
        new_bottom = new_bottom + jnp.where(lane >= 120, roll(ghost, 56, 1), 0.0)
    return jnp.concatenate([new_top, new_bottom], axis=0)


def ends(value):
    lane = lane_iota(HALF)
    return jnp.where(lane < 8, value[:HALF], jnp.where(lane >= 120, value[HALF:], 0.0))


def store_assembled(kv_ref, far_ref, near_ref, even, source, field=0, pack_ref=None):
    pack = None
    for i in range(NODES):
        value = own_assembly(source(i))
        kv_ref[i] = value
        if i == 0:
            first = value
        last = value
        if pack_ref is not None:
            piece = ends(value)
            if i:
                piece = roll(piece, 16 * i, 1)
            pack = piece if pack is None else pack + piece
    near_ref[field] = jnp.where(even, last, first)
    far_ref[field] = jnp.where(even, first, last)
    if pack_ref is not None:
        pack_ref[field] = pack


def is_even():
    return lax.broadcast_in_dim(lax.rem(lax.axis_index("ring"), 2), (ROWS, LANES), ()) == 0


def near_face(near_ref, field, even):
    if near_ref.ndim == 4:
        return jnp.where(even, near_ref[1, field], near_ref[0, field])
    return near_ref[field]


def pack_kernel(pack_in, far_ref, near_ref, pack_ref):
    even = is_even()
    for field in range(pack_ref.shape[0]):
        near, far = near_face(near_ref, field, even), far_ref[field]
        first = jnp.where(even, far, near)
        last = jnp.where(even, near, far)
        pack_ref[field, :HALF] = (
            pack_in[field] + ends(first) + roll(ends(last), 16 * (NODES - 1), 1)
        )
        if pack_ref.shape[1] > HALF:
            pack_ref[field, HALF:ROWS] = edge(first)
            pack_ref[field, ROWS:] = edge(last)


def pack_edges_kernel(step, pack_in, edges_in, inverse_ref, far_ref, near_ref, pack_ref):
    even = is_even()
    near, far = near_ref[0], far_ref[0]
    first = jnp.where(even, far, near)
    last = jnp.where(even, near, far)
    pack_ref[0, :HALF] = pack_in[0] + ends(first) + roll(ends(last), 16 * (NODES - 1), 1)
    zero = jnp.zeros((HALF, LANES), jnp.float32)
    for b in range(NODES // 2):
        lo, hi = edges_in[0, b], edges_in[1, b]
        if b == 0:
            add = packed_edges(edge(-step * inverse_ref[0] * first), zero)
            lo, hi = lo + add[0], hi + add[1]
        if b == NODES // 2 - 1:
            add = packed_edges(zero, edge(-step * inverse_ref[NODES - 1] * last))
            lo, hi = lo + add[0], hi + add[1]
        pack_ref[0, HALF * (1 + b) : HALF * (2 + b)] = lo
        pack_ref[0, HALF * (5 + b) : HALF * (6 + b)] = hi


WHOLE = (1, 3, 5)
LINES = (0, 2, 4, 6)


def line_pack(field):
    pack = None
    for i in range(NODES):
        piece = ends(field(i))
        if i:
            piece = roll(piece, 16 * i, 1)
        pack = piece if pack is None else pack + piece
    return pack


def ghost_lines(left, right):
    lane = lane_iota(HALF)
    both = jnp.where(lane % 16 >= 8, left, right)
    inner = (lane >= 56) & (lane < 72)
    return [jnp.where(inner, roll(both, 64 - 16 * i, 1), 0.0) for i in range(NODES)]


def beside(packs_ref):
    count = packs_ref.shape[0]
    here = lax.axis_index("narrow")
    return lax.rem(here + count - 1, count), lax.rem(here + 1, count)


def completed(kv, halo, field=0):
    far_ref, near_ref = halo[:2]
    even = is_even()
    near, far = near_face(near_ref, field, even), far_ref[field]
    lane = lane_iota(HALF)
    if len(halo) > 2:
        left, right = beside(halo[2])
        side = jnp.where(
            lane % 16 < 8,
            roll(halo[2][left, field, :HALF], 8, 1),
            roll(halo[2][right, field, :HALF], -8, 1),
        )

    def value(i):
        u = kv[i]
        if len(halo) > 2:
            piece = roll(side, -16 * i, 1) if i else side
            u = u + jnp.concatenate(
                [jnp.where(lane < 8, piece, 0.0), jnp.where(lane >= 120, piece, 0.0)], axis=0
            )
        if i == 0:
            u = u + jnp.where(even, far, near)
        if i == NODES - 1:
            u = u + jnp.where(even, near, far)
        return u

    return value


def ghost_sums(packs_ref, field=0, wide_too=False):
    left, right = beside(packs_ref)
    lane = lane_iota(HALF)
    own = packs_ref[lax.axis_index("narrow"), field, :HALF]
    lines = jnp.where(lane % 16 < 8, own, roll(own, 16, 1))
    inner = (lane >= 56) & (lane < 72)

    def value(i):
        u = jnp.where(inner, roll(lines, 56 - 16 * i, 1), 0.0)
        if wide_too and i in (0, NODES - 1):
            rows = slice(HALF, ROWS) if i == 0 else slice(ROWS, GROWS)
            u = u + facing(packs_ref[left, field, rows], packs_ref[right, field, rows])
        return u

    return value


def apply_flux(v_ref, metric_ref, ghost_ref, grad_ref, flux_ref, part_ref):
    count = v_ref.shape[1]
    side = dot_grad(v_ref[...].reshape(NODES * count, LANES), grad_ref)
    flux_ref[0] = side[:, :LANES]
    flux_ref[1] = side[:, LANES:]
    for chunk in range(count // 8):
        rows = pl.ds(chunk * 8, 8)
        if chunk < ROWS // 8:
            geometry, there = metric_ref, rows
        else:
            geometry, there = ghost_ref, pl.ds(chunk * 8 - ROWS, 8)
        values = [v_ref[i, rows] for i in range(NODES)]
        grad_z = along_nodes(values, DERIV)
        flux_z = []
        for i in range(NODES):
            at = pl.ds(i * count + chunk * 8, 8)
            g_z, g_a, g_r = grad_z[i], flux_ref[0, at], flux_ref[1, at]
            m = [geometry[c, i, there] for c in range(6)]
            flux_z.append(m[0] * g_z + m[3] * g_a + m[4] * g_r)
            flux_ref[0, at] = m[3] * g_z + m[1] * g_a + m[5] * g_r
            flux_ref[1, at] = m[4] * g_z + m[5] * g_a + m[2] * g_r
        part_z = along_nodes(flux_z, DERIV.T)
        for i in range(NODES):
            part_ref[i, rows] = part_z[i] + geometry[6, i, there] * values[i]


def whole_planes(flux_ref, part_ref, diver_ref, planes):
    count = part_ref.shape[1]

    def flux(f):
        if len(planes) == NODES:
            return flux_ref[f]
        return jnp.concatenate([flux_ref[f, i * count : (i + 1) * count] for i in planes], axis=0)

    total = dot_diver(jnp.concatenate([flux(0), flux(1)], axis=1), diver_ref)
    return [
        part_ref[i] + total[n * count : (n + 1) * count] for n, i in enumerate(planes)
    ]


def store_faces(flux_ref, part_ref, diver_ref, far_ref, near_ref):
    first, last = (
        own_assembly(u) for u in whole_planes(flux_ref, part_ref, diver_ref, (0, NODES - 1))
    )
    even = is_even()
    near_ref[0] = jnp.where(even, last, first)
    far_ref[0] = jnp.where(even, first, last)


def apply_element(v_ref, metric_ref, ghost_ref, grad_ref, diver_ref, flux_ref, out_ref):
    apply_flux(v_ref, metric_ref, ghost_ref, grad_ref, flux_ref, out_ref)
    planes = whole_planes(flux_ref, out_ref, diver_ref, range(NODES))
    for i in range(NODES):
        out_ref[i] = planes[i]


def rest_kernel(flux_ref, part_ref, diver_ref, kv_ref):
    for i, u in enumerate(whole_planes(flux_ref, part_ref, diver_ref, range(NODES))):
        kv_ref[i] = own_assembly(u)


def rest_energy_kernel(flux_ref, part_ref, diver_ref, v_ref, sums_in, kv_ref, sums_ref):
    energy = jnp.zeros((ROWS, LANES), jnp.float32)
    for i, u in enumerate(whole_planes(flux_ref, part_ref, diver_ref, range(NODES))):
        kv_ref[i] = own_assembly(u)
        energy = energy + v_ref[i] * u[:ROWS]
    sums_ref[...] = sums_in[...] + sum_row([jnp.zeros((1, LANES), jnp.float32), energy])


def rest_edges_kernel(
    step, flux_ref, part_ref, diver_ref, start_ref, inverse_ref, kv_ref, pack_ref, edges_ref
):
    for i, u in enumerate(whole_planes(flux_ref, part_ref, diver_ref, range(NODES))):
        kv_ref[i] = own_assembly(u)
    pack_ref[0] = line_pack(lambda i: kv_ref[i])
    store_edges(
        edges_ref, edges_ref, 0, 1,
        [edge(start_ref[i] - step * inverse_ref[i] * kv_ref[i]) for i in range(NODES)],
    )


def weight_plane():
    lane, row = lane_iota(ROWS), row_iota(ROWS)
    j, k, er = (lane // 8) % 8, lane % 8, row % HALF
    w_a = jnp.where((j == 0) | (j == 7), 0.5, 1.0)
    shared = ((k == 0) & (er > 0)) | ((k == 7) & (er < HALF - 1))
    return w_a * jnp.where(shared, 0.5, 1.0)


def node_weight(i):
    return 0.5 if i in (0, NODES - 1) else 1.0


def sum_row(sums):
    lane = lane_iota(1)
    row = jnp.zeros((1, LANES), jnp.float32)
    for d, value in enumerate(sums):
        row = jnp.where(lane == d, jnp.sum(value), row)
    return row


SIGMA = ((INTERVAL_HIGH + INTERVAL_LOW) / 2.0) / ((INTERVAL_HIGH - INTERVAL_LOW) / 2.0)
CENTER = (INTERVAL_HIGH + INTERVAL_LOW) / 2.0
HALF_WIDTH = (INTERVAL_HIGH - INTERVAL_LOW) / 2.0
RHO0 = 1.0 / SIGMA
RHO1 = 1.0 / (2.0 * SIGMA - RHO0)
RHO2 = 1.0 / (2.0 * SIGMA - RHO1)


STEP1 = 2.0 * RHO1 / HALF_WIDTH
STEP2 = 2.0 * RHO2 / HALF_WIDTH


def place_kernel(
    order_hbm, load_hbm, geom_hbm, abs_hbm,
    metric_ref, load_kv, bound_kv, far_ref, near_ref, pack_ref, lo_ref, hi_ref,
    flux_ref, work_ref, order_ref, load_ref, geom_ref, abs_ref, sems,
):
    copies = [
        pltpu.make_async_copy(source, target, sems.at[c])
        for c, (source, target) in enumerate(
            [(order_hbm, order_ref), (load_hbm, load_ref), (geom_hbm, geom_ref), (abs_hbm, abs_ref)]
        )
    ]
    for copy in copies:
        copy.start()
    copies[0].wait()
    copies[1].wait()
    pick = jnp.where(
        lax.broadcasted_iota(jnp.int32, (64, 64), 0) == order_ref[...], 1.0, 0.0
    ).astype(jnp.bfloat16)
    low = lane_iota(ROWS) < 64

    def spread(placed, store):
        for b in range(4):
            piece = placed[:, b * LANES : (b + 1) * LANES]
            first, second = piece[:ROWS], piece[ROWS:]
            store(2 * b, jnp.where(low, first, roll(second, 64, 1)))
            store(2 * b + 1, jnp.where(low, roll(first, 64, 1), second))

    load = load_ref[...]
    high, rest = split(load)
    middle = (load - high.astype(jnp.float32) - rest.astype(jnp.float32)).astype(jnp.bfloat16)

    def store_load(i, value):
        work_ref[i] = value

    spread(dot(pick, high) + (dot(pick, rest) + dot(pick, middle)), store_load)
    even = is_even()
    store_assembled(
        load_kv, far_ref, near_ref, even, lambda i: work_ref[i], 0, pack_ref
    )
    store_edges(lo_ref, hi_ref, 3, 3, [edge(load_kv[i]) for i in range(NODES)])

    copies[2].wait()
    for c in range(7):

        def store_metric(i, value, c=c):
            metric_ref[c, i] = value

        spread(dot(pick, geom_ref[c]), store_metric)
    for slot, c in enumerate(WHOLE):
        store_edges(lo_ref, hi_ref, slot, slot, [edge(metric_ref[c, i]) for i in range(NODES)])
    for slot, c in enumerate(LINES):
        lines = line_pack(lambda i, c=c: metric_ref[c, i])
        lo_ref[5, slot] = lines
        hi_ref[5, slot] = lines

    lane = lane_iota(8)
    q_a = jnp.zeros((8, LANES), jnp.float32)
    q_r = jnp.zeros((8, LANES), jnp.float32)
    for m in range(NODES):
        q_a = jnp.where((lane // 8) % 8 == m, float(ROW_TOTAL[m]), q_a)
        q_r = jnp.where(lane % 8 == m, float(ROW_TOTAL[m]), q_r)
    for chunk in range(ROWS // 8):
        rows = pl.ds(chunk * 8, 8)
        h_z = []
        for i in range(NODES):
            at = pl.ds(i * ROWS + chunk * 8, 8)
            q_z = float(ROW_TOTAL[i])
            g = [jnp.abs(metric_ref[c, i, rows]) for c in range(6)]
            h_z.append(g[0] * q_z + g[3] * q_a + g[4] * q_r)
            flux_ref[0, at] = g[3] * q_z + g[1] * q_a + g[5] * q_r
            flux_ref[1, at] = g[4] * q_z + g[5] * q_a + g[2] * q_r
        part_z = along_nodes_plain(h_z, ABS_DERIV.T)
        for i in range(NODES):
            work_ref[i, rows] = part_z[i] + jnp.abs(metric_ref[6, i, rows])
    flux = jnp.concatenate([flux_ref[0], flux_ref[1]], axis=1)
    copies[3].wait()
    work_ref[...] += dot_split(flux, abs_ref).reshape(FIELD)
    store_assembled(
        bound_kv, far_ref, near_ref, even, lambda i: work_ref[i], 1, pack_ref
    )
    store_edges(lo_ref, hi_ref, 4, 4, [edge(bound_kv[i]) for i in range(NODES)])


def first_kernel(
    load_kv, bound_kv, h0, h1, h2, left_ref, right_ref, metric_ref, grad_ref, diver_ref,
    residual_ref, inverse_ref, update_ref, ghost_inverse, ghost_metric, flux_ref, part_ref, far_ref, near_ref,
    v_ref,
):
    residual = completed(load_kv, (h0, h1, h2), 0)
    bound = completed(bound_kv, (h0, h1, h2), 1)
    for i in range(NODES):
        r = residual(i)
        inverse = 1.0 / bound(i)
        update = r * inverse * (1.0 / CENTER)
        residual_ref[i] = r
        inverse_ref[i] = inverse
        update_ref[i] = update
        v_ref[i, :ROWS] = update
    residual, residual_sums = ghost_columns(left_ref[3], right_ref[3]), ghost_sums(h2, 0, True)
    bound, bound_sums = ghost_columns(left_ref[4], right_ref[4]), ghost_sums(h2, 1, True)
    for i in range(NODES):
        inverse = 1.0 / (bound[i] + bound_sums(i))
        ghost_inverse[i] = inverse
        v_ref[i, ROWS:] = (residual[i] + residual_sums(i)) * inverse * (1.0 / CENTER)
    for slot, c in enumerate(WHOLE):
        for i, value in enumerate(ghost_columns(left_ref[slot], right_ref[slot])):
            ghost_metric[c, i] = value
    for slot, c in enumerate(LINES):
        for i, value in enumerate(ghost_lines(left_ref[5, slot], right_ref[5, slot])):
            ghost_metric[c, i] = value
    apply_flux(v_ref, metric_ref, ghost_metric, grad_ref, flux_ref, part_ref)
    store_faces(flux_ref, part_ref, diver_ref, far_ref, near_ref)


def second_kernel(
    kv_in, h0, h1, source_ref, inverse_ref, update_in, metric_ref, grad_ref, diver_ref,
    start_ref, flux_ref, part_ref, far_ref, near_ref, v_ref,
):
    image = completed(kv_in, (h0, h1))
    for i in range(NODES):
        old = update_in[i]
        inverse = inverse_ref[i]
        source = source_ref[i]
        update = (RHO1 * RHO0) * old + STEP1 * inverse * (source - image(i))
        result = old + update
        v_ref[i] = result
        start_ref[i] = result + (RHO2 * RHO1) * update + STEP2 * inverse * source
    apply_flux(v_ref, metric_ref, None, grad_ref, flux_ref, part_ref)
    store_faces(flux_ref, part_ref, diver_ref, far_ref, near_ref)


def third_kernel(
    kv_in, h0, h1, h2, source_ref, inverse_ref, start_ref,
    ghost_inverse, ghost_metric, metric_ref, grad_ref, diver_ref,
    result_ref, flux_ref, part_ref, far_ref, near_ref, sums_ref, v_ref,
):
    image = completed(kv_in, (h0, h1, h2))
    plane = weight_plane()
    rz = jnp.zeros((ROWS, LANES), jnp.float32)
    for i in range(NODES):
        result = start_ref[i] - STEP2 * inverse_ref[i] * image(i)
        result_ref[i] = result
        v_ref[i, :ROWS] = result
        rz = rz + source_ref[i] * result * node_weight(i)
    start, sums = gathered_ghost(h2), ghost_sums(h2)
    for i in range(NODES):
        v_ref[i, ROWS:] = start[i] - STEP2 * ghost_inverse[i] * sums(i)
    apply_flux(v_ref, metric_ref, ghost_metric, grad_ref, flux_ref, part_ref)
    store_faces(flux_ref, part_ref, diver_ref, far_ref, near_ref)
    sums_ref[...] = sum_row([rz * plane])


def fourth_kernel(
    kv_in, h0, h1, inverse_ref, metric_ref, grad_ref, diver_ref,
    image_ref, update_ref, start_ref, flux_ref, part_ref, far_ref, near_ref,
):
    image = completed(kv_in, (h0, h1))
    for i in range(NODES):
        value = image(i)
        image_ref[i] = value
        update = value * inverse_ref[i] * (1.0 / CENTER)
        update_ref[i] = update
        start_ref[i] = (1.0 + RHO1 * RHO0 + STEP1 * CENTER) * update
    apply_flux(update_ref, metric_ref, None, grad_ref, flux_ref, part_ref)
    store_faces(flux_ref, part_ref, diver_ref, far_ref, near_ref)


def fifth_kernel(
    kv_in, h0, h1, h2, source_ref, inverse_ref, update_in,
    ghost_inverse, ghost_metric, metric_ref, grad_ref, diver_ref,
    start_ref, flux_ref, part_ref, far_ref, near_ref, v_ref,
):
    image = completed(kv_in, (h0, h1, h2))
    for i in range(NODES):
        old = update_in[i]
        inverse = inverse_ref[i]
        source = source_ref[i]
        update = (RHO1 * RHO0) * old + STEP1 * inverse * (source - image(i))
        result = old + update
        v_ref[i, :ROWS] = result
        start_ref[i] = result + (RHO2 * RHO1) * update + STEP2 * inverse * source
    start, sums = gathered_ghost(h2), ghost_sums(h2)
    for i in range(NODES):
        v_ref[i, ROWS:] = start[i] - STEP1 * ghost_inverse[i] * sums(i)
    apply_flux(v_ref, metric_ref, ghost_metric, grad_ref, flux_ref, part_ref)
    store_faces(flux_ref, part_ref, diver_ref, far_ref, near_ref)


def sixth_kernel(
    kv_in, h0, h1, source_ref, inverse_ref, start_ref, residual_ref, first_ref, early_ref,
    metric_ref, grad_ref, diver_ref,
    result_ref, kv_ref, far_ref, near_ref, pack_ref, sums_ref, flux_ref, work_ref,
):
    image = completed(kv_in, (h0, h1))
    plane = weight_plane()
    r_y = jnp.zeros((ROWS, LANES), jnp.float32)
    w_y = jnp.zeros((ROWS, LANES), jnp.float32)
    for i in range(NODES):
        result = start_ref[i] - STEP2 * inverse_ref[i] * image(i)
        result_ref[i] = result
        r_y = r_y + residual_ref[i] * result * node_weight(i)
        w_y = w_y + source_ref[i] * result * node_weight(i)
    apply_element(result_ref, metric_ref, None, grad_ref, diver_ref, flux_ref, work_ref)
    z_ky = jnp.zeros((ROWS, LANES), jnp.float32)
    y_ky = jnp.zeros((ROWS, LANES), jnp.float32)
    for i in range(NODES):
        z_ky = z_ky + first_ref[i] * work_ref[i]
        y_ky = y_ky + result_ref[i] * work_ref[i]
    zero = jnp.zeros((1, LANES), jnp.float32)
    late = sum_row([zero, zero, r_y * plane, w_y * plane, z_ky, y_ky])
    sums_ref[...] = jnp.broadcast_to(early_ref[...] + late, sums_ref.shape)
    store_assembled(
        kv_ref, far_ref, near_ref, is_even(), lambda i: work_ref[i], 0, pack_ref
    )


def spread_kernel(
    kv_in, h0, h1, h2, order_ref, residual_ref, first_ref, image_ref, second_ref, out_ref, spread_ref
):
    image = completed(kv_in, (h0, h1, h2))
    low = lane_iota(ROWS) < 64
    pick = jnp.where(
        lax.broadcasted_iota(jnp.int32, (64, 64), 1) == order_ref[...], 1.0, 0.0
    ).astype(jnp.bfloat16)
    fields = [lambda i, ref=ref: ref[i] for ref in (first_ref, second_ref, residual_ref, image_ref)]
    for f, field in enumerate(fields + [image]):
        for b in range(NODES // 2):
            even, odd = field(2 * b), field(2 * b + 1)
            lanes = pl.ds(b * LANES, LANES)
            spread_ref[:ROWS, lanes] = jnp.where(low, even, roll(odd, 64, 1))
            spread_ref[ROWS:, lanes] = jnp.where(low, roll(even, 64, 1), odd)
        value = spread_ref[...]
        high, middle = split(value)
        rest = (value - high.astype(jnp.float32) - middle.astype(jnp.float32)).astype(jnp.bfloat16)
        out_ref[f] = dot(pick, high) + (dot(pick, middle) + dot(pick, rest))


def last_kernel(sums_ref, spread_ref, solution_ref, residual_ref):
    sums = jnp.sum(sums_ref[...], axis=0, keepdims=True)
    lane = lane_iota(1)

    def total(d):
        return jnp.sum(jnp.where(lane == d, sums, 0.0), axis=1, keepdims=True)

    rz0, zw, ry, wy, zq, yq = (total(d) for d in range(6))
    alpha0 = rz0 / zw
    rz1 = rz0 - alpha0 * (zw + ry) + alpha0 * alpha0 * wy
    beta = rz1 / rz0
    share = 1.0 + beta
    energy = share * share * zw - 2.0 * share * alpha0 * zq + alpha0 * alpha0 * yq
    alpha1 = rz1 / energy
    first_scale = alpha0 + alpha1 * share
    second_scale = alpha1 * alpha0
    solution_ref[...] = first_scale * spread_ref[0] - second_scale * spread_ref[1]
    residual_ref[...] = (
        spread_ref[2] - first_scale * spread_ref[3] + second_scale * spread_ref[4]
    )


VMEM_LIMIT = 24 * 1024 * 1024
F32 = jnp.float32


def call(kernel, outs, scratch, *operands, space=pltpu.VMEM, cost=None):
    vmem = pl.BlockSpec(memory_space=pltpu.VMEM)
    return pl.pallas_call(
        kernel,
        out_shape=[jax.ShapeDtypeStruct(s, F32) for s in outs],
        in_specs=[pl.BlockSpec(memory_space=space)] * len(operands),
        out_specs=[vmem] * len(outs),
        scratch_shapes=[pltpu.VMEM(s, F32) if isinstance(s, tuple) else s for s in scratch],
        cost_estimate=cost,
        compiler_params=pltpu.CompilerParams(vmem_limit_bytes=VMEM_LIMIT),
    )(*operands)


FLUX = (2, NODES * ROWS, LANES)
COST = pl.CostEstimate(flops=10**11, transcendentals=0, bytes_accessed=10**8)
BIG_FLUX = (2, NODES * GROWS, LANES)


def faces(fields=1):
    return [(fields, ROWS, LANES), (fields, ROWS, LANES)]


def packs(fields=1):
    return [(fields, HALF, LANES)]


def swap_far(far):
    count = lax.axis_size(WIDE)
    return lax.ppermute(
        far, WIDE, [(w, (w + 1 if w % 2 else w - 1) % count) for w in range(count)]
    )


def swap_wide(far, near):
    count = lax.axis_size(WIDE)
    return swap_far(far), lax.ppermute(near, WIDE, [(w, w ^ 1) for w in range(count)])


def swap_all(far, near, pack, rows):
    far, near = swap_wide(far, near)
    (pack,) = call(pack_kernel, [(pack.shape[0], rows, LANES)], [], pack, far, near, cost=COST)
    return far, near, lax.all_gather(pack, "narrow")


def edges(fields):
    return (fields, NODES // 2, HALF, LANES)


def swap_edged(step, inverse, far, near, pack, edges_out):
    far, near = swap_wide(far, near)
    (pack,) = call(
        functools.partial(pack_edges_kernel, step),
        [(1, HALF * (1 + NODES), LANES)],
        [],
        pack, edges_out, inverse, far, near,
    )
    return far, near, lax.all_gather(pack, "narrow")


def swap_edges(lo, hi):
    count = lax.axis_size("narrow")
    left = lax.ppermute(hi, "narrow", [(n, (n + 1) % count) for n in range(count)])
    right = lax.ppermute(lo, "narrow", [(n, (n - 1) % count) for n in range(count)])
    return left, right


def local(load, geom, element_order):
    grad = jnp.asarray(GRAD_HL)
    diver = jnp.asarray(DIVER_HL)
    metric, load_kv, bound_kv, *face, lo, hi = call(
        place_kernel,
        [(7,) + FIELD, FIELD, FIELD] + faces(2) + packs(2) + [edges(6)] * 2,
        [
            FLUX, FIELD,
            pltpu.VMEM((1, 64), jnp.int32), pltpu.VMEM(load.shape, load.dtype),
            pltpu.VMEM(geom.shape, geom.dtype), pltpu.VMEM(ABS_HL.shape, jnp.bfloat16),
            pltpu.SemaphoreType.DMA((4,)),
        ],
        *(pltpu.with_memory_space_constraint(x, pltpu.HBM) for x in (element_order.reshape(1, 64), load, geom, jnp.asarray(ABS_HL))),
        space=pltpu.HBM,
    )
    sides = swap_edges(lo, hi)
    halo = swap_all(*face, GROWS)
    residual, inverse, update, ghost_inverse, ghost_metric, *parts, far, near = call(
        first_kernel,
        [FIELD, FIELD, FIELD, GHOST, (7,) + GHOST, BIG_FLUX, BIG] + faces(),
        [BIG],
        load_kv, bound_kv, *halo, *sides, metric, grad, diver,
    )
    (kv,) = call(rest_kernel, [FIELD], [], *parts, diver)
    halo = swap_wide(far, near)
    start, *parts, far, near = call(
        second_kernel,
        [FIELD, FLUX, FIELD] + faces(),
        [FIELD],
        kv, *halo, residual, inverse, update, metric, grad, diver,
    )
    kv, *side = call(
        functools.partial(rest_edges_kernel, STEP2),
        [FIELD] + packs() + [edges(2)],
        [],
        *parts, diver, start, inverse,
    )
    halo = swap_edged(STEP2, inverse, far, near, *side)
    first, *parts, far, near, early = call(
        third_kernel,
        [FIELD, BIG_FLUX, BIG] + faces() + [(1, LANES)],
        [BIG],
        kv, *halo, residual, inverse, start, ghost_inverse, ghost_metric, metric, grad, diver,
    )
    kv, early = call(rest_energy_kernel, [FIELD, (1, LANES)], [], *parts, diver, first, early)
    halo = swap_wide(far, near)
    image, update, start, *parts, far, near = call(
        fourth_kernel,
        [FIELD, FIELD, FIELD, FLUX, FIELD] + faces(),
        [],
        kv, *halo, inverse, metric, grad, diver,
    )
    kv, *side = call(
        functools.partial(rest_edges_kernel, STEP1),
        [FIELD] + packs() + [edges(2)],
        [],
        *parts, diver, start, inverse,
    )
    halo = swap_edged(STEP1, inverse, far, near, *side)
    start, *parts, far, near = call(
        fifth_kernel,
        [FIELD, BIG_FLUX, BIG] + faces(),
        [BIG],
        kv, *halo, image, inverse, update, ghost_inverse, ghost_metric, metric, grad, diver,
    )
    (kv,) = call(rest_kernel, [FIELD], [], *parts, diver)
    halo = swap_wide(far, near)
    second, kv, *face, sums = call(
        sixth_kernel,
        [FIELD, FIELD] + faces() + packs() + [(lax.axis_size(REST), LANES)],
        [FLUX, FIELD],
        kv, *halo, image, inverse, start, residual, first, early, metric, grad, diver,
    )
    far, near, pack = face
    far = swap_far(far)
    ring = lax.axis_size("ring")
    sums = lax.all_to_all(sums, REST, 0, 0)
    sums = jnp.broadcast_to(jnp.sum(sums, axis=0, keepdims=True), (ring, LANES))
    near, sums = lax.optimization_barrier((near, sums))
    sums = lax.all_to_all(sums, "ring", 0, 0)
    near = lax.all_gather(
        near, "ring", axis_index_groups=[[v, v + 1] for v in range(0, ring, 2)]
    )
    (pack,) = call(pack_kernel, [pack.shape], [], pack, far, near)
    halo = far, near, lax.all_gather(pack, "narrow")
    (spread,) = call(
        spread_kernel,
        [(5, 64, 512)],
        [(64, 512)],
        kv, *halo, element_order.reshape(64, 1), residual, first, image, second,
    )
    return tuple(call(last_kernel, [(64, 512), (64, 512)], [], sums, spread))


def solution(mesh):
    wide, narrow = mesh.devices.shape
    ring = 12 if wide % 12 == 0 else 2
    fine = jax.sharding.Mesh(
        mesh.devices.reshape(wide // ring, ring, narrow), ("outer", "ring", "narrow")
    )
    rows = ("outer", "ring", "narrow")
    return jax.shard_map(
        local,
        mesh=fine,
        in_specs=(P(rows, None), P(None, rows, None), P(WIDE, "narrow", None)),
        out_specs=(P(rows, None), P(rows, None)),
        check_vma=False,
    )
```

```python
import functools

import jax
import jax.numpy as jnp
import ml_dtypes
import numpy as np
from jax import lax
from jax.experimental import pallas as pl
from jax.experimental.pallas import tpu as pltpu
from jax.sharding import PartitionSpec as P

NODES = 8
ROWS = 32
LANES = 128
HALF = 16
GROWS = ROWS + HALF
INTERVAL_LOW = 0.03
INTERVAL_HIGH = 1.0
FIELD = (NODES, ROWS, LANES)
GHOST = (NODES, HALF, LANES)
BIG = (NODES, GROWS, LANES)
WIDE = ("outer", "ring")
REST = ("outer", "narrow")


def legendre_seven(point):
    before = 1.0
    current = point
    for degree in range(1, 7):
        after = ((2.0 * degree + 1.0) * point * current - degree * before) / (degree + 1.0)
        before = current
        current = after
    return current


def gll_derivative():
    points = 8
    inner_nodes = [
        -0.8717401485096066,
        -0.5917001814331423,
        -0.2092992179024789,
        0.2092992179024789,
        0.5917001814331423,
        0.8717401485096066,
    ]
    nodes = [-1.0] + inner_nodes + [1.0]
    values_at = [legendre_seven(node) for node in nodes]
    matrix = np.zeros((points, points))
    for source in range(points):
        for target in range(points):
            if source != target:
                matrix[source, target] = values_at[source] / (
                    values_at[target] * (nodes[source] - nodes[target])
                )
    matrix[0, 0] = -(points - 1) * points / 4.0
    matrix[points - 1, points - 1] = (points - 1) * points / 4.0
    return matrix


DERIV = gll_derivative().astype(np.float32)
ABS_DERIV = np.abs(DERIV)
ROW_TOTAL = ABS_DERIV.sum(axis=1)
EYE8 = np.eye(8, dtype=np.float32)


def cycle_matrix(small):
    return np.kron(np.eye(2, dtype=np.float32), np.kron(small, EYE8))


def radial_matrix(small):
    return np.kron(np.eye(16, dtype=np.float32), small)


def split_const(matrix):
    high = matrix.astype(ml_dtypes.bfloat16)
    low = (matrix - high.astype(np.float32)).astype(ml_dtypes.bfloat16)
    return high, low


GRAD = np.concatenate([cycle_matrix(DERIV.T), radial_matrix(DERIV.T)], axis=1)
DIVER = np.concatenate([cycle_matrix(DERIV), radial_matrix(DERIV)], axis=0)
GRAD_PARTS = split_const(GRAD)
GRAD_HL = np.concatenate([GRAD_PARTS[0], GRAD_PARTS[0], GRAD_PARTS[1]], axis=0)
DIVER_HL = np.concatenate(split_const(DIVER), axis=1)
ABS_HL = np.stack(split_const(np.abs(DIVER)))


def split(value):
    high = value.astype(jnp.bfloat16)
    return high, (value - high.astype(jnp.float32)).astype(jnp.bfloat16)


def dot(left, right):
    return lax.dot_general(
        left, right, (((1,), (0,)), ((), ())), preferred_element_type=jnp.float32
    )


def dot_split(value, matrix_ref):
    high, low = split(value)
    return dot(high, matrix_ref[0]) + (dot(low, matrix_ref[0]) + dot(high, matrix_ref[1]))


def dot_grad(value, grad_ref):
    high, low = split(value)
    both = jnp.concatenate([high, low], axis=1)
    return dot(both, grad_ref[: 2 * LANES]) + dot(high, grad_ref[2 * LANES :])


def dot_diver(value, diver_ref):
    high, low = split(value)
    both = dot(high, diver_ref[...])
    return both[:, :LANES] + (both[:, LANES:] + dot(low, diver_ref[:, :LANES]))


def lane_iota(rows):
    return lax.broadcasted_iota(jnp.int32, (rows, LANES), 1)


def row_iota(rows):
    return lax.broadcasted_iota(jnp.int32, (rows, LANES), 0)


def roll(value, shift, axis):
    size = value.shape[axis]
    return pltpu.roll(value, shift % size, axis)


def along_nodes(values, small):
    half = NODES // 2
    even = [values[i] + values[NODES - 1 - i] for i in range(half)]
    odd = [values[i] - values[NODES - 1 - i] for i in range(half)]
    out = [None] * NODES
    for m in range(half):
        from_even, from_odd = None, None
        for i in range(half):
            near, far = float(small[m][i]), float(small[m][NODES - 1 - i])
            one = even[i] * (0.5 * (near + far))
            two = odd[i] * (0.5 * (near - far))
            from_even = one if from_even is None else from_even + one
            from_odd = two if from_odd is None else from_odd + two
        out[m] = from_odd + from_even
        out[NODES - 1 - m] = from_odd - from_even
    return out


def along_nodes_plain(values, small):
    out = []
    for m in range(NODES):
        total = None
        for i in range(NODES):
            term = values[i] * float(small[m][i])
            total = term if total is None else total + term
        out.append(total)
    return out


def edge(value):
    return jnp.where(lane_iota(HALF) < 64, value[:HALF], value[HALF:])


def packed_edges(even, odd):
    low = lane_iota(HALF) < 64
    return jnp.where(low, even, roll(odd, 64, 1)), jnp.where(low, roll(even, 64, 1), odd)


def store_edges(lo_ref, hi_ref, lo_at, hi_at, values):
    for b in range(NODES // 2):
        lo_ref[lo_at, b], hi_ref[hi_at, b] = packed_edges(values[2 * b], values[2 * b + 1])


def ghost_columns(lefts, rights):
    low = lane_iota(HALF) < 64
    out = []
    for b in range(NODES // 2):
        left, right = lefts[b], rights[b]
        out.append(jnp.where(low, left, roll(right, 64, 1)))
        out.append(jnp.where(low, roll(left, 64, 1), right))
    return out


def gathered_ghost(packs_ref):
    left, right = beside(packs_ref)
    half = range(NODES // 2)
    return ghost_columns(
        [packs_ref[left, 0, HALF * (5 + b) : HALF * (6 + b)] for b in half],
        [packs_ref[right, 0, HALF * (1 + b) : HALF * (2 + b)] for b in half],
    )


def facing(left, right):
    return roll(jnp.where(lane_iota(HALF) < 64, right, left), 64, 1)


def own_assembly(u):
    count = u.shape[0]
    k = lane_iota(count) % 8
    er = row_iota(count) % HALF
    up = roll(roll(u, -1, 0), 7, 1)
    down = roll(roll(u, 1, 0), -7, 1)
    u = (
        u
        + jnp.where((k == 7) & (er < HALF - 1), up, 0.0)
        + jnp.where((k == 0) & (er > 0), down, 0.0)
    )
    top, bottom = u[:HALF], u[HALF:ROWS]
    lane = lane_iota(HALF)
    j = (lane // 8) % 8
    block = lane // 64
    new_top = (
        top
        + jnp.where(j == 7, roll(bottom, 56, 1), 0.0)
        + jnp.where((j == 0) & (block == 1), roll(bottom, 8, 1), 0.0)
    )
    new_bottom = (
        bottom
        + jnp.where(j == 0, roll(top, -56, 1), 0.0)
        + jnp.where((j == 7) & (block == 0), roll(top, -8, 1), 0.0)
    )
    if count == GROWS:
        ghost = u[ROWS:]
        new_top = new_top + jnp.where(lane < 8, roll(ghost, -56, 1), 0.0)
        new_bottom = new_bottom + jnp.where(lane >= 120, roll(ghost, 56, 1), 0.0)
    return jnp.concatenate([new_top, new_bottom], axis=0)


def ends(value):
    lane = lane_iota(HALF)
    return jnp.where(lane < 8, value[:HALF], jnp.where(lane >= 120, value[HALF:], 0.0))


def store_assembled(kv_ref, far_ref, near_ref, even, source, field=0, pack_ref=None):
    pack = None
    for i in range(NODES):
        value = own_assembly(source(i))
        kv_ref[i] = value
        if i == 0:
            first = value
        last = value
        if pack_ref is not None:
            piece = ends(value)
            if i:
                piece = roll(piece, 16 * i, 1)
            pack = piece if pack is None else pack + piece
    near_ref[field] = jnp.where(even, last, first)
    far_ref[field] = jnp.where(even, first, last)
    if pack_ref is not None:
        pack_ref[field] = pack


def is_even():
    return lax.broadcast_in_dim(lax.rem(lax.axis_index("ring"), 2), (ROWS, LANES), ()) == 0


def near_face(near_ref, field, even):
    if near_ref.ndim == 4:
        return jnp.where(even, near_ref[1, field], near_ref[0, field])
    return near_ref[field]


def pack_kernel(pack_in, far_ref, near_ref, pack_ref):
    even = is_even()
    for field in range(pack_ref.shape[0]):
        near, far = near_face(near_ref, field, even), far_ref[field]
        first = jnp.where(even, far, near)
        last = jnp.where(even, near, far)
        pack_ref[field, :HALF] = (
            pack_in[field] + ends(first) + roll(ends(last), 16 * (NODES - 1), 1)
        )
        if pack_ref.shape[1] > HALF:
            pack_ref[field, HALF:ROWS] = edge(first)
            pack_ref[field, ROWS:] = edge(last)


def pack_edges_kernel(step, pack_in, edges_in, inverse_ref, far_ref, near_ref, pack_ref):
    even = is_even()
    near, far = near_ref[0], far_ref[0]
    first = jnp.where(even, far, near)
    last = jnp.where(even, near, far)
    pack_ref[0, :HALF] = pack_in[0] + ends(first) + roll(ends(last), 16 * (NODES - 1), 1)
    zero = jnp.zeros((HALF, LANES), jnp.float32)
    for b in range(NODES // 2):
        lo, hi = edges_in[0, b], edges_in[1, b]
        if b == 0:
            add = packed_edges(edge(-step * inverse_ref[0] * first), zero)
            lo, hi = lo + add[0], hi + add[1]
        if b == NODES // 2 - 1:
            add = packed_edges(zero, edge(-step * inverse_ref[NODES - 1] * last))
            lo, hi = lo + add[0], hi + add[1]
        pack_ref[0, HALF * (1 + b) : HALF * (2 + b)] = lo
        pack_ref[0, HALF * (5 + b) : HALF * (6 + b)] = hi


WHOLE = (1, 3, 5)
LINES = (0, 2, 4, 6)


def line_pack(field):
    pack = None
    for i in range(NODES):
        piece = ends(field(i))
        if i:
            piece = roll(piece, 16 * i, 1)
        pack = piece if pack is None else pack + piece
    return pack


def ghost_lines(left, right):
    lane = lane_iota(HALF)
    both = jnp.where(lane % 16 >= 8, left, right)
    inner = (lane >= 56) & (lane < 72)
    return [jnp.where(inner, roll(both, 64 - 16 * i, 1), 0.0) for i in range(NODES)]


def beside(packs_ref):
    count = packs_ref.shape[0]
    here = lax.axis_index("narrow")
    return lax.rem(here + count - 1, count), lax.rem(here + 1, count)


def completed(kv, halo, field=0):
    far_ref, near_ref = halo[:2]
    even = is_even()
    near, far = near_face(near_ref, field, even), far_ref[field]
    lane = lane_iota(HALF)
    if len(halo) > 2:
        left, right = beside(halo[2])
        side = jnp.where(
            lane % 16 < 8,
            roll(halo[2][left, field, :HALF], 8, 1),
            roll(halo[2][right, field, :HALF], -8, 1),
        )

    def value(i):
        u = kv[i]
        if len(halo) > 2:
            piece = roll(side, -16 * i, 1) if i else side
            u = u + jnp.concatenate(
                [jnp.where(lane < 8, piece, 0.0), jnp.where(lane >= 120, piece, 0.0)], axis=0
            )
        if i == 0:
            u = u + jnp.where(even, far, near)
        if i == NODES - 1:
            u = u + jnp.where(even, near, far)
        return u

    return value


def ghost_sums(packs_ref, field=0, wide_too=False):
    left, right = beside(packs_ref)
    lane = lane_iota(HALF)
    own = packs_ref[lax.axis_index("narrow"), field, :HALF]
    lines = jnp.where(lane % 16 < 8, own, roll(own, 16, 1))
    inner = (lane >= 56) & (lane < 72)

    def value(i):
        u = jnp.where(inner, roll(lines, 56 - 16 * i, 1), 0.0)
        if wide_too and i in (0, NODES - 1):
            rows = slice(HALF, ROWS) if i == 0 else slice(ROWS, GROWS)
            u = u + facing(packs_ref[left, field, rows], packs_ref[right, field, rows])
        return u

    return value


def apply_flux(v_ref, metric_ref, ghost_ref, grad_ref, flux_ref, part_ref, with_energy=False):
    count = v_ref.shape[1]
    energy = jnp.zeros((8, LANES), jnp.float32)
    side = dot_grad(v_ref[...].reshape(NODES * count, LANES), grad_ref)
    flux_ref[0] = side[:, :LANES]
    flux_ref[1] = side[:, LANES:]
    for chunk in range(count // 8):
        rows = pl.ds(chunk * 8, 8)
        if chunk < ROWS // 8:
            geometry, there = metric_ref, rows
        else:
            geometry, there = ghost_ref, pl.ds(chunk * 8 - ROWS, 8)
        values = [v_ref[i, rows] for i in range(NODES)]
        grad_z = along_nodes(values, DERIV)
        flux_z = []
        for i in range(NODES):
            at = pl.ds(i * count + chunk * 8, 8)
            g_z, g_a, g_r = grad_z[i], flux_ref[0, at], flux_ref[1, at]
            m = [geometry[c, i, there] for c in range(6)]
            f_z = m[0] * g_z + m[3] * g_a + m[4] * g_r
            f_a = m[3] * g_z + m[1] * g_a + m[5] * g_r
            f_r = m[4] * g_z + m[5] * g_a + m[2] * g_r
            flux_z.append(f_z)
            flux_ref[0, at] = f_a
            flux_ref[1, at] = f_r
            if with_energy:
                energy = energy + (g_z * f_z + g_a * f_a + g_r * f_r)
        part_z = along_nodes(flux_z, DERIV.T)
        for i in range(NODES):
            screened = geometry[6, i, there] * values[i]
            part_ref[i, rows] = part_z[i] + screened
            if with_energy:
                energy = energy + screened * values[i]
    return energy


def whole_planes(flux_ref, part_ref, diver_ref, planes):
    count = part_ref.shape[1]

    def flux(f):
        if len(planes) == NODES:
            return flux_ref[f]
        return jnp.concatenate([flux_ref[f, i * count : (i + 1) * count] for i in planes], axis=0)

    total = dot_diver(jnp.concatenate([flux(0), flux(1)], axis=1), diver_ref)
    return [
        part_ref[i] + total[n * count : (n + 1) * count] for n, i in enumerate(planes)
    ]


def store_faces(flux_ref, part_ref, diver_ref, far_ref, near_ref):
    first, last = (
        own_assembly(u) for u in whole_planes(flux_ref, part_ref, diver_ref, (0, NODES - 1))
    )
    even = is_even()
    near_ref[0] = jnp.where(even, last, first)
    far_ref[0] = jnp.where(even, first, last)


def rest_kernel(flux_ref, part_ref, diver_ref, kv_ref):
    for i, u in enumerate(whole_planes(flux_ref, part_ref, diver_ref, range(NODES))):
        kv_ref[i] = own_assembly(u)


def rest_energy_kernel(flux_ref, part_ref, diver_ref, v_ref, sums_in, kv_ref, sums_ref):
    energy = jnp.zeros((ROWS, LANES), jnp.float32)
    for i, u in enumerate(whole_planes(flux_ref, part_ref, diver_ref, range(NODES))):
        kv_ref[i] = own_assembly(u)
        energy = energy + v_ref[i] * u[:ROWS]
    sums_ref[...] = sums_in[...] + sum_row([jnp.zeros((1, LANES), jnp.float32), energy])


def rest_edges_kernel(
    step, flux_ref, part_ref, diver_ref, start_ref, inverse_ref, kv_ref, pack_ref, edges_ref
):
    for i, u in enumerate(whole_planes(flux_ref, part_ref, diver_ref, range(NODES))):
        kv_ref[i] = own_assembly(u)
    pack_ref[0] = line_pack(lambda i: kv_ref[i])
    store_edges(
        edges_ref, edges_ref, 0, 1,
        [edge(start_ref[i] - step * inverse_ref[i] * kv_ref[i]) for i in range(NODES)],
    )


def weight_plane():
    lane, row = lane_iota(ROWS), row_iota(ROWS)
    j, k, er = (lane // 8) % 8, lane % 8, row % HALF
    w_a = jnp.where((j == 0) | (j == 7), 0.5, 1.0)
    shared = ((k == 0) & (er > 0)) | ((k == 7) & (er < HALF - 1))
    return w_a * jnp.where(shared, 0.5, 1.0)


def node_weight(i):
    return 0.5 if i in (0, NODES - 1) else 1.0


def sum_row(sums):
    lane = lane_iota(1)
    row = jnp.zeros((1, LANES), jnp.float32)
    for d, value in enumerate(sums):
        row = jnp.where(lane == d, jnp.sum(value), row)
    return row


SIGMA = ((INTERVAL_HIGH + INTERVAL_LOW) / 2.0) / ((INTERVAL_HIGH - INTERVAL_LOW) / 2.0)
CENTER = (INTERVAL_HIGH + INTERVAL_LOW) / 2.0
HALF_WIDTH = (INTERVAL_HIGH - INTERVAL_LOW) / 2.0
RHO0 = 1.0 / SIGMA
RHO1 = 1.0 / (2.0 * SIGMA - RHO0)
RHO2 = 1.0 / (2.0 * SIGMA - RHO1)


STEP1 = 2.0 * RHO1 / HALF_WIDTH
STEP2 = 2.0 * RHO2 / HALF_WIDTH


def place_kernel(
    order_hbm, load_hbm, geom_hbm, abs_hbm,
    metric_ref, load_kv, bound_kv, far_ref, near_ref, pack_ref, lo_ref, hi_ref,
    flux_ref, work_ref, order_ref, load_ref, geom_ref, abs_ref, sems,
):
    copies = [
        pltpu.make_async_copy(source, target, sems.at[c])
        for c, (source, target) in enumerate(
            [(order_hbm, order_ref), (load_hbm, load_ref), (geom_hbm, geom_ref), (abs_hbm, abs_ref)]
        )
    ]
    for copy in copies:
        copy.start()
    copies[0].wait()
    copies[1].wait()
    pick = jnp.where(
        lax.broadcasted_iota(jnp.int32, (64, 64), 0) == order_ref[...], 1.0, 0.0
    ).astype(jnp.bfloat16)
    low = lane_iota(ROWS) < 64

    def spread(placed, store):
        for b in range(4):
            piece = placed[:, b * LANES : (b + 1) * LANES]
            first, second = piece[:ROWS], piece[ROWS:]
            store(2 * b, jnp.where(low, first, roll(second, 64, 1)))
            store(2 * b + 1, jnp.where(low, roll(first, 64, 1), second))

    load = load_ref[...]
    high, rest = split(load)
    middle = (load - high.astype(jnp.float32) - rest.astype(jnp.float32)).astype(jnp.bfloat16)

    def store_load(i, value):
        work_ref[i] = value

    spread(dot(pick, high) + (dot(pick, rest) + dot(pick, middle)), store_load)
    even = is_even()
    store_assembled(
        load_kv, far_ref, near_ref, even, lambda i: work_ref[i], 0, pack_ref
    )
    store_edges(lo_ref, hi_ref, 3, 3, [edge(load_kv[i]) for i in range(NODES)])

    copies[2].wait()
    for c in range(7):

        def store_metric(i, value, c=c):
            metric_ref[c, i] = value

        spread(dot(pick, geom_ref[c]), store_metric)
    for slot, c in enumerate(WHOLE):
        store_edges(lo_ref, hi_ref, slot, slot, [edge(metric_ref[c, i]) for i in range(NODES)])
    for slot, c in enumerate(LINES):
        lines = line_pack(lambda i, c=c: metric_ref[c, i])
        lo_ref[5, slot] = lines
        hi_ref[5, slot] = lines

    lane = lane_iota(8)
    q_a = jnp.zeros((8, LANES), jnp.float32)
    q_r = jnp.zeros((8, LANES), jnp.float32)
    for m in range(NODES):
        q_a = jnp.where((lane // 8) % 8 == m, float(ROW_TOTAL[m]), q_a)
        q_r = jnp.where(lane % 8 == m, float(ROW_TOTAL[m]), q_r)
    for chunk in range(ROWS // 8):
        rows = pl.ds(chunk * 8, 8)
        h_z = []
        for i in range(NODES):
            at = pl.ds(i * ROWS + chunk * 8, 8)
            q_z = float(ROW_TOTAL[i])
            g = [jnp.abs(metric_ref[c, i, rows]) for c in range(6)]
            h_z.append(g[0] * q_z + g[3] * q_a + g[4] * q_r)
            flux_ref[0, at] = g[3] * q_z + g[1] * q_a + g[5] * q_r
            flux_ref[1, at] = g[4] * q_z + g[5] * q_a + g[2] * q_r
        part_z = along_nodes_plain(h_z, ABS_DERIV.T)
        for i in range(NODES):
            work_ref[i, rows] = part_z[i] + jnp.abs(metric_ref[6, i, rows])
    flux = jnp.concatenate([flux_ref[0], flux_ref[1]], axis=1)
    copies[3].wait()
    work_ref[...] += dot_split(flux, abs_ref).reshape(FIELD)
    store_assembled(
        bound_kv, far_ref, near_ref, even, lambda i: work_ref[i], 1, pack_ref
    )
    store_edges(lo_ref, hi_ref, 4, 4, [edge(bound_kv[i]) for i in range(NODES)])


def first_kernel(
    load_kv, bound_kv, h0, h1, h2, left_ref, right_ref, metric_ref, grad_ref, diver_ref,
    residual_ref, inverse_ref, update_ref, ghost_inverse, ghost_metric, flux_ref, part_ref, far_ref, near_ref,
    v_ref,
):
    residual = completed(load_kv, (h0, h1, h2), 0)
    bound = completed(bound_kv, (h0, h1, h2), 1)
    for i in range(NODES):
        r = residual(i)
        inverse = 1.0 / bound(i)
        update = r * inverse * (1.0 / CENTER)
        residual_ref[i] = r
        inverse_ref[i] = inverse
        update_ref[i] = update
        v_ref[i, :ROWS] = update
    residual, residual_sums = ghost_columns(left_ref[3], right_ref[3]), ghost_sums(h2, 0, True)
    bound, bound_sums = ghost_columns(left_ref[4], right_ref[4]), ghost_sums(h2, 1, True)
    for i in range(NODES):
        inverse = 1.0 / (bound[i] + bound_sums(i))
        ghost_inverse[i] = inverse
        v_ref[i, ROWS:] = (residual[i] + residual_sums(i)) * inverse * (1.0 / CENTER)
    for slot, c in enumerate(WHOLE):
        for i, value in enumerate(ghost_columns(left_ref[slot], right_ref[slot])):
            ghost_metric[c, i] = value
    for slot, c in enumerate(LINES):
        for i, value in enumerate(ghost_lines(left_ref[5, slot], right_ref[5, slot])):
            ghost_metric[c, i] = value
    apply_flux(v_ref, metric_ref, ghost_metric, grad_ref, flux_ref, part_ref)
    store_faces(flux_ref, part_ref, diver_ref, far_ref, near_ref)


def second_kernel(
    kv_in, h0, h1, source_ref, inverse_ref, update_in, metric_ref, grad_ref, diver_ref,
    start_ref, flux_ref, part_ref, far_ref, near_ref, v_ref,
):
    image = completed(kv_in, (h0, h1))
    for i in range(NODES):
        old = update_in[i]
        inverse = inverse_ref[i]
        source = source_ref[i]
        update = (RHO1 * RHO0) * old + STEP1 * inverse * (source - image(i))
        result = old + update
        v_ref[i] = result
        start_ref[i] = result + (RHO2 * RHO1) * update + STEP2 * inverse * source
    apply_flux(v_ref, metric_ref, None, grad_ref, flux_ref, part_ref)
    store_faces(flux_ref, part_ref, diver_ref, far_ref, near_ref)


def third_kernel(
    kv_in, h0, h1, h2, source_ref, inverse_ref, start_ref,
    ghost_inverse, ghost_metric, metric_ref, grad_ref, diver_ref,
    result_ref, flux_ref, part_ref, far_ref, near_ref, sums_ref, v_ref,
):
    image = completed(kv_in, (h0, h1, h2))
    plane = weight_plane()
    rz = jnp.zeros((ROWS, LANES), jnp.float32)
    for i in range(NODES):
        result = start_ref[i] - STEP2 * inverse_ref[i] * image(i)
        result_ref[i] = result
        v_ref[i, :ROWS] = result
        rz = rz + source_ref[i] * result * node_weight(i)
    start, sums = gathered_ghost(h2), ghost_sums(h2)
    for i in range(NODES):
        v_ref[i, ROWS:] = start[i] - STEP2 * ghost_inverse[i] * sums(i)
    apply_flux(v_ref, metric_ref, ghost_metric, grad_ref, flux_ref, part_ref)
    store_faces(flux_ref, part_ref, diver_ref, far_ref, near_ref)
    sums_ref[...] = sum_row([rz * plane])


def fourth_kernel(
    kv_in, h0, h1, inverse_ref, metric_ref, grad_ref, diver_ref,
    image_ref, update_ref, start_ref, flux_ref, part_ref, far_ref, near_ref,
):
    image = completed(kv_in, (h0, h1))
    for i in range(NODES):
        value = image(i)
        image_ref[i] = value
        update = value * inverse_ref[i] * (1.0 / CENTER)
        update_ref[i] = update
        start_ref[i] = (1.0 + RHO1 * RHO0 + STEP1 * CENTER) * update
    apply_flux(update_ref, metric_ref, None, grad_ref, flux_ref, part_ref)
    store_faces(flux_ref, part_ref, diver_ref, far_ref, near_ref)


def fifth_kernel(
    kv_in, h0, h1, h2, source_ref, inverse_ref, update_in,
    ghost_inverse, ghost_metric, metric_ref, grad_ref, diver_ref,
    start_ref, flux_ref, part_ref, far_ref, near_ref, v_ref,
):
    image = completed(kv_in, (h0, h1, h2))
    for i in range(NODES):
        old = update_in[i]
        inverse = inverse_ref[i]
        source = source_ref[i]
        update = (RHO1 * RHO0) * old + STEP1 * inverse * (source - image(i))
        result = old + update
        v_ref[i, :ROWS] = result
        start_ref[i] = result + (RHO2 * RHO1) * update + STEP2 * inverse * source
    start, sums = gathered_ghost(h2), ghost_sums(h2)
    for i in range(NODES):
        v_ref[i, ROWS:] = start[i] - STEP1 * ghost_inverse[i] * sums(i)
    apply_flux(v_ref, metric_ref, ghost_metric, grad_ref, flux_ref, part_ref)
    store_faces(flux_ref, part_ref, diver_ref, far_ref, near_ref)


def sixth_kernel(
    kv_in, h0, h1, source_ref, inverse_ref, start_ref, residual_ref, early_ref,
    metric_ref, grad_ref, diver_ref,
    result_ref, kv_ref, far_ref, near_ref, pack_ref, sums_hbm, flux_ref, work_ref, sums_ref, sem,
):
    image = completed(kv_in, (h0, h1))
    plane = weight_plane()
    r_y = jnp.zeros((ROWS, LANES), jnp.float32)
    w_y = jnp.zeros((ROWS, LANES), jnp.float32)
    for i in range(NODES):
        result = start_ref[i] - STEP2 * inverse_ref[i] * image(i)
        result_ref[i] = result
        r_y = r_y + residual_ref[i] * result * node_weight(i)
        w_y = w_y + source_ref[i] * result * node_weight(i)
    energy = apply_flux(
        result_ref, metric_ref, None, grad_ref, flux_ref, work_ref, with_energy=True
    )
    zero = jnp.zeros((1, LANES), jnp.float32)
    late = sum_row([zero, zero, r_y * plane, w_y * plane, energy])
    sums_ref[...] = jnp.broadcast_to(early_ref[...] + late, sums_ref.shape)
    leave = pltpu.make_async_copy(sums_ref, sums_hbm, sem)
    leave.start()
    planes = whole_planes(flux_ref, work_ref, diver_ref, range(NODES))
    store_assembled(kv_ref, far_ref, near_ref, is_even(), lambda i: planes[i], 0, pack_ref)
    leave.wait()


def spread_fields(order_ref, fields, out_ref, spread_ref):
    low = lane_iota(ROWS) < 64
    pick = jnp.where(
        lax.broadcasted_iota(jnp.int32, (64, 64), 1) == order_ref[...], 1.0, 0.0
    ).astype(jnp.bfloat16)
    for f, field in enumerate(fields):
        for b in range(NODES // 2):
            even, odd = field(2 * b), field(2 * b + 1)
            lanes = pl.ds(b * LANES, LANES)
            spread_ref[:ROWS, lanes] = jnp.where(low, even, roll(odd, 64, 1))
            spread_ref[ROWS:, lanes] = jnp.where(low, roll(even, 64, 1), odd)
        value = spread_ref[...]
        high, middle = split(value)
        rest = (value - high.astype(jnp.float32) - middle.astype(jnp.float32)).astype(jnp.bfloat16)
        out_ref[f] = dot(pick, high) + (dot(pick, middle) + dot(pick, rest))


def spread_early_kernel(
    order_ref, first_ref, second_ref, residual_ref, image_ref, out_ref, spread_ref
):
    refs = (first_ref, second_ref, residual_ref, image_ref)
    spread_fields(order_ref, [lambda i, ref=ref: ref[i] for ref in refs], out_ref, spread_ref)


def spread_late_kernel(kv_in, h0, h1, h2, order_ref, out_ref, spread_ref):
    spread_fields(order_ref, [completed(kv_in, (h0, h1, h2))], out_ref, spread_ref)


def last_kernel(sums_ref, spread_ref, late_ref, solution_ref, residual_ref):
    sums = jnp.sum(sums_ref[...], axis=0, keepdims=True)
    lane = lane_iota(1)

    def total(d):
        return jnp.sum(jnp.where(lane == d, sums, 0.0), axis=1, keepdims=True)

    rz0, zw, ry, wy, yq = (total(d) for d in range(5))
    alpha0 = rz0 / zw
    rz1 = rz0 - alpha0 * (zw + ry) + alpha0 * alpha0 * wy
    beta = rz1 / rz0
    share = 1.0 + beta
    energy = share * share * zw - 2.0 * share * alpha0 * wy + alpha0 * alpha0 * yq
    alpha1 = rz1 / energy
    first_scale = alpha0 + alpha1 * share
    second_scale = alpha1 * alpha0
    solution_ref[...] = first_scale * spread_ref[0] - second_scale * spread_ref[1]
    residual_ref[...] = (
        spread_ref[2] - first_scale * spread_ref[3] + second_scale * late_ref[0]
    )


VMEM_LIMIT = 24 * 1024 * 1024
F32 = jnp.float32


def call(kernel, outs, scratch, *operands, space=pltpu.VMEM, out_spaces=None, cost=None):
    out_spaces = out_spaces or [pltpu.VMEM] * len(outs)
    return pl.pallas_call(
        kernel,
        out_shape=[jax.ShapeDtypeStruct(s, F32) for s in outs],
        in_specs=[pl.BlockSpec(memory_space=space)] * len(operands),
        out_specs=[pl.BlockSpec(memory_space=s) for s in out_spaces],
        scratch_shapes=[pltpu.VMEM(s, F32) if isinstance(s, tuple) else s for s in scratch],
        cost_estimate=cost,
        compiler_params=pltpu.CompilerParams(vmem_limit_bytes=VMEM_LIMIT),
    )(*operands)


FLUX = (2, NODES * ROWS, LANES)
COST = pl.CostEstimate(flops=10**11, transcendentals=0, bytes_accessed=10**8)
BIG_FLUX = (2, NODES * GROWS, LANES)


def faces(fields=1):
    return [(fields, ROWS, LANES), (fields, ROWS, LANES)]


def packs(fields=1):
    return [(fields, HALF, LANES)]


def swap_far(far):
    count = lax.axis_size(WIDE)
    return lax.ppermute(
        far, WIDE, [(w, (w + 1 if w % 2 else w - 1) % count) for w in range(count)]
    )


def swap_wide(far, near):
    count = lax.axis_size(WIDE)
    return swap_far(far), lax.ppermute(near, WIDE, [(w, w ^ 1) for w in range(count)])


def swap_all(far, near, pack, rows):
    far, near = swap_wide(far, near)
    (pack,) = call(pack_kernel, [(pack.shape[0], rows, LANES)], [], pack, far, near, cost=COST)
    return far, near, lax.all_gather(pack, "narrow")


def edges(fields):
    return (fields, NODES // 2, HALF, LANES)


def swap_edged(step, inverse, far, near, pack, edges_out):
    far, near = swap_wide(far, near)
    (pack,) = call(
        functools.partial(pack_edges_kernel, step),
        [(1, HALF * (1 + NODES), LANES)],
        [],
        pack, edges_out, inverse, far, near,
    )
    return far, near, lax.all_gather(pack, "narrow")


def swap_edges(lo, hi):
    count = lax.axis_size("narrow")
    left = lax.ppermute(hi, "narrow", [(n, (n + 1) % count) for n in range(count)])
    right = lax.ppermute(lo, "narrow", [(n, (n - 1) % count) for n in range(count)])
    return left, right


def local(load, geom, element_order):
    grad = jnp.asarray(GRAD_HL)
    diver = jnp.asarray(DIVER_HL)
    metric, load_kv, bound_kv, *face, lo, hi = call(
        place_kernel,
        [(7,) + FIELD, FIELD, FIELD] + faces(2) + packs(2) + [edges(6)] * 2,
        [
            FLUX, FIELD,
            pltpu.VMEM((1, 64), jnp.int32), pltpu.VMEM(load.shape, load.dtype),
            pltpu.VMEM(geom.shape, geom.dtype), pltpu.VMEM(ABS_HL.shape, jnp.bfloat16),
            pltpu.SemaphoreType.DMA((4,)),
        ],
        *(pltpu.with_memory_space_constraint(x, pltpu.HBM) for x in (element_order.reshape(1, 64), load, geom, jnp.asarray(ABS_HL))),
        space=pltpu.HBM,
    )
    sides = swap_edges(lo, hi)
    halo = swap_all(*face, GROWS)
    residual, inverse, update, ghost_inverse, ghost_metric, *parts, far, near = call(
        first_kernel,
        [FIELD, FIELD, FIELD, GHOST, (7,) + GHOST, BIG_FLUX, BIG] + faces(),
        [BIG],
        load_kv, bound_kv, *halo, *sides, metric, grad, diver,
    )
    (kv,) = call(rest_kernel, [FIELD], [], *parts, diver)
    halo = swap_wide(far, near)
    start, *parts, far, near = call(
        second_kernel,
        [FIELD, FLUX, FIELD] + faces(),
        [FIELD],
        kv, *halo, residual, inverse, update, metric, grad, diver,
    )
    kv, *side = call(
        functools.partial(rest_edges_kernel, STEP2),
        [FIELD] + packs() + [edges(2)],
        [],
        *parts, diver, start, inverse,
    )
    halo = swap_edged(STEP2, inverse, far, near, *side)
    first, *parts, far, near, early = call(
        third_kernel,
        [FIELD, BIG_FLUX, BIG] + faces() + [(1, LANES)],
        [BIG],
        kv, *halo, residual, inverse, start, ghost_inverse, ghost_metric, metric, grad, diver,
    )
    kv, early = call(rest_energy_kernel, [FIELD, (1, LANES)], [], *parts, diver, first, early)
    halo = swap_wide(far, near)
    image, update, start, *parts, far, near = call(
        fourth_kernel,
        [FIELD, FIELD, FIELD, FLUX, FIELD] + faces(),
        [],
        kv, *halo, inverse, metric, grad, diver,
    )
    kv, *side = call(
        functools.partial(rest_edges_kernel, STEP1),
        [FIELD] + packs() + [edges(2)],
        [],
        *parts, diver, start, inverse,
    )
    halo = swap_edged(STEP1, inverse, far, near, *side)
    start, *parts, far, near = call(
        fifth_kernel,
        [FIELD, BIG_FLUX, BIG] + faces(),
        [BIG],
        kv, *halo, image, inverse, update, ghost_inverse, ghost_metric, metric, grad, diver,
    )
    (kv,) = call(rest_kernel, [FIELD], [], *parts, diver)
    halo = swap_wide(far, near)
    sums_shape = (lax.axis_size(REST), LANES)
    second, kv, *face, sums = call(
        sixth_kernel,
        [FIELD, FIELD] + faces() + packs() + [sums_shape],
        [FLUX, FIELD, sums_shape, pltpu.SemaphoreType.DMA(())],
        kv, *halo, image, inverse, start, residual, early, metric, grad, diver,
        out_spaces=[pltpu.VMEM] * 5 + [pltpu.HBM],
    )
    order = element_order.reshape(64, 1)
    (spread,) = call(
        spread_early_kernel, [(4, 64, 512)], [(64, 512)], order, first, second, residual, image
    )
    far, near, pack = face
    far = swap_far(far)
    ring = lax.axis_size("ring")
    sums = lax.all_to_all(sums, REST, 0, 0)
    sums = jnp.broadcast_to(jnp.sum(sums, axis=0, keepdims=True), (ring, LANES))
    near, sums = lax.optimization_barrier((near, sums))
    sums = lax.all_to_all(sums, "ring", 0, 0)
    near = lax.all_gather(
        near, "ring", axis_index_groups=[[v, v + 1] for v in range(0, ring, 2)]
    )
    (pack,) = call(pack_kernel, [pack.shape], [], pack, far, near)
    halo = far, near, lax.all_gather(pack, "narrow")
    (late,) = call(spread_late_kernel, [(1, 64, 512)], [(64, 512)], kv, *halo, order)
    return tuple(call(last_kernel, [(64, 512), (64, 512)], [], sums, spread, late))


def solution(mesh):
    wide, narrow = mesh.devices.shape
    ring = 12 if wide % 12 == 0 else 2
    fine = jax.sharding.Mesh(
        mesh.devices.reshape(wide // ring, ring, narrow), ("outer", "ring", "narrow")
    )
    rows = ("outer", "ring", "narrow")
    return jax.shard_map(
        local,
        mesh=fine,
        in_specs=(P(rows, None), P(None, rows, None), P(WIDE, "narrow", None)),
        out_specs=(P(rows, None), P(rows, None)),
        check_vma=False,
    )
```

```python
import functools

import jax
import jax.numpy as jnp
import ml_dtypes
import numpy as np
from jax import lax
from jax.experimental import pallas as pl
from jax.experimental.pallas import tpu as pltpu
from jax.sharding import PartitionSpec as P

NODES = 8
ROWS = 32
LANES = 128
HALF = 16
GROWS = ROWS + HALF
INTERVAL_LOW = 0.03
INTERVAL_HIGH = 1.0
FIELD = (NODES, ROWS, LANES)
GHOST = (NODES, HALF, LANES)
BIG = (NODES, GROWS, LANES)
WIDE = ("outer", "ring")
REST = ("outer", "narrow")


def legendre_seven(point):
    before = 1.0
    current = point
    for degree in range(1, 7):
        after = ((2.0 * degree + 1.0) * point * current - degree * before) / (degree + 1.0)
        before = current
        current = after
    return current


def gll_derivative():
    points = 8
    inner_nodes = [
        -0.8717401485096066,
        -0.5917001814331423,
        -0.2092992179024789,
        0.2092992179024789,
        0.5917001814331423,
        0.8717401485096066,
    ]
    nodes = [-1.0] + inner_nodes + [1.0]
    values_at = [legendre_seven(node) for node in nodes]
    matrix = np.zeros((points, points))
    for source in range(points):
        for target in range(points):
            if source != target:
                matrix[source, target] = values_at[source] / (
                    values_at[target] * (nodes[source] - nodes[target])
                )
    matrix[0, 0] = -(points - 1) * points / 4.0
    matrix[points - 1, points - 1] = (points - 1) * points / 4.0
    return matrix


DERIV = gll_derivative().astype(np.float32)
ABS_DERIV = np.abs(DERIV)
ROW_TOTAL = ABS_DERIV.sum(axis=1)
EYE8 = np.eye(8, dtype=np.float32)


def cycle_matrix(small):
    return np.kron(np.eye(2, dtype=np.float32), np.kron(small, EYE8))


def radial_matrix(small):
    return np.kron(np.eye(16, dtype=np.float32), small)


def split_const(matrix):
    high = matrix.astype(ml_dtypes.bfloat16)
    low = (matrix - high.astype(np.float32)).astype(ml_dtypes.bfloat16)
    return high, low


GRAD = np.concatenate([cycle_matrix(DERIV.T), radial_matrix(DERIV.T)], axis=1)
DIVER = np.concatenate([cycle_matrix(DERIV), radial_matrix(DERIV)], axis=0)
GRAD_PARTS = split_const(GRAD)
GRAD_HL = np.concatenate([GRAD_PARTS[0], GRAD_PARTS[0], GRAD_PARTS[1]], axis=0)
DIVER_HL = np.concatenate(split_const(DIVER), axis=1)
ABS_HL = np.stack(split_const(np.abs(DIVER)))


def split(value):
    high = value.astype(jnp.bfloat16)
    return high, (value - high.astype(jnp.float32)).astype(jnp.bfloat16)


def dot(left, right):
    return lax.dot_general(
        left, right, (((1,), (0,)), ((), ())), preferred_element_type=jnp.float32
    )


def dot_split(value, matrix_ref):
    high, low = split(value)
    return dot(high, matrix_ref[0]) + (dot(low, matrix_ref[0]) + dot(high, matrix_ref[1]))


def dot_grad(value, grad_ref):
    high, low = split(value)
    both = jnp.concatenate([high, low], axis=1)
    return dot(both, grad_ref[: 2 * LANES]) + dot(high, grad_ref[2 * LANES :])


def dot_diver(value, diver_ref):
    high, low = split(value)
    both = dot(high, diver_ref[...])
    return both[:, :LANES] + (both[:, LANES:] + dot(low, diver_ref[:, :LANES]))


def lane_iota(rows):
    return lax.broadcasted_iota(jnp.int32, (rows, LANES), 1)


def row_iota(rows):
    return lax.broadcasted_iota(jnp.int32, (rows, LANES), 0)


def roll(value, shift, axis):
    size = value.shape[axis]
    return pltpu.roll(value, shift % size, axis)


def along_nodes(values, small):
    half = NODES // 2
    even = [values[i] + values[NODES - 1 - i] for i in range(half)]
    odd = [values[i] - values[NODES - 1 - i] for i in range(half)]
    out = [None] * NODES
    for m in range(half):
        from_even, from_odd = None, None
        for i in range(half):
            near, far = float(small[m][i]), float(small[m][NODES - 1 - i])
            one = even[i] * (0.5 * (near + far))
            two = odd[i] * (0.5 * (near - far))
            from_even = one if from_even is None else from_even + one
            from_odd = two if from_odd is None else from_odd + two
        out[m] = from_odd + from_even
        out[NODES - 1 - m] = from_odd - from_even
    return out


def along_nodes_plain(values, small):
    out = []
    for m in range(NODES):
        total = None
        for i in range(NODES):
            term = values[i] * float(small[m][i])
            total = term if total is None else total + term
        out.append(total)
    return out


def edge(value):
    return jnp.where(lane_iota(HALF) < 64, value[:HALF], value[HALF:])


def packed_edges(even, odd):
    low = lane_iota(HALF) < 64
    return jnp.where(low, even, roll(odd, 64, 1)), jnp.where(low, roll(even, 64, 1), odd)


def store_edges(lo_ref, hi_ref, lo_at, hi_at, values):
    for b in range(NODES // 2):
        lo_ref[lo_at, b], hi_ref[hi_at, b] = packed_edges(values[2 * b], values[2 * b + 1])


def ghost_columns(lefts, rights):
    low = lane_iota(HALF) < 64
    out = []
    for b in range(NODES // 2):
        left, right = lefts[b], rights[b]
        out.append(jnp.where(low, left, roll(right, 64, 1)))
        out.append(jnp.where(low, roll(left, 64, 1), right))
    return out


def gathered_ghost(packs_ref):
    left, right = beside(packs_ref)
    half = range(NODES // 2)
    return ghost_columns(
        [packs_ref[left, 0, HALF * (5 + b) : HALF * (6 + b)] for b in half],
        [packs_ref[right, 0, HALF * (1 + b) : HALF * (2 + b)] for b in half],
    )


def facing(left, right):
    return roll(jnp.where(lane_iota(HALF) < 64, right, left), 64, 1)


def own_assembly(u):
    count = u.shape[0]
    k = lane_iota(count) % 8
    er = row_iota(count) % HALF
    up = roll(roll(u, -1, 0), 7, 1)
    down = roll(roll(u, 1, 0), -7, 1)
    u = (
        u
        + jnp.where((k == 7) & (er < HALF - 1), up, 0.0)
        + jnp.where((k == 0) & (er > 0), down, 0.0)
    )
    top, bottom = u[:HALF], u[HALF:ROWS]
    lane = lane_iota(HALF)
    j = (lane // 8) % 8
    block = lane // 64
    new_top = (
        top
        + jnp.where(j == 7, roll(bottom, 56, 1), 0.0)
        + jnp.where((j == 0) & (block == 1), roll(bottom, 8, 1), 0.0)
    )
    new_bottom = (
        bottom
        + jnp.where(j == 0, roll(top, -56, 1), 0.0)
        + jnp.where((j == 7) & (block == 0), roll(top, -8, 1), 0.0)
    )
    if count == GROWS:
        ghost = u[ROWS:]
        new_top = new_top + jnp.where(lane < 8, roll(ghost, -56, 1), 0.0)
        new_bottom = new_bottom + jnp.where(lane >= 120, roll(ghost, 56, 1), 0.0)
    return jnp.concatenate([new_top, new_bottom], axis=0)


def ends(value):
    lane = lane_iota(HALF)
    return jnp.where(lane < 8, value[:HALF], jnp.where(lane >= 120, value[HALF:], 0.0))


def store_assembled(kv_ref, far_ref, near_ref, even, source, field=0, pack_ref=None):
    pack = None
    for i in range(NODES):
        value = own_assembly(source(i))
        kv_ref[i] = value
        if i == 0:
            first = value
        last = value
        if pack_ref is not None:
            piece = ends(value)
            if i:
                piece = roll(piece, 16 * i, 1)
            pack = piece if pack is None else pack + piece
    near_ref[field] = jnp.where(even, last, first)
    far_ref[field] = jnp.where(even, first, last)
    if pack_ref is not None:
        pack_ref[field] = pack


def is_even():
    return lax.broadcast_in_dim(lax.rem(lax.axis_index("ring"), 2), (ROWS, LANES), ()) == 0


def near_face(near_ref, field, even):
    if near_ref.ndim == 4:
        return jnp.where(even, near_ref[1, field], near_ref[0, field])
    return near_ref[field]


def pack_kernel(pack_in, far_ref, near_ref, pack_ref):
    even = is_even()
    for field in range(pack_ref.shape[0]):
        near, far = near_face(near_ref, field, even), far_ref[field]
        first = jnp.where(even, far, near)
        last = jnp.where(even, near, far)
        pack_ref[field, :HALF] = (
            pack_in[field] + ends(first) + roll(ends(last), 16 * (NODES - 1), 1)
        )
        if pack_ref.shape[1] > HALF:
            pack_ref[field, HALF:ROWS] = edge(first)
            pack_ref[field, ROWS:] = edge(last)


def pack_edges_kernel(step, pack_in, edges_in, inverse_ref, far_ref, near_ref, pack_ref):
    even = is_even()
    near, far = near_ref[0], far_ref[0]
    first = jnp.where(even, far, near)
    last = jnp.where(even, near, far)
    pack_ref[0, :HALF] = pack_in[0] + ends(first) + roll(ends(last), 16 * (NODES - 1), 1)
    zero = jnp.zeros((HALF, LANES), jnp.float32)
    for b in range(NODES // 2):
        lo, hi = edges_in[0, b], edges_in[1, b]
        if b == 0:
            add = packed_edges(edge(-step * inverse_ref[0] * first), zero)
            lo, hi = lo + add[0], hi + add[1]
        if b == NODES // 2 - 1:
            add = packed_edges(zero, edge(-step * inverse_ref[NODES - 1] * last))
            lo, hi = lo + add[0], hi + add[1]
        pack_ref[0, HALF * (1 + b) : HALF * (2 + b)] = lo
        pack_ref[0, HALF * (5 + b) : HALF * (6 + b)] = hi


WHOLE = (1, 3, 5)
LINES = (0, 2, 4, 6)


def line_pack(field):
    pack = None
    for i in range(NODES):
        piece = ends(field(i))
        if i:
            piece = roll(piece, 16 * i, 1)
        pack = piece if pack is None else pack + piece
    return pack


def ghost_lines(left, right):
    lane = lane_iota(HALF)
    both = jnp.where(lane % 16 >= 8, left, right)
    inner = (lane >= 56) & (lane < 72)
    return [jnp.where(inner, roll(both, 64 - 16 * i, 1), 0.0) for i in range(NODES)]


def beside(packs_ref):
    count = packs_ref.shape[0]
    here = lax.axis_index("narrow")
    return lax.rem(here + count - 1, count), lax.rem(here + 1, count)


def completed(kv, halo, field=0):
    far_ref, near_ref = halo[:2]
    even = is_even()
    near, far = near_face(near_ref, field, even), far_ref[field]
    lane = lane_iota(HALF)
    if len(halo) > 2:
        left, right = beside(halo[2])
        side = jnp.where(
            lane % 16 < 8,
            roll(halo[2][left, field, :HALF], 8, 1),
            roll(halo[2][right, field, :HALF], -8, 1),
        )

    def value(i):
        u = kv[i]
        if len(halo) > 2:
            piece = roll(side, -16 * i, 1) if i else side
            u = u + jnp.concatenate(
                [jnp.where(lane < 8, piece, 0.0), jnp.where(lane >= 120, piece, 0.0)], axis=0
            )
        if i == 0:
            u = u + jnp.where(even, far, near)
        if i == NODES - 1:
            u = u + jnp.where(even, near, far)
        return u

    return value


def ghost_sums(packs_ref, field=0, wide_too=False):
    left, right = beside(packs_ref)
    lane = lane_iota(HALF)
    own = packs_ref[lax.axis_index("narrow"), field, :HALF]
    lines = jnp.where(lane % 16 < 8, own, roll(own, 16, 1))
    inner = (lane >= 56) & (lane < 72)

    def value(i):
        u = jnp.where(inner, roll(lines, 56 - 16 * i, 1), 0.0)
        if wide_too and i in (0, NODES - 1):
            rows = slice(HALF, ROWS) if i == 0 else slice(ROWS, GROWS)
            u = u + facing(packs_ref[left, field, rows], packs_ref[right, field, rows])
        return u

    return value


def apply_flux(v_ref, metric_ref, ghost_ref, grad_ref, flux_ref, part_ref, with_energy=False):
    count = v_ref.shape[1]
    energy = jnp.zeros((8, LANES), jnp.float32)
    side = dot_grad(v_ref[...].reshape(NODES * count, LANES), grad_ref)
    flux_ref[0] = side[:, :LANES]
    flux_ref[1] = side[:, LANES:]
    for chunk in range(count // 8):
        rows = pl.ds(chunk * 8, 8)
        if chunk < ROWS // 8:
            geometry, there = metric_ref, rows
        else:
            geometry, there = ghost_ref, pl.ds(chunk * 8 - ROWS, 8)
        values = [v_ref[i, rows] for i in range(NODES)]
        grad_z = along_nodes(values, DERIV)
        flux_z = []
        for i in range(NODES):
            at = pl.ds(i * count + chunk * 8, 8)
            g_z, g_a, g_r = grad_z[i], flux_ref[0, at], flux_ref[1, at]
            m = [geometry[c, i, there] for c in range(6)]
            f_z = m[0] * g_z + m[3] * g_a + m[4] * g_r
            f_a = m[3] * g_z + m[1] * g_a + m[5] * g_r
            f_r = m[4] * g_z + m[5] * g_a + m[2] * g_r
            flux_z.append(f_z)
            flux_ref[0, at] = f_a
            flux_ref[1, at] = f_r
            if with_energy:
                energy = energy + (g_z * f_z + g_a * f_a + g_r * f_r)
        part_z = along_nodes(flux_z, DERIV.T)
        for i in range(NODES):
            screened = geometry[6, i, there] * values[i]
            part_ref[i, rows] = part_z[i] + screened
            if with_energy:
                energy = energy + screened * values[i]
    return energy


def whole_planes(flux_ref, part_ref, diver_ref, planes):
    count = part_ref.shape[1]

    def flux(f):
        if len(planes) == NODES:
            return flux_ref[f]
        return jnp.concatenate([flux_ref[f, i * count : (i + 1) * count] for i in planes], axis=0)

    total = dot_diver(jnp.concatenate([flux(0), flux(1)], axis=1), diver_ref)
    return [
        part_ref[i] + total[n * count : (n + 1) * count] for n, i in enumerate(planes)
    ]


def store_faces(flux_ref, part_ref, diver_ref, far_ref, near_ref):
    first, last = (
        own_assembly(u) for u in whole_planes(flux_ref, part_ref, diver_ref, (0, NODES - 1))
    )
    even = is_even()
    near_ref[0] = jnp.where(even, last, first)
    far_ref[0] = jnp.where(even, first, last)


def rest_kernel(flux_ref, part_ref, diver_ref, kv_ref):
    for i, u in enumerate(whole_planes(flux_ref, part_ref, diver_ref, range(NODES))):
        kv_ref[i] = own_assembly(u)


def rest_energy_kernel(flux_ref, part_ref, diver_ref, v_ref, sums_in, kv_ref, sums_ref):
    energy = jnp.zeros((ROWS, LANES), jnp.float32)
    for i, u in enumerate(whole_planes(flux_ref, part_ref, diver_ref, range(NODES))):
        kv_ref[i] = own_assembly(u)
        energy = energy + v_ref[i] * u[:ROWS]
    sums_ref[...] = sums_in[...] + sum_row([jnp.zeros((1, LANES), jnp.float32), energy])


def rest_edges_kernel(
    step, flux_ref, part_ref, diver_ref, start_ref, inverse_ref, kv_ref, pack_ref, edges_ref
):
    for i, u in enumerate(whole_planes(flux_ref, part_ref, diver_ref, range(NODES))):
        kv_ref[i] = own_assembly(u)
    pack_ref[0] = line_pack(lambda i: kv_ref[i])
    store_edges(
        edges_ref, edges_ref, 0, 1,
        [edge(start_ref[i] - step * inverse_ref[i] * kv_ref[i]) for i in range(NODES)],
    )


def weight_plane():
    lane, row = lane_iota(ROWS), row_iota(ROWS)
    j, k, er = (lane // 8) % 8, lane % 8, row % HALF
    w_a = jnp.where((j == 0) | (j == 7), 0.5, 1.0)
    shared = ((k == 0) & (er > 0)) | ((k == 7) & (er < HALF - 1))
    return w_a * jnp.where(shared, 0.5, 1.0)


def node_weight(i):
    return 0.5 if i in (0, NODES - 1) else 1.0


def sum_row(sums):
    lane = lane_iota(1)
    row = jnp.zeros((1, LANES), jnp.float32)
    for d, value in enumerate(sums):
        row = jnp.where(lane == d, jnp.sum(value), row)
    return row


SIGMA = ((INTERVAL_HIGH + INTERVAL_LOW) / 2.0) / ((INTERVAL_HIGH - INTERVAL_LOW) / 2.0)
CENTER = (INTERVAL_HIGH + INTERVAL_LOW) / 2.0
HALF_WIDTH = (INTERVAL_HIGH - INTERVAL_LOW) / 2.0
RHO0 = 1.0 / SIGMA
RHO1 = 1.0 / (2.0 * SIGMA - RHO0)
RHO2 = 1.0 / (2.0 * SIGMA - RHO1)


STEP1 = 2.0 * RHO1 / HALF_WIDTH
STEP2 = 2.0 * RHO2 / HALF_WIDTH


def place_kernel(
    order_hbm, load_hbm, geom_hbm, abs_hbm,
    metric_ref, load_kv, bound_kv, far_ref, near_ref, pack_ref, lo_ref, hi_ref,
    flux_ref, work_ref, order_ref, load_ref, geom_ref, abs_ref, sems,
):
    copies = [
        pltpu.make_async_copy(source, target, sems.at[c])
        for c, (source, target) in enumerate(
            [(order_hbm, order_ref), (load_hbm, load_ref), (geom_hbm, geom_ref), (abs_hbm, abs_ref)]
        )
    ]
    for copy in copies:
        copy.start()
    copies[0].wait()
    copies[1].wait()
    pick = jnp.where(
        lax.broadcasted_iota(jnp.int32, (64, 64), 0) == order_ref[...], 1.0, 0.0
    ).astype(jnp.bfloat16)
    low = lane_iota(ROWS) < 64

    def spread(placed, store):
        for b in range(4):
            piece = placed[:, b * LANES : (b + 1) * LANES]
            first, second = piece[:ROWS], piece[ROWS:]
            store(2 * b, jnp.where(low, first, roll(second, 64, 1)))
            store(2 * b + 1, jnp.where(low, roll(first, 64, 1), second))

    load = load_ref[...]
    high, rest = split(load)
    middle = (load - high.astype(jnp.float32) - rest.astype(jnp.float32)).astype(jnp.bfloat16)

    def store_load(i, value):
        work_ref[i] = value

    spread(dot(pick, high) + (dot(pick, rest) + dot(pick, middle)), store_load)
    even = is_even()
    store_assembled(
        load_kv, far_ref, near_ref, even, lambda i: work_ref[i], 0, pack_ref
    )
    store_edges(lo_ref, hi_ref, 3, 3, [edge(load_kv[i]) for i in range(NODES)])

    copies[2].wait()
    for c in range(7):

        def store_metric(i, value, c=c):
            metric_ref[c, i] = value

        spread(dot(pick, geom_ref[c]), store_metric)
    for slot, c in enumerate(WHOLE):
        store_edges(lo_ref, hi_ref, slot, slot, [edge(metric_ref[c, i]) for i in range(NODES)])
    for slot, c in enumerate(LINES):
        lines = line_pack(lambda i, c=c: metric_ref[c, i])
        lo_ref[5, slot] = lines
        hi_ref[5, slot] = lines

    lane = lane_iota(8)
    q_a = jnp.zeros((8, LANES), jnp.float32)
    q_r = jnp.zeros((8, LANES), jnp.float32)
    for m in range(NODES):
        q_a = jnp.where((lane // 8) % 8 == m, float(ROW_TOTAL[m]), q_a)
        q_r = jnp.where(lane % 8 == m, float(ROW_TOTAL[m]), q_r)
    for chunk in range(ROWS // 8):
        rows = pl.ds(chunk * 8, 8)
        h_z = []
        for i in range(NODES):
            at = pl.ds(i * ROWS + chunk * 8, 8)
            q_z = float(ROW_TOTAL[i])
            g = [jnp.abs(metric_ref[c, i, rows]) for c in range(6)]
            h_z.append(g[0] * q_z + g[3] * q_a + g[4] * q_r)
            flux_ref[0, at] = g[3] * q_z + g[1] * q_a + g[5] * q_r
            flux_ref[1, at] = g[4] * q_z + g[5] * q_a + g[2] * q_r
        part_z = along_nodes_plain(h_z, ABS_DERIV.T)
        for i in range(NODES):
            work_ref[i, rows] = part_z[i] + jnp.abs(metric_ref[6, i, rows])
    flux = jnp.concatenate([flux_ref[0], flux_ref[1]], axis=1)
    copies[3].wait()
    work_ref[...] += dot_split(flux, abs_ref).reshape(FIELD)
    store_assembled(
        bound_kv, far_ref, near_ref, even, lambda i: work_ref[i], 1, pack_ref
    )
    store_edges(lo_ref, hi_ref, 4, 4, [edge(bound_kv[i]) for i in range(NODES)])


def first_kernel(
    load_kv, bound_kv, h0, h1, h2, left_ref, right_ref, metric_ref, grad_ref, diver_ref,
    residual_ref, inverse_ref, update_ref, ghost_inverse, ghost_metric, flux_ref, part_ref, far_ref, near_ref,
    v_ref,
):
    residual = completed(load_kv, (h0, h1, h2), 0)
    bound = completed(bound_kv, (h0, h1, h2), 1)
    for i in range(NODES):
        r = residual(i)
        inverse = 1.0 / bound(i)
        update = r * inverse * (1.0 / CENTER)
        residual_ref[i] = r
        inverse_ref[i] = inverse
        update_ref[i] = update
        v_ref[i, :ROWS] = update
    residual, residual_sums = ghost_columns(left_ref[3], right_ref[3]), ghost_sums(h2, 0, True)
    bound, bound_sums = ghost_columns(left_ref[4], right_ref[4]), ghost_sums(h2, 1, True)
    for i in range(NODES):
        inverse = 1.0 / (bound[i] + bound_sums(i))
        ghost_inverse[i] = inverse
        v_ref[i, ROWS:] = (residual[i] + residual_sums(i)) * inverse * (1.0 / CENTER)
    for slot, c in enumerate(WHOLE):
        for i, value in enumerate(ghost_columns(left_ref[slot], right_ref[slot])):
            ghost_metric[c, i] = value
    for slot, c in enumerate(LINES):
        for i, value in enumerate(ghost_lines(left_ref[5, slot], right_ref[5, slot])):
            ghost_metric[c, i] = value
    apply_flux(v_ref, metric_ref, ghost_metric, grad_ref, flux_ref, part_ref)
    store_faces(flux_ref, part_ref, diver_ref, far_ref, near_ref)


def second_kernel(
    kv_in, h0, h1, source_ref, inverse_ref, update_in, metric_ref, grad_ref, diver_ref,
    start_ref, flux_ref, part_ref, far_ref, near_ref, v_ref,
):
    image = completed(kv_in, (h0, h1))
    for i in range(NODES):
        old = update_in[i]
        inverse = inverse_ref[i]
        source = source_ref[i]
        update = (RHO1 * RHO0) * old + STEP1 * inverse * (source - image(i))
        result = old + update
        v_ref[i] = result
        start_ref[i] = result + (RHO2 * RHO1) * update + STEP2 * inverse * source
    apply_flux(v_ref, metric_ref, None, grad_ref, flux_ref, part_ref)
    store_faces(flux_ref, part_ref, diver_ref, far_ref, near_ref)


def third_kernel(
    kv_in, h0, h1, h2, source_ref, inverse_ref, start_ref,
    ghost_inverse, ghost_metric, metric_ref, grad_ref, diver_ref,
    result_ref, flux_ref, part_ref, far_ref, near_ref, sums_ref, v_ref,
):
    image = completed(kv_in, (h0, h1, h2))
    plane = weight_plane()
    rz = jnp.zeros((ROWS, LANES), jnp.float32)
    for i in range(NODES):
        result = start_ref[i] - STEP2 * inverse_ref[i] * image(i)
        result_ref[i] = result
        v_ref[i, :ROWS] = result
        rz = rz + source_ref[i] * result * node_weight(i)
    start, sums = gathered_ghost(h2), ghost_sums(h2)
    for i in range(NODES):
        v_ref[i, ROWS:] = start[i] - STEP2 * ghost_inverse[i] * sums(i)
    apply_flux(v_ref, metric_ref, ghost_metric, grad_ref, flux_ref, part_ref)
    store_faces(flux_ref, part_ref, diver_ref, far_ref, near_ref)
    sums_ref[...] = sum_row([rz * plane])


def fourth_kernel(
    kv_in, h0, h1, inverse_ref, metric_ref, grad_ref, diver_ref,
    image_ref, update_ref, start_ref, flux_ref, part_ref, far_ref, near_ref,
):
    image = completed(kv_in, (h0, h1))
    for i in range(NODES):
        value = image(i)
        image_ref[i] = value
        update = value * inverse_ref[i] * (1.0 / CENTER)
        update_ref[i] = update
        start_ref[i] = (1.0 + RHO1 * RHO0 + STEP1 * CENTER) * update
    apply_flux(update_ref, metric_ref, None, grad_ref, flux_ref, part_ref)
    store_faces(flux_ref, part_ref, diver_ref, far_ref, near_ref)


def fifth_kernel(
    kv_in, h0, h1, h2, source_ref, inverse_ref, update_in,
    ghost_inverse, ghost_metric, metric_ref, grad_ref, diver_ref,
    start_ref, flux_ref, part_ref, far_ref, near_ref, v_ref,
):
    image = completed(kv_in, (h0, h1, h2))
    for i in range(NODES):
        old = update_in[i]
        inverse = inverse_ref[i]
        source = source_ref[i]
        update = (RHO1 * RHO0) * old + STEP1 * inverse * (source - image(i))
        result = old + update
        v_ref[i, :ROWS] = result
        start_ref[i] = result + (RHO2 * RHO1) * update + STEP2 * inverse * source
    start, sums = gathered_ghost(h2), ghost_sums(h2)
    for i in range(NODES):
        v_ref[i, ROWS:] = start[i] - STEP1 * ghost_inverse[i] * sums(i)
    apply_flux(v_ref, metric_ref, ghost_metric, grad_ref, flux_ref, part_ref)
    store_faces(flux_ref, part_ref, diver_ref, far_ref, near_ref)


def sixth_kernel(
    kv_in, h0, h1, source_ref, inverse_ref, start_ref, residual_ref, early_ref,
    metric_ref, grad_ref,
    result_ref, flux_ref, part_ref, sums_hbm, sums_ref, sem,
):
    image = completed(kv_in, (h0, h1))
    plane = weight_plane()
    r_y = jnp.zeros((ROWS, LANES), jnp.float32)
    w_y = jnp.zeros((ROWS, LANES), jnp.float32)
    for i in range(NODES):
        result = start_ref[i] - STEP2 * inverse_ref[i] * image(i)
        result_ref[i] = result
        r_y = r_y + residual_ref[i] * result * node_weight(i)
        w_y = w_y + source_ref[i] * result * node_weight(i)
    energy = apply_flux(
        result_ref, metric_ref, None, grad_ref, flux_ref, part_ref, with_energy=True
    )
    zero = jnp.zeros((1, LANES), jnp.float32)
    late = sum_row([zero, zero, r_y * plane, w_y * plane, energy])
    sums_ref[...] = jnp.broadcast_to(early_ref[...] + late, sums_ref.shape)
    leave = pltpu.make_async_copy(sums_ref, sums_hbm, sem)
    leave.start()
    leave.wait()


def rest_faces_kernel(flux_ref, part_ref, diver_ref, kv_ref, far_ref, near_ref, pack_ref):
    planes = whole_planes(flux_ref, part_ref, diver_ref, range(NODES))
    store_assembled(kv_ref, far_ref, near_ref, is_even(), lambda i: planes[i], 0, pack_ref)


def spread_fields(order_ref, fields, out_ref, spread_ref):
    low = lane_iota(ROWS) < 64
    pick = jnp.where(
        lax.broadcasted_iota(jnp.int32, (64, 64), 1) == order_ref[...], 1.0, 0.0
    ).astype(jnp.bfloat16)
    for f, field in enumerate(fields):
        for b in range(NODES // 2):
            even, odd = field(2 * b), field(2 * b + 1)
            lanes = pl.ds(b * LANES, LANES)
            spread_ref[:ROWS, lanes] = jnp.where(low, even, roll(odd, 64, 1))
            spread_ref[ROWS:, lanes] = jnp.where(low, roll(even, 64, 1), odd)
        value = spread_ref[...]
        high, middle = split(value)
        rest = (value - high.astype(jnp.float32) - middle.astype(jnp.float32)).astype(jnp.bfloat16)
        out_ref[f] = dot(pick, high) + (dot(pick, middle) + dot(pick, rest))


def spread_early_kernel(
    order_ref, first_ref, second_ref, residual_ref, image_ref, out_ref, spread_ref
):
    refs = (first_ref, second_ref, residual_ref, image_ref)
    spread_fields(order_ref, [lambda i, ref=ref: ref[i] for ref in refs], out_ref, spread_ref)


def spread_late_kernel(kv_in, h0, h1, h2, order_ref, out_ref, spread_ref):
    spread_fields(order_ref, [completed(kv_in, (h0, h1, h2))], out_ref, spread_ref)


def last_kernel(sums_ref, spread_ref, late_ref, solution_ref, residual_ref):
    sums = jnp.sum(sums_ref[...], axis=0, keepdims=True)
    lane = lane_iota(1)

    def total(d):
        return jnp.sum(jnp.where(lane == d, sums, 0.0), axis=1, keepdims=True)

    rz0, zw, ry, wy, yq = (total(d) for d in range(5))
    alpha0 = rz0 / zw
    rz1 = rz0 - alpha0 * (zw + ry) + alpha0 * alpha0 * wy
    beta = rz1 / rz0
    share = 1.0 + beta
    energy = share * share * zw - 2.0 * share * alpha0 * wy + alpha0 * alpha0 * yq
    alpha1 = rz1 / energy
    first_scale = alpha0 + alpha1 * share
    second_scale = alpha1 * alpha0
    solution_ref[...] = first_scale * spread_ref[0] - second_scale * spread_ref[1]
    residual_ref[...] = (
        spread_ref[2] - first_scale * spread_ref[3] + second_scale * late_ref[0]
    )


VMEM_LIMIT = 24 * 1024 * 1024
F32 = jnp.float32


def call(kernel, outs, scratch, *operands, space=pltpu.VMEM, out_spaces=None, cost=None):
    out_spaces = out_spaces or [pltpu.VMEM] * len(outs)
    return pl.pallas_call(
        kernel,
        out_shape=[jax.ShapeDtypeStruct(s, F32) for s in outs],
        in_specs=[pl.BlockSpec(memory_space=space)] * len(operands),
        out_specs=[pl.BlockSpec(memory_space=s) for s in out_spaces],
        scratch_shapes=[pltpu.VMEM(s, F32) if isinstance(s, tuple) else s for s in scratch],
        cost_estimate=cost,
        compiler_params=pltpu.CompilerParams(vmem_limit_bytes=VMEM_LIMIT),
    )(*operands)


FLUX = (2, NODES * ROWS, LANES)
COST = pl.CostEstimate(flops=10**11, transcendentals=0, bytes_accessed=10**8)
BIG_FLUX = (2, NODES * GROWS, LANES)


def faces(fields=1):
    return [(fields, ROWS, LANES), (fields, ROWS, LANES)]


def packs(fields=1):
    return [(fields, HALF, LANES)]


def swap_far(far):
    count = lax.axis_size(WIDE)
    return lax.ppermute(
        far, WIDE, [(w, (w + 1 if w % 2 else w - 1) % count) for w in range(count)]
    )


def swap_wide(far, near):
    count = lax.axis_size(WIDE)
    return swap_far(far), lax.ppermute(near, WIDE, [(w, w ^ 1) for w in range(count)])


def swap_all(far, near, pack, rows):
    far, near = swap_wide(far, near)
    (pack,) = call(pack_kernel, [(pack.shape[0], rows, LANES)], [], pack, far, near, cost=COST)
    return far, near, lax.all_gather(pack, "narrow")


def edges(fields):
    return (fields, NODES // 2, HALF, LANES)


def swap_edged(step, inverse, far, near, pack, edges_out):
    far, near = swap_wide(far, near)
    (pack,) = call(
        functools.partial(pack_edges_kernel, step),
        [(1, HALF * (1 + NODES), LANES)],
        [],
        pack, edges_out, inverse, far, near,
    )
    return far, near, lax.all_gather(pack, "narrow")


def swap_edges(lo, hi):
    count = lax.axis_size("narrow")
    left = lax.ppermute(hi, "narrow", [(n, (n + 1) % count) for n in range(count)])
    right = lax.ppermute(lo, "narrow", [(n, (n - 1) % count) for n in range(count)])
    return left, right


def local(load, geom, element_order):
    grad = jnp.asarray(GRAD_HL)
    diver = jnp.asarray(DIVER_HL)
    metric, load_kv, bound_kv, *face, lo, hi = call(
        place_kernel,
        [(7,) + FIELD, FIELD, FIELD] + faces(2) + packs(2) + [edges(6)] * 2,
        [
            FLUX, FIELD,
            pltpu.VMEM((1, 64), jnp.int32), pltpu.VMEM(load.shape, load.dtype),
            pltpu.VMEM(geom.shape, geom.dtype), pltpu.VMEM(ABS_HL.shape, jnp.bfloat16),
            pltpu.SemaphoreType.DMA((4,)),
        ],
        *(pltpu.with_memory_space_constraint(x, pltpu.HBM) for x in (element_order.reshape(1, 64), load, geom, jnp.asarray(ABS_HL))),
        space=pltpu.HBM,
    )
    sides = swap_edges(lo, hi)
    halo = swap_all(*face, GROWS)
    residual, inverse, update, ghost_inverse, ghost_metric, *parts, far, near = call(
        first_kernel,
        [FIELD, FIELD, FIELD, GHOST, (7,) + GHOST, BIG_FLUX, BIG] + faces(),
        [BIG],
        load_kv, bound_kv, *halo, *sides, metric, grad, diver,
    )
    (kv,) = call(rest_kernel, [FIELD], [], *parts, diver)
    halo = swap_wide(far, near)
    start, *parts, far, near = call(
        second_kernel,
        [FIELD, FLUX, FIELD] + faces(),
        [FIELD],
        kv, *halo, residual, inverse, update, metric, grad, diver,
    )
    kv, *side = call(
        functools.partial(rest_edges_kernel, STEP2),
        [FIELD] + packs() + [edges(2)],
        [],
        *parts, diver, start, inverse,
    )
    halo = swap_edged(STEP2, inverse, far, near, *side)
    first, *parts, far, near, early = call(
        third_kernel,
        [FIELD, BIG_FLUX, BIG] + faces() + [(1, LANES)],
        [BIG],
        kv, *halo, residual, inverse, start, ghost_inverse, ghost_metric, metric, grad, diver,
    )
    kv, early = call(rest_energy_kernel, [FIELD, (1, LANES)], [], *parts, diver, first, early)
    halo = swap_wide(far, near)
    image, update, start, *parts, far, near = call(
        fourth_kernel,
        [FIELD, FIELD, FIELD, FLUX, FIELD] + faces(),
        [],
        kv, *halo, inverse, metric, grad, diver,
    )
    kv, *side = call(
        functools.partial(rest_edges_kernel, STEP1),
        [FIELD] + packs() + [edges(2)],
        [],
        *parts, diver, start, inverse,
    )
    halo = swap_edged(STEP1, inverse, far, near, *side)
    start, *parts, far, near = call(
        fifth_kernel,
        [FIELD, BIG_FLUX, BIG] + faces(),
        [BIG],
        kv, *halo, image, inverse, update, ghost_inverse, ghost_metric, metric, grad, diver,
    )
    (kv,) = call(rest_kernel, [FIELD], [], *parts, diver)
    halo = swap_wide(far, near)
    sums_shape = (lax.axis_size(REST), LANES)
    second, *parts, sums = call(
        sixth_kernel,
        [FIELD, FLUX, FIELD, sums_shape],
        [sums_shape, pltpu.SemaphoreType.DMA(())],
        kv, *halo, image, inverse, start, residual, early, metric, grad,
        out_spaces=[pltpu.VMEM] * 3 + [pltpu.HBM],
    )
    sums = lax.all_to_all(sums, REST, 0, 0)
    kv, far, near, pack = call(
        rest_faces_kernel, [FIELD] + faces() + packs(), [], *parts, diver
    )
    order = element_order.reshape(64, 1)
    (spread,) = call(
        spread_early_kernel, [(4, 64, 512)], [(64, 512)], order, first, second, residual, image
    )
    far = swap_far(far)
    ring = lax.axis_size("ring")
    sums = jnp.broadcast_to(jnp.sum(sums, axis=0, keepdims=True), (ring, LANES))
    near, sums = lax.optimization_barrier((near, sums))
    sums = lax.all_to_all(sums, "ring", 0, 0)
    near = lax.all_gather(
        near, "ring", axis_index_groups=[[v, v + 1] for v in range(0, ring, 2)]
    )
    (pack,) = call(pack_kernel, [pack.shape], [], pack, far, near)
    halo = far, near, lax.all_gather(pack, "narrow")
    (late,) = call(spread_late_kernel, [(1, 64, 512)], [(64, 512)], kv, *halo, order)
    return tuple(call(last_kernel, [(64, 512), (64, 512)], [], sums, spread, late))


def solution(mesh):
    wide, narrow = mesh.devices.shape
    ring = 12 if wide % 12 == 0 else 2
    fine = jax.sharding.Mesh(
        mesh.devices.reshape(wide // ring, ring, narrow), ("outer", "ring", "narrow")
    )
    rows = ("outer", "ring", "narrow")
    return jax.shard_map(
        local,
        mesh=fine,
        in_specs=(P(rows, None), P(None, rows, None), P(WIDE, "narrow", None)),
        out_specs=(P(rows, None), P(rows, None)),
        check_vma=False,
    )
```

```python
import functools

import jax
import jax.numpy as jnp
import ml_dtypes
import numpy as np
from jax import lax
from jax.experimental import pallas as pl
from jax.experimental.pallas import tpu as pltpu
from jax.sharding import PartitionSpec as P

NODES = 8
ROWS = 32
LANES = 128
HALF = 16
GROWS = ROWS + HALF
INTERVAL_LOW = 0.03
INTERVAL_HIGH = 1.0
FIELD = (NODES, ROWS, LANES)
GHOST = (NODES, HALF, LANES)
BIG = (NODES, GROWS, LANES)
WIDE = ("outer", "ring")
REST = ("outer", "narrow")


def legendre_seven(point):
    before = 1.0
    current = point
    for degree in range(1, 7):
        after = ((2.0 * degree + 1.0) * point * current - degree * before) / (degree + 1.0)
        before = current
        current = after
    return current


def gll_derivative():
    points = 8
    inner_nodes = [
        -0.8717401485096066,
        -0.5917001814331423,
        -0.2092992179024789,
        0.2092992179024789,
        0.5917001814331423,
        0.8717401485096066,
    ]
    nodes = [-1.0] + inner_nodes + [1.0]
    values_at = [legendre_seven(node) for node in nodes]
    matrix = np.zeros((points, points))
    for source in range(points):
        for target in range(points):
            if source != target:
                matrix[source, target] = values_at[source] / (
                    values_at[target] * (nodes[source] - nodes[target])
                )
    matrix[0, 0] = -(points - 1) * points / 4.0
    matrix[points - 1, points - 1] = (points - 1) * points / 4.0
    return matrix


DERIV = gll_derivative().astype(np.float32)
ABS_DERIV = np.abs(DERIV)
ROW_TOTAL = ABS_DERIV.sum(axis=1)
EYE8 = np.eye(8, dtype=np.float32)


def cycle_matrix(small):
    return np.kron(np.eye(2, dtype=np.float32), np.kron(small, EYE8))


def radial_matrix(small):
    return np.kron(np.eye(16, dtype=np.float32), small)


def split_const(matrix):
    high = matrix.astype(ml_dtypes.bfloat16)
    low = (matrix - high.astype(np.float32)).astype(ml_dtypes.bfloat16)
    return high, low


GRAD = np.concatenate([cycle_matrix(DERIV.T), radial_matrix(DERIV.T)], axis=1)
DIVER = np.concatenate([cycle_matrix(DERIV), radial_matrix(DERIV)], axis=0)
GRAD_PARTS = split_const(GRAD)
GRAD_HL = np.concatenate([GRAD_PARTS[0], GRAD_PARTS[0], GRAD_PARTS[1]], axis=0)
DIVER_HL = np.concatenate(split_const(DIVER), axis=1)
ABS_HL = np.stack(split_const(np.abs(DIVER)))


def split(value):
    high = value.astype(jnp.bfloat16)
    return high, (value - high.astype(jnp.float32)).astype(jnp.bfloat16)


def dot(left, right):
    return lax.dot_general(
        left, right, (((1,), (0,)), ((), ())), preferred_element_type=jnp.float32
    )


def dot_split(value, matrix_ref):
    high, low = split(value)
    return dot(high, matrix_ref[0]) + (dot(low, matrix_ref[0]) + dot(high, matrix_ref[1]))


def dot_grad(value, grad_ref):
    high, low = split(value)
    both = jnp.concatenate([high, low], axis=1)
    return dot(both, grad_ref[: 2 * LANES]) + dot(high, grad_ref[2 * LANES :])


def dot_diver(value, diver_ref):
    high, low = split(value)
    both = dot(high, diver_ref[...])
    return both[:, :LANES] + (both[:, LANES:] + dot(low, diver_ref[:, :LANES]))


def lane_iota(rows):
    return lax.broadcasted_iota(jnp.int32, (rows, LANES), 1)


def row_iota(rows):
    return lax.broadcasted_iota(jnp.int32, (rows, LANES), 0)


def roll(value, shift, axis):
    size = value.shape[axis]
    return pltpu.roll(value, shift % size, axis)


def along_nodes(values, small):
    half = NODES // 2
    even = [values[i] + values[NODES - 1 - i] for i in range(half)]
    odd = [values[i] - values[NODES - 1 - i] for i in range(half)]
    out = [None] * NODES
    for m in range(half):
        from_even, from_odd = None, None
        for i in range(half):
            near, far = float(small[m][i]), float(small[m][NODES - 1 - i])
            one = even[i] * (0.5 * (near + far))
            two = odd[i] * (0.5 * (near - far))
            from_even = one if from_even is None else from_even + one
            from_odd = two if from_odd is None else from_odd + two
        out[m] = from_odd + from_even
        out[NODES - 1 - m] = from_odd - from_even
    return out


def along_nodes_plain(values, small):
    out = []
    for m in range(NODES):
        total = None
        for i in range(NODES):
            term = values[i] * float(small[m][i])
            total = term if total is None else total + term
        out.append(total)
    return out


def edge(value):
    return jnp.where(lane_iota(HALF) < 64, value[:HALF], value[HALF:])


def packed_edges(even, odd):
    low = lane_iota(HALF) < 64
    return jnp.where(low, even, roll(odd, 64, 1)), jnp.where(low, roll(even, 64, 1), odd)


def store_edges(lo_ref, hi_ref, lo_at, hi_at, values):
    for b in range(NODES // 2):
        lo_ref[lo_at, b], hi_ref[hi_at, b] = packed_edges(values[2 * b], values[2 * b + 1])


def ghost_columns(lefts, rights):
    low = lane_iota(HALF) < 64
    out = []
    for b in range(NODES // 2):
        left, right = lefts[b], rights[b]
        out.append(jnp.where(low, left, roll(right, 64, 1)))
        out.append(jnp.where(low, roll(left, 64, 1), right))
    return out


def gathered_ghost(packs_ref):
    left, right = beside(packs_ref)
    half = range(NODES // 2)
    return ghost_columns(
        [packs_ref[left, 0, HALF * (5 + b) : HALF * (6 + b)] for b in half],
        [packs_ref[right, 0, HALF * (1 + b) : HALF * (2 + b)] for b in half],
    )


def facing(left, right):
    return roll(jnp.where(lane_iota(HALF) < 64, right, left), 64, 1)


def own_assembly(u):
    count = u.shape[0]
    k = lane_iota(count) % 8
    er = row_iota(count) % HALF
    up = roll(roll(u, -1, 0), 7, 1)
    down = roll(roll(u, 1, 0), -7, 1)
    u = (
        u
        + jnp.where((k == 7) & (er < HALF - 1), up, 0.0)
        + jnp.where((k == 0) & (er > 0), down, 0.0)
    )
    top, bottom = u[:HALF], u[HALF:ROWS]
    lane = lane_iota(HALF)
    j = (lane // 8) % 8
    block = lane // 64
    new_top = (
        top
        + jnp.where(j == 7, roll(bottom, 56, 1), 0.0)
        + jnp.where((j == 0) & (block == 1), roll(bottom, 8, 1), 0.0)
    )
    new_bottom = (
        bottom
        + jnp.where(j == 0, roll(top, -56, 1), 0.0)
        + jnp.where((j == 7) & (block == 0), roll(top, -8, 1), 0.0)
    )
    if count == GROWS:
        ghost = u[ROWS:]
        new_top = new_top + jnp.where(lane < 8, roll(ghost, -56, 1), 0.0)
        new_bottom = new_bottom + jnp.where(lane >= 120, roll(ghost, 56, 1), 0.0)
    return jnp.concatenate([new_top, new_bottom], axis=0)


def ends(value):
    lane = lane_iota(HALF)
    return jnp.where(lane < 8, value[:HALF], jnp.where(lane >= 120, value[HALF:], 0.0))


def store_assembled(kv_ref, far_ref, near_ref, even, source, field=0, pack_ref=None):
    pack = None
    for i in range(NODES):
        value = own_assembly(source(i))
        kv_ref[i] = value
        if i == 0:
            first = value
        last = value
        if pack_ref is not None:
            piece = ends(value)
            if i:
                piece = roll(piece, 16 * i, 1)
            pack = piece if pack is None else pack + piece
    near_ref[field] = jnp.where(even, last, first)
    far_ref[field] = jnp.where(even, first, last)
    if pack_ref is not None:
        pack_ref[field] = pack


def is_even():
    return lax.broadcast_in_dim(lax.rem(lax.axis_index("ring"), 2), (ROWS, LANES), ()) == 0


def near_face(near_ref, field, even):
    if near_ref.ndim == 4:
        return jnp.where(even, near_ref[1, field], near_ref[0, field])
    return near_ref[field]


def pack_kernel(pack_in, far_ref, near_ref, pack_ref):
    even = is_even()
    for field in range(pack_ref.shape[0]):
        near, far = near_face(near_ref, field, even), far_ref[field]
        first = jnp.where(even, far, near)
        last = jnp.where(even, near, far)
        pack_ref[field, :HALF] = (
            pack_in[field] + ends(first) + roll(ends(last), 16 * (NODES - 1), 1)
        )
        if pack_ref.shape[1] > HALF:
            pack_ref[field, HALF:ROWS] = edge(first)
            pack_ref[field, ROWS:] = edge(last)


def pack_edges_kernel(step, pack_in, edges_in, inverse_ref, far_ref, near_ref, pack_ref):
    even = is_even()
    near, far = near_ref[0], far_ref[0]
    first = jnp.where(even, far, near)
    last = jnp.where(even, near, far)
    pack_ref[0, :HALF] = pack_in[0] + ends(first) + roll(ends(last), 16 * (NODES - 1), 1)
    zero = jnp.zeros((HALF, LANES), jnp.float32)
    for b in range(NODES // 2):
        lo, hi = edges_in[0, b], edges_in[1, b]
        if b == 0:
            add = packed_edges(edge(-step * inverse_ref[0] * first), zero)
            lo, hi = lo + add[0], hi + add[1]
        if b == NODES // 2 - 1:
            add = packed_edges(zero, edge(-step * inverse_ref[NODES - 1] * last))
            lo, hi = lo + add[0], hi + add[1]
        pack_ref[0, HALF * (1 + b) : HALF * (2 + b)] = lo
        pack_ref[0, HALF * (5 + b) : HALF * (6 + b)] = hi


WHOLE = (1, 3, 5)
LINES = (0, 2, 4, 6)


def line_pack(field):
    pack = None
    for i in range(NODES):
        piece = ends(field(i))
        if i:
            piece = roll(piece, 16 * i, 1)
        pack = piece if pack is None else pack + piece
    return pack


def ghost_lines(left, right):
    lane = lane_iota(HALF)
    both = jnp.where(lane % 16 >= 8, left, right)
    inner = (lane >= 56) & (lane < 72)
    return [jnp.where(inner, roll(both, 64 - 16 * i, 1), 0.0) for i in range(NODES)]


def beside(packs_ref):
    count = packs_ref.shape[0]
    here = lax.axis_index("narrow")
    return lax.rem(here + count - 1, count), lax.rem(here + 1, count)


def completed(kv, halo, field=0):
    far_ref, near_ref = halo[:2]
    even = is_even()
    near, far = near_face(near_ref, field, even), far_ref[field]
    lane = lane_iota(HALF)
    if len(halo) > 2:
        left, right = beside(halo[2])
        side = jnp.where(
            lane % 16 < 8,
            roll(halo[2][left, field, :HALF], 8, 1),
            roll(halo[2][right, field, :HALF], -8, 1),
        )

    def value(i):
        u = kv[i]
        if len(halo) > 2:
            piece = roll(side, -16 * i, 1) if i else side
            u = u + jnp.concatenate(
                [jnp.where(lane < 8, piece, 0.0), jnp.where(lane >= 120, piece, 0.0)], axis=0
            )
        if i == 0:
            u = u + jnp.where(even, far, near)
        if i == NODES - 1:
            u = u + jnp.where(even, near, far)
        return u

    return value


def ghost_sums(packs_ref, field=0, wide_too=False):
    left, right = beside(packs_ref)
    lane = lane_iota(HALF)
    own = packs_ref[lax.axis_index("narrow"), field, :HALF]
    lines = jnp.where(lane % 16 < 8, own, roll(own, 16, 1))
    inner = (lane >= 56) & (lane < 72)

    def value(i):
        u = jnp.where(inner, roll(lines, 56 - 16 * i, 1), 0.0)
        if wide_too and i in (0, NODES - 1):
            rows = slice(HALF, ROWS) if i == 0 else slice(ROWS, GROWS)
            u = u + facing(packs_ref[left, field, rows], packs_ref[right, field, rows])
        return u

    return value


def apply_flux(v_ref, metric_ref, ghost_ref, grad_ref, flux_ref, part_ref, with_energy=False):
    count = v_ref.shape[1]
    energy = jnp.zeros((8, LANES), jnp.float32)
    side = dot_grad(v_ref[...].reshape(NODES * count, LANES), grad_ref)
    flux_ref[0] = side[:, :LANES]
    flux_ref[1] = side[:, LANES:]
    for chunk in range(count // 8):
        rows = pl.ds(chunk * 8, 8)
        if chunk < ROWS // 8:
            geometry, there = metric_ref, rows
        else:
            geometry, there = ghost_ref, pl.ds(chunk * 8 - ROWS, 8)
        values = [v_ref[i, rows] for i in range(NODES)]
        grad_z = along_nodes(values, DERIV)
        flux_z = []
        for i in range(NODES):
            at = pl.ds(i * count + chunk * 8, 8)
            g_z, g_a, g_r = grad_z[i], flux_ref[0, at], flux_ref[1, at]
            m = [geometry[c, i, there] for c in range(6)]
            f_z = m[0] * g_z + m[3] * g_a + m[4] * g_r
            f_a = m[3] * g_z + m[1] * g_a + m[5] * g_r
            f_r = m[4] * g_z + m[5] * g_a + m[2] * g_r
            flux_z.append(f_z)
            flux_ref[0, at] = f_a
            flux_ref[1, at] = f_r
            if with_energy:
                energy = energy + (g_z * f_z + g_a * f_a + g_r * f_r)
        part_z = along_nodes(flux_z, DERIV.T)
        for i in range(NODES):
            screened = geometry[6, i, there] * values[i]
            part_ref[i, rows] = part_z[i] + screened
            if with_energy:
                energy = energy + screened * values[i]
    return energy


def whole_planes(flux_ref, part_ref, diver_ref, planes):
    count = part_ref.shape[1]

    def flux(f):
        if len(planes) == NODES:
            return flux_ref[f]
        return jnp.concatenate([flux_ref[f, i * count : (i + 1) * count] for i in planes], axis=0)

    total = dot_diver(jnp.concatenate([flux(0), flux(1)], axis=1), diver_ref)
    return [
        part_ref[i] + total[n * count : (n + 1) * count] for n, i in enumerate(planes)
    ]


def store_faces(flux_ref, part_ref, diver_ref, far_ref, near_ref):
    first, last = (
        own_assembly(u) for u in whole_planes(flux_ref, part_ref, diver_ref, (0, NODES - 1))
    )
    even = is_even()
    near_ref[0] = jnp.where(even, last, first)
    far_ref[0] = jnp.where(even, first, last)


def rest_kernel(flux_ref, part_ref, diver_ref, kv_ref):
    for i, u in enumerate(whole_planes(flux_ref, part_ref, diver_ref, range(NODES))):
        kv_ref[i] = own_assembly(u)


def rest_energy_kernel(flux_ref, part_ref, diver_ref, v_ref, sums_in, kv_ref, sums_ref):
    energy = jnp.zeros((ROWS, LANES), jnp.float32)
    for i, u in enumerate(whole_planes(flux_ref, part_ref, diver_ref, range(NODES))):
        kv_ref[i] = own_assembly(u)
        energy = energy + v_ref[i] * u[:ROWS]
    sums_ref[...] = sums_in[...] + sum_row([jnp.zeros((1, LANES), jnp.float32), energy])


def rest_edges_kernel(
    step, flux_ref, part_ref, diver_ref, start_ref, inverse_ref, kv_ref, pack_ref, edges_ref
):
    for i, u in enumerate(whole_planes(flux_ref, part_ref, diver_ref, range(NODES))):
        kv_ref[i] = own_assembly(u)
    pack_ref[0] = line_pack(lambda i: kv_ref[i])
    store_edges(
        edges_ref, edges_ref, 0, 1,
        [edge(start_ref[i] - step * inverse_ref[i] * kv_ref[i]) for i in range(NODES)],
    )


def weight_plane():
    lane, row = lane_iota(ROWS), row_iota(ROWS)
    j, k, er = (lane // 8) % 8, lane % 8, row % HALF
    w_a = jnp.where((j == 0) | (j == 7), 0.5, 1.0)
    shared = ((k == 0) & (er > 0)) | ((k == 7) & (er < HALF - 1))
    return w_a * jnp.where(shared, 0.5, 1.0)


def node_weight(i):
    return 0.5 if i in (0, NODES - 1) else 1.0


def sum_row(sums):
    lane = lane_iota(1)
    row = jnp.zeros((1, LANES), jnp.float32)
    for d, value in enumerate(sums):
        row = jnp.where(lane == d, jnp.sum(value), row)
    return row


SIGMA = ((INTERVAL_HIGH + INTERVAL_LOW) / 2.0) / ((INTERVAL_HIGH - INTERVAL_LOW) / 2.0)
CENTER = (INTERVAL_HIGH + INTERVAL_LOW) / 2.0
HALF_WIDTH = (INTERVAL_HIGH - INTERVAL_LOW) / 2.0
RHO0 = 1.0 / SIGMA
RHO1 = 1.0 / (2.0 * SIGMA - RHO0)
RHO2 = 1.0 / (2.0 * SIGMA - RHO1)


STEP1 = 2.0 * RHO1 / HALF_WIDTH
STEP2 = 2.0 * RHO2 / HALF_WIDTH


def place_kernel(
    order_hbm, load_hbm, geom_hbm, abs_hbm,
    metric_ref, load_kv, bound_kv, far_ref, near_ref, pack_ref, lo_ref, hi_ref,
    flux_ref, work_ref, order_ref, load_ref, geom_ref, abs_ref, sems,
):
    copies = [
        pltpu.make_async_copy(source, target, sems.at[c])
        for c, (source, target) in enumerate(
            [(order_hbm, order_ref), (load_hbm, load_ref), (geom_hbm, geom_ref), (abs_hbm, abs_ref)]
        )
    ]
    for copy in copies:
        copy.start()
    copies[0].wait()
    copies[1].wait()
    pick = jnp.where(
        lax.broadcasted_iota(jnp.int32, (64, 64), 0) == order_ref[...], 1.0, 0.0
    ).astype(jnp.bfloat16)
    low = lane_iota(ROWS) < 64

    def spread(placed, store):
        for b in range(4):
            piece = placed[:, b * LANES : (b + 1) * LANES]
            first, second = piece[:ROWS], piece[ROWS:]
            store(2 * b, jnp.where(low, first, roll(second, 64, 1)))
            store(2 * b + 1, jnp.where(low, roll(first, 64, 1), second))

    load = load_ref[...]
    high, rest = split(load)
    middle = (load - high.astype(jnp.float32) - rest.astype(jnp.float32)).astype(jnp.bfloat16)

    def store_load(i, value):
        work_ref[i] = value

    spread(dot(pick, high) + (dot(pick, rest) + dot(pick, middle)), store_load)
    even = is_even()
    store_assembled(
        load_kv, far_ref, near_ref, even, lambda i: work_ref[i], 0, pack_ref
    )
    store_edges(lo_ref, hi_ref, 3, 3, [edge(load_kv[i]) for i in range(NODES)])

    copies[2].wait()
    for c in range(7):

        def store_metric(i, value, c=c):
            metric_ref[c, i] = value

        spread(dot(pick, geom_ref[c]), store_metric)
    for slot, c in enumerate(WHOLE):
        store_edges(lo_ref, hi_ref, slot, slot, [edge(metric_ref[c, i]) for i in range(NODES)])
    for slot, c in enumerate(LINES):
        lines = line_pack(lambda i, c=c: metric_ref[c, i])
        lo_ref[5, slot] = lines
        hi_ref[5, slot] = lines

    lane = lane_iota(8)
    q_a = jnp.zeros((8, LANES), jnp.float32)
    q_r = jnp.zeros((8, LANES), jnp.float32)
    for m in range(NODES):
        q_a = jnp.where((lane // 8) % 8 == m, float(ROW_TOTAL[m]), q_a)
        q_r = jnp.where(lane % 8 == m, float(ROW_TOTAL[m]), q_r)
    for chunk in range(ROWS // 8):
        rows = pl.ds(chunk * 8, 8)
        h_z = []
        for i in range(NODES):
            at = pl.ds(i * ROWS + chunk * 8, 8)
            q_z = float(ROW_TOTAL[i])
            g = [jnp.abs(metric_ref[c, i, rows]) for c in range(6)]
            h_z.append(g[0] * q_z + g[3] * q_a + g[4] * q_r)
            flux_ref[0, at] = g[3] * q_z + g[1] * q_a + g[5] * q_r
            flux_ref[1, at] = g[4] * q_z + g[5] * q_a + g[2] * q_r
        part_z = along_nodes_plain(h_z, ABS_DERIV.T)
        for i in range(NODES):
            work_ref[i, rows] = part_z[i] + jnp.abs(metric_ref[6, i, rows])
    flux = jnp.concatenate([flux_ref[0], flux_ref[1]], axis=1)
    copies[3].wait()
    work_ref[...] += dot_split(flux, abs_ref).reshape(FIELD)
    store_assembled(
        bound_kv, far_ref, near_ref, even, lambda i: work_ref[i], 1, pack_ref
    )
    store_edges(lo_ref, hi_ref, 4, 4, [edge(bound_kv[i]) for i in range(NODES)])


def first_kernel(
    load_kv, bound_kv, h0, h1, h2, left_ref, right_ref, metric_ref, grad_ref, diver_ref,
    residual_ref, inverse_ref, update_ref, ghost_inverse, ghost_metric, flux_ref, part_ref, far_ref, near_ref,
    v_ref,
):
    residual = completed(load_kv, (h0, h1, h2), 0)
    bound = completed(bound_kv, (h0, h1, h2), 1)
    for i in range(NODES):
        r = residual(i)
        inverse = 1.0 / bound(i)
        update = r * inverse * (1.0 / CENTER)
        residual_ref[i] = r
        inverse_ref[i] = inverse
        update_ref[i] = update
        v_ref[i, :ROWS] = update
    residual, residual_sums = ghost_columns(left_ref[3], right_ref[3]), ghost_sums(h2, 0, True)
    bound, bound_sums = ghost_columns(left_ref[4], right_ref[4]), ghost_sums(h2, 1, True)
    for i in range(NODES):
        inverse = 1.0 / (bound[i] + bound_sums(i))
        ghost_inverse[i] = inverse
        v_ref[i, ROWS:] = (residual[i] + residual_sums(i)) * inverse * (1.0 / CENTER)
    for slot, c in enumerate(WHOLE):
        for i, value in enumerate(ghost_columns(left_ref[slot], right_ref[slot])):
            ghost_metric[c, i] = value
    for slot, c in enumerate(LINES):
        for i, value in enumerate(ghost_lines(left_ref[5, slot], right_ref[5, slot])):
            ghost_metric[c, i] = value
    apply_flux(v_ref, metric_ref, ghost_metric, grad_ref, flux_ref, part_ref)
    store_faces(flux_ref, part_ref, diver_ref, far_ref, near_ref)


def second_kernel(
    kv_in, h0, h1, source_ref, inverse_ref, update_in, metric_ref, grad_ref, diver_ref,
    start_ref, flux_ref, part_ref, far_ref, near_ref, v_ref,
):
    image = completed(kv_in, (h0, h1))
    for i in range(NODES):
        old = update_in[i]
        inverse = inverse_ref[i]
        source = source_ref[i]
        update = (RHO1 * RHO0) * old + STEP1 * inverse * (source - image(i))
        result = old + update
        v_ref[i] = result
        start_ref[i] = result + (RHO2 * RHO1) * update + STEP2 * inverse * source
    apply_flux(v_ref, metric_ref, None, grad_ref, flux_ref, part_ref)
    store_faces(flux_ref, part_ref, diver_ref, far_ref, near_ref)


def third_kernel(
    kv_in, h0, h1, h2, source_ref, inverse_ref, start_ref,
    ghost_inverse, ghost_metric, metric_ref, grad_ref, diver_ref,
    result_ref, flux_ref, part_ref, far_ref, near_ref, sums_ref, v_ref,
):
    image = completed(kv_in, (h0, h1, h2))
    plane = weight_plane()
    rz = jnp.zeros((ROWS, LANES), jnp.float32)
    for i in range(NODES):
        result = start_ref[i] - STEP2 * inverse_ref[i] * image(i)
        result_ref[i] = result
        v_ref[i, :ROWS] = result
        rz = rz + source_ref[i] * result * node_weight(i)
    start, sums = gathered_ghost(h2), ghost_sums(h2)
    for i in range(NODES):
        v_ref[i, ROWS:] = start[i] - STEP2 * ghost_inverse[i] * sums(i)
    apply_flux(v_ref, metric_ref, ghost_metric, grad_ref, flux_ref, part_ref)
    store_faces(flux_ref, part_ref, diver_ref, far_ref, near_ref)
    sums_ref[...] = sum_row([rz * plane])


def fourth_kernel(
    kv_in, h0, h1, inverse_ref, metric_ref, grad_ref, diver_ref,
    image_ref, update_ref, start_ref, flux_ref, part_ref, far_ref, near_ref,
):
    image = completed(kv_in, (h0, h1))
    for i in range(NODES):
        value = image(i)
        image_ref[i] = value
        update = value * inverse_ref[i] * (1.0 / CENTER)
        update_ref[i] = update
        start_ref[i] = (1.0 + RHO1 * RHO0 + STEP1 * CENTER) * update
    apply_flux(update_ref, metric_ref, None, grad_ref, flux_ref, part_ref)
    store_faces(flux_ref, part_ref, diver_ref, far_ref, near_ref)


def fifth_kernel(
    kv_in, h0, h1, h2, source_ref, inverse_ref, update_in,
    ghost_inverse, ghost_metric, metric_ref, grad_ref, diver_ref,
    start_ref, flux_ref, part_ref, far_ref, near_ref, v_ref,
):
    image = completed(kv_in, (h0, h1, h2))
    for i in range(NODES):
        old = update_in[i]
        inverse = inverse_ref[i]
        source = source_ref[i]
        update = (RHO1 * RHO0) * old + STEP1 * inverse * (source - image(i))
        result = old + update
        v_ref[i, :ROWS] = result
        start_ref[i] = result + (RHO2 * RHO1) * update + STEP2 * inverse * source
    start, sums = gathered_ghost(h2), ghost_sums(h2)
    for i in range(NODES):
        v_ref[i, ROWS:] = start[i] - STEP1 * ghost_inverse[i] * sums(i)
    apply_flux(v_ref, metric_ref, ghost_metric, grad_ref, flux_ref, part_ref)
    store_faces(flux_ref, part_ref, diver_ref, far_ref, near_ref)


def sixth_kernel(
    kv_in, h0, h1, source_ref, inverse_ref, start_ref, residual_ref, early_ref,
    metric_ref, grad_ref,
    result_ref, flux_ref, part_ref, sums_hbm, sums_ref, sem,
):
    image = completed(kv_in, (h0, h1))
    plane = weight_plane()
    r_y = jnp.zeros((ROWS, LANES), jnp.float32)
    w_y = jnp.zeros((ROWS, LANES), jnp.float32)
    for i in range(NODES):
        result = start_ref[i] - STEP2 * inverse_ref[i] * image(i)
        result_ref[i] = result
        r_y = r_y + residual_ref[i] * result * node_weight(i)
        w_y = w_y + source_ref[i] * result * node_weight(i)
    energy = apply_flux(
        result_ref, metric_ref, None, grad_ref, flux_ref, part_ref, with_energy=True
    )
    zero = jnp.zeros((1, LANES), jnp.float32)
    late = sum_row([zero, zero, r_y * plane, w_y * plane, energy])
    sums_ref[...] = jnp.broadcast_to(early_ref[...] + late, sums_ref.shape)
    leave = pltpu.make_async_copy(sums_ref, sums_hbm, sem)
    leave.start()
    leave.wait()


def rest_faces_kernel(flux_ref, part_ref, diver_ref, kv_ref, far_ref, near_ref, pack_ref):
    planes = whole_planes(flux_ref, part_ref, diver_ref, range(NODES))
    store_assembled(kv_ref, far_ref, near_ref, is_even(), lambda i: planes[i], 0, pack_ref)


def spread_fields(order_ref, fields, out_ref, spread_ref):
    low = lane_iota(ROWS) < 64
    pick = jnp.where(
        lax.broadcasted_iota(jnp.int32, (64, 64), 1) == order_ref[...], 1.0, 0.0
    ).astype(jnp.bfloat16)
    for f, field in enumerate(fields):
        for b in range(NODES // 2):
            even, odd = field(2 * b), field(2 * b + 1)
            lanes = pl.ds(b * LANES, LANES)
            spread_ref[:ROWS, lanes] = jnp.where(low, even, roll(odd, 64, 1))
            spread_ref[ROWS:, lanes] = jnp.where(low, roll(even, 64, 1), odd)
        value = spread_ref[...]
        high, middle = split(value)
        rest = (value - high.astype(jnp.float32) - middle.astype(jnp.float32)).astype(jnp.bfloat16)
        out_ref[f] = dot(pick, high) + (dot(pick, middle) + dot(pick, rest))


def spread_early_kernel(order_ref, first_ref, residual_ref, image_ref, out_ref, spread_ref):
    refs = (first_ref, residual_ref, image_ref)
    spread_fields(order_ref, [lambda i, ref=ref: ref[i] for ref in refs], out_ref, spread_ref)


def spread_late_kernel(kv_in, h0, h1, h2, second_ref, order_ref, out_ref, spread_ref):
    fields = [lambda i: second_ref[i], completed(kv_in, (h0, h1, h2))]
    spread_fields(order_ref, fields, out_ref, spread_ref)


def half_sum_kernel(rows_ref, out_ref):
    out_ref[...] = jnp.broadcast_to(
        jnp.sum(rows_ref[...], axis=0, keepdims=True), out_ref.shape
    )


def last_kernel(sums_ref, spread_ref, late_ref, solution_ref, residual_ref):
    sums = jnp.sum(sums_ref[...], axis=0)
    lane = lane_iota(1)

    def total(d):
        return jnp.sum(jnp.where(lane == d, sums, 0.0), axis=1, keepdims=True)

    rz0, zw, ry, wy, yq = (total(d) for d in range(5))
    alpha0 = rz0 / zw
    rz1 = rz0 - alpha0 * (zw + ry) + alpha0 * alpha0 * wy
    beta = rz1 / rz0
    share = 1.0 + beta
    energy = share * share * zw - 2.0 * share * alpha0 * wy + alpha0 * alpha0 * yq
    alpha1 = rz1 / energy
    first_scale = alpha0 + alpha1 * share
    second_scale = alpha1 * alpha0
    solution_ref[...] = first_scale * spread_ref[0] - second_scale * late_ref[0]
    residual_ref[...] = (
        spread_ref[1] - first_scale * spread_ref[2] + second_scale * late_ref[1]
    )


VMEM_LIMIT = 24 * 1024 * 1024
F32 = jnp.float32


def call(kernel, outs, scratch, *operands, space=pltpu.VMEM, out_spaces=None, cost=None):
    out_spaces = out_spaces or [pltpu.VMEM] * len(outs)
    return pl.pallas_call(
        kernel,
        out_shape=[jax.ShapeDtypeStruct(s, F32) for s in outs],
        in_specs=[pl.BlockSpec(memory_space=space)] * len(operands),
        out_specs=[pl.BlockSpec(memory_space=s) for s in out_spaces],
        scratch_shapes=[pltpu.VMEM(s, F32) if isinstance(s, tuple) else s for s in scratch],
        cost_estimate=cost,
        compiler_params=pltpu.CompilerParams(vmem_limit_bytes=VMEM_LIMIT),
    )(*operands)


FLUX = (2, NODES * ROWS, LANES)
COST = pl.CostEstimate(flops=10**11, transcendentals=0, bytes_accessed=10**8)
BIG_FLUX = (2, NODES * GROWS, LANES)


def faces(fields=1):
    return [(fields, ROWS, LANES), (fields, ROWS, LANES)]


def packs(fields=1):
    return [(fields, HALF, LANES)]


def swap_far(far):
    count = lax.axis_size(WIDE)
    return lax.ppermute(
        far, WIDE, [(w, (w + 1 if w % 2 else w - 1) % count) for w in range(count)]
    )


def swap_wide(far, near):
    count = lax.axis_size(WIDE)
    return swap_far(far), lax.ppermute(near, WIDE, [(w, w ^ 1) for w in range(count)])


def swap_all(far, near, pack, rows):
    far, near = swap_wide(far, near)
    (pack,) = call(pack_kernel, [(pack.shape[0], rows, LANES)], [], pack, far, near, cost=COST)
    return far, near, lax.all_gather(pack, "narrow")


def edges(fields):
    return (fields, NODES // 2, HALF, LANES)


def swap_edged(step, inverse, far, near, pack, edges_out):
    far, near = swap_wide(far, near)
    (pack,) = call(
        functools.partial(pack_edges_kernel, step),
        [(1, HALF * (1 + NODES), LANES)],
        [],
        pack, edges_out, inverse, far, near,
    )
    return far, near, lax.all_gather(pack, "narrow")


def swap_edges(lo, hi):
    count = lax.axis_size("narrow")
    left = lax.ppermute(hi, "narrow", [(n, (n + 1) % count) for n in range(count)])
    right = lax.ppermute(lo, "narrow", [(n, (n - 1) % count) for n in range(count)])
    return left, right


def local(load, geom, element_order):
    grad = jnp.asarray(GRAD_HL)
    diver = jnp.asarray(DIVER_HL)
    metric, load_kv, bound_kv, *face, lo, hi = call(
        place_kernel,
        [(7,) + FIELD, FIELD, FIELD] + faces(2) + packs(2) + [edges(6)] * 2,
        [
            FLUX, FIELD,
            pltpu.VMEM((1, 64), jnp.int32), pltpu.VMEM(load.shape, load.dtype),
            pltpu.VMEM(geom.shape, geom.dtype), pltpu.VMEM(ABS_HL.shape, jnp.bfloat16),
            pltpu.SemaphoreType.DMA((4,)),
        ],
        *(pltpu.with_memory_space_constraint(x, pltpu.HBM) for x in (element_order.reshape(1, 64), load, geom, jnp.asarray(ABS_HL))),
        space=pltpu.HBM,
    )
    sides = swap_edges(lo, hi)
    halo = swap_all(*face, GROWS)
    residual, inverse, update, ghost_inverse, ghost_metric, *parts, far, near = call(
        first_kernel,
        [FIELD, FIELD, FIELD, GHOST, (7,) + GHOST, BIG_FLUX, BIG] + faces(),
        [BIG],
        load_kv, bound_kv, *halo, *sides, metric, grad, diver,
    )
    (kv,) = call(rest_kernel, [FIELD], [], *parts, diver)
    halo = swap_wide(far, near)
    start, *parts, far, near = call(
        second_kernel,
        [FIELD, FLUX, FIELD] + faces(),
        [FIELD],
        kv, *halo, residual, inverse, update, metric, grad, diver,
    )
    kv, *side = call(
        functools.partial(rest_edges_kernel, STEP2),
        [FIELD] + packs() + [edges(2)],
        [],
        *parts, diver, start, inverse,
    )
    halo = swap_edged(STEP2, inverse, far, near, *side)
    first, *parts, far, near, early = call(
        third_kernel,
        [FIELD, BIG_FLUX, BIG] + faces() + [(1, LANES)],
        [BIG],
        kv, *halo, residual, inverse, start, ghost_inverse, ghost_metric, metric, grad, diver,
    )
    kv, early = call(rest_energy_kernel, [FIELD, (1, LANES)], [], *parts, diver, first, early)
    halo = swap_wide(far, near)
    image, update, start, *parts, far, near = call(
        fourth_kernel,
        [FIELD, FIELD, FIELD, FLUX, FIELD] + faces(),
        [],
        kv, *halo, inverse, metric, grad, diver,
    )
    kv, *side = call(
        functools.partial(rest_edges_kernel, STEP1),
        [FIELD] + packs() + [edges(2)],
        [],
        *parts, diver, start, inverse,
    )
    halo = swap_edged(STEP1, inverse, far, near, *side)
    start, *parts, far, near = call(
        fifth_kernel,
        [FIELD, BIG_FLUX, BIG] + faces(),
        [BIG],
        kv, *halo, image, inverse, update, ghost_inverse, ghost_metric, metric, grad, diver,
    )
    (kv,) = call(rest_kernel, [FIELD], [], *parts, diver)
    halo = swap_wide(far, near)
    order = element_order.reshape(64, 1)
    (spread,) = call(
        spread_early_kernel, [(3, 64, 512)], [(64, 512)], order, first, residual, image
    )
    kv, spread = lax.optimization_barrier((kv, spread))
    sums_shape = (lax.axis_size(REST), LANES)
    second, *parts, sums = call(
        sixth_kernel,
        [FIELD, FLUX, FIELD, sums_shape],
        [sums_shape, pltpu.SemaphoreType.DMA(())],
        kv, *halo, image, inverse, start, residual, early, metric, grad,
        out_spaces=[pltpu.VMEM] * 3 + [pltpu.HBM],
    )
    sums = lax.all_to_all(sums[:, None], REST, 0, 0)
    kv, far, near, pack = call(
        rest_faces_kernel, [FIELD] + faces() + packs(), [], *parts, diver
    )
    far = swap_far(far)
    ring = lax.axis_size("ring")
    (sums,) = call(half_sum_kernel, [(ring, 1, LANES)], [], sums)
    near, sums = lax.optimization_barrier((near, sums))
    sums = lax.all_to_all(sums, "ring", 0, 0)
    near = lax.all_gather(
        near, "ring", axis_index_groups=[[v, v + 1] for v in range(0, ring, 2)]
    )
    (pack,) = call(pack_kernel, [pack.shape], [], pack, far, near)
    halo = far, near, lax.all_gather(pack, "narrow")
    (late,) = call(spread_late_kernel, [(2, 64, 512)], [(64, 512)], kv, *halo, second, order)
    return tuple(call(last_kernel, [(64, 512), (64, 512)], [], sums, spread, late))


def solution(mesh):
    wide, narrow = mesh.devices.shape
    ring = 12 if wide % 12 == 0 else 2
    fine = jax.sharding.Mesh(
        mesh.devices.reshape(wide // ring, ring, narrow), ("outer", "ring", "narrow")
    )
    rows = ("outer", "ring", "narrow")
    return jax.shard_map(
        local,
        mesh=fine,
        in_specs=(P(rows, None), P(None, rows, None), P(WIDE, "narrow", None)),
        out_specs=(P(rows, None), P(rows, None)),
        check_vma=False,
    )
```

```python
import functools

import jax
import jax.numpy as jnp
import ml_dtypes
import numpy as np
from jax import lax
from jax.experimental import pallas as pl
from jax.experimental.pallas import tpu as pltpu
from jax.sharding import PartitionSpec as P

NODES = 8
ROWS = 32
LANES = 128
HALF = 16
GROWS = ROWS + HALF
INTERVAL_LOW = 0.03
INTERVAL_HIGH = 1.0
FIELD = (NODES, ROWS, LANES)
GHOST = (NODES, HALF, LANES)
BIG = (NODES, GROWS, LANES)
WIDE = ("outer", "ring")
REST = ("outer", "narrow")


def legendre_seven(point):
    before = 1.0
    current = point
    for degree in range(1, 7):
        after = ((2.0 * degree + 1.0) * point * current - degree * before) / (degree + 1.0)
        before = current
        current = after
    return current


def gll_derivative():
    points = 8
    inner_nodes = [
        -0.8717401485096066,
        -0.5917001814331423,
        -0.2092992179024789,
        0.2092992179024789,
        0.5917001814331423,
        0.8717401485096066,
    ]
    nodes = [-1.0] + inner_nodes + [1.0]
    values_at = [legendre_seven(node) for node in nodes]
    matrix = np.zeros((points, points))
    for source in range(points):
        for target in range(points):
            if source != target:
                matrix[source, target] = values_at[source] / (
                    values_at[target] * (nodes[source] - nodes[target])
                )
    matrix[0, 0] = -(points - 1) * points / 4.0
    matrix[points - 1, points - 1] = (points - 1) * points / 4.0
    return matrix


DERIV = gll_derivative().astype(np.float32)
ABS_DERIV = np.abs(DERIV)
ROW_TOTAL = ABS_DERIV.sum(axis=1)
EYE8 = np.eye(8, dtype=np.float32)


def cycle_matrix(small):
    return np.kron(np.eye(2, dtype=np.float32), np.kron(small, EYE8))


def radial_matrix(small):
    return np.kron(np.eye(16, dtype=np.float32), small)


def split_const(matrix):
    high = matrix.astype(ml_dtypes.bfloat16)
    low = (matrix - high.astype(np.float32)).astype(ml_dtypes.bfloat16)
    return high, low


GRAD = np.concatenate([cycle_matrix(DERIV.T), radial_matrix(DERIV.T)], axis=1)
DIVER = np.concatenate([cycle_matrix(DERIV), radial_matrix(DERIV)], axis=0)
GRAD_PARTS = split_const(GRAD)
GRAD_HL = np.concatenate([GRAD_PARTS[0], GRAD_PARTS[0], GRAD_PARTS[1]], axis=0)
DIVER_HL = np.concatenate(split_const(DIVER), axis=1)
ABS_HL = np.concatenate(split_const(np.abs(DIVER)), axis=1)


def split(value):
    high = value.astype(jnp.bfloat16)
    return high, (value - high.astype(jnp.float32)).astype(jnp.bfloat16)


def dot(left, right):
    return lax.dot_general(
        left, right, (((1,), (0,)), ((), ())), preferred_element_type=jnp.float32
    )


def dot_grad(value, grad_ref):
    high, low = split(value)
    both = jnp.concatenate([high, low], axis=1)
    return dot(both, grad_ref[: 2 * LANES]) + dot(high, grad_ref[2 * LANES :])


def dot_diver(value, diver_ref):
    high, low = split(value)
    both = dot(high, diver_ref[...])
    return both[:, :LANES] + (both[:, LANES:] + dot(low, diver_ref[:, :LANES]))


def lane_iota(rows):
    return lax.broadcasted_iota(jnp.int32, (rows, LANES), 1)


def row_iota(rows):
    return lax.broadcasted_iota(jnp.int32, (rows, LANES), 0)


def roll(value, shift, axis):
    size = value.shape[axis]
    return pltpu.roll(value, shift % size, axis)


def along_nodes(values, small):
    half = NODES // 2
    even = [values[i] + values[NODES - 1 - i] for i in range(half)]
    odd = [values[i] - values[NODES - 1 - i] for i in range(half)]
    out = [None] * NODES
    for m in range(half):
        from_even, from_odd = None, None
        for i in range(half):
            near, far = float(small[m][i]), float(small[m][NODES - 1 - i])
            one = even[i] * (0.5 * (near + far))
            two = odd[i] * (0.5 * (near - far))
            from_even = one if from_even is None else from_even + one
            from_odd = two if from_odd is None else from_odd + two
        out[m] = from_odd + from_even
        out[NODES - 1 - m] = from_odd - from_even
    return out


def along_nodes_plain(values, small):
    out = []
    for m in range(NODES):
        total = None
        for i in range(NODES):
            term = values[i] * float(small[m][i])
            total = term if total is None else total + term
        out.append(total)
    return out


def edge(value):
    return jnp.where(lane_iota(HALF) < 64, value[:HALF], value[HALF:])


def packed_edges(even, odd):
    low = lane_iota(HALF) < 64
    return jnp.where(low, even, roll(odd, 64, 1)), jnp.where(low, roll(even, 64, 1), odd)


def store_edges(lo_ref, hi_ref, lo_at, hi_at, values):
    for b in range(NODES // 2):
        lo_ref[lo_at, b], hi_ref[hi_at, b] = packed_edges(values[2 * b], values[2 * b + 1])


def ghost_columns(lefts, rights):
    low = lane_iota(HALF) < 64
    out = []
    for b in range(NODES // 2):
        left, right = lefts[b], rights[b]
        out.append(jnp.where(low, left, roll(right, 64, 1)))
        out.append(jnp.where(low, roll(left, 64, 1), right))
    return out


def gathered_ghost(packs_ref):
    left, right = beside(packs_ref)
    half = range(NODES // 2)
    return ghost_columns(
        [packs_ref[left, 0, HALF * (5 + b) : HALF * (6 + b)] for b in half],
        [packs_ref[right, 0, HALF * (1 + b) : HALF * (2 + b)] for b in half],
    )


def facing(left, right):
    return roll(jnp.where(lane_iota(HALF) < 64, right, left), 64, 1)


def own_assembly(u):
    count = u.shape[0]
    k = lane_iota(count) % 8
    er = row_iota(count) % HALF
    up = roll(roll(u, -1, 0), 7, 1)
    down = roll(roll(u, 1, 0), -7, 1)
    u = (
        u
        + jnp.where((k == 7) & (er < HALF - 1), up, 0.0)
        + jnp.where((k == 0) & (er > 0), down, 0.0)
    )
    top, bottom = u[:HALF], u[HALF:ROWS]
    lane = lane_iota(HALF)
    j = (lane // 8) % 8
    block = lane // 64
    new_top = (
        top
        + jnp.where(j == 7, roll(bottom, 56, 1), 0.0)
        + jnp.where((j == 0) & (block == 1), roll(bottom, 8, 1), 0.0)
    )
    new_bottom = (
        bottom
        + jnp.where(j == 0, roll(top, -56, 1), 0.0)
        + jnp.where((j == 7) & (block == 0), roll(top, -8, 1), 0.0)
    )
    if count == GROWS:
        ghost = u[ROWS:]
        new_top = new_top + jnp.where(lane < 8, roll(ghost, -56, 1), 0.0)
        new_bottom = new_bottom + jnp.where(lane >= 120, roll(ghost, 56, 1), 0.0)
    return jnp.concatenate([new_top, new_bottom], axis=0)


def ends(value):
    lane = lane_iota(HALF)
    return jnp.where(lane < 8, value[:HALF], jnp.where(lane >= 120, value[HALF:], 0.0))


def store_assembled(kv_ref, far_ref, near_ref, even, source, field=0, pack_ref=None):
    pack = None
    for i in range(NODES):
        value = own_assembly(source(i))
        kv_ref[i] = value
        if i == 0:
            first = value
        last = value
        if pack_ref is not None:
            piece = ends(value)
            if i:
                piece = roll(piece, 16 * i, 1)
            pack = piece if pack is None else pack + piece
    near_ref[field] = jnp.where(even, last, first)
    far_ref[field] = jnp.where(even, first, last)
    if pack_ref is not None:
        pack_ref[field] = pack


def is_even():
    return lax.broadcast_in_dim(lax.rem(lax.axis_index("ring"), 2), (ROWS, LANES), ()) == 0


def near_face(near_ref, field, even):
    if near_ref.ndim == 4:
        return jnp.where(even, near_ref[1, field], near_ref[0, field])
    return near_ref[field]


def pack_kernel(pack_in, far_ref, near_ref, pack_ref):
    even = is_even()
    for field in range(pack_ref.shape[0]):
        near, far = near_face(near_ref, field, even), far_ref[field]
        first = jnp.where(even, far, near)
        last = jnp.where(even, near, far)
        pack_ref[field, :HALF] = (
            pack_in[field] + ends(first) + roll(ends(last), 16 * (NODES - 1), 1)
        )
        if pack_ref.shape[1] > HALF:
            pack_ref[field, HALF:ROWS] = edge(first)
            pack_ref[field, ROWS:] = edge(last)


def pack_edges_kernel(step, pack_in, edges_in, inverse_ref, far_ref, near_ref, pack_ref):
    even = is_even()
    near, far = near_ref[0], far_ref[0]
    first = jnp.where(even, far, near)
    last = jnp.where(even, near, far)
    pack_ref[0, :HALF] = pack_in[0] + ends(first) + roll(ends(last), 16 * (NODES - 1), 1)
    zero = jnp.zeros((HALF, LANES), jnp.float32)
    for b in range(NODES // 2):
        lo, hi = edges_in[0, b], edges_in[1, b]
        if b == 0:
            add = packed_edges(edge(-step * inverse_ref[0] * first), zero)
            lo, hi = lo + add[0], hi + add[1]
        if b == NODES // 2 - 1:
            add = packed_edges(zero, edge(-step * inverse_ref[NODES - 1] * last))
            lo, hi = lo + add[0], hi + add[1]
        pack_ref[0, HALF * (1 + b) : HALF * (2 + b)] = lo
        pack_ref[0, HALF * (5 + b) : HALF * (6 + b)] = hi


WHOLE = (1, 3, 5)
LINES = (0, 2, 4, 6)


def line_pack(field):
    pack = None
    for i in range(NODES):
        piece = ends(field(i))
        if i:
            piece = roll(piece, 16 * i, 1)
        pack = piece if pack is None else pack + piece
    return pack


def ghost_lines(left, right):
    lane = lane_iota(HALF)
    both = jnp.where(lane % 16 >= 8, left, right)
    inner = (lane >= 56) & (lane < 72)
    return [jnp.where(inner, roll(both, 64 - 16 * i, 1), 0.0) for i in range(NODES)]


def beside(packs_ref):
    count = packs_ref.shape[0]
    here = lax.axis_index("narrow")
    return lax.rem(here + count - 1, count), lax.rem(here + 1, count)


def completed(kv, halo, field=0):
    far_ref, near_ref = halo[:2]
    even = is_even()
    near, far = near_face(near_ref, field, even), far_ref[field]
    lane = lane_iota(HALF)
    if len(halo) > 2:
        left, right = beside(halo[2])
        side = jnp.where(
            lane % 16 < 8,
            roll(halo[2][left, field, :HALF], 8, 1),
            roll(halo[2][right, field, :HALF], -8, 1),
        )

    def value(i):
        u = kv[i]
        if len(halo) > 2:
            piece = roll(side, -16 * i, 1) if i else side
            u = u + jnp.concatenate(
                [jnp.where(lane < 8, piece, 0.0), jnp.where(lane >= 120, piece, 0.0)], axis=0
            )
        if i == 0:
            u = u + jnp.where(even, far, near)
        if i == NODES - 1:
            u = u + jnp.where(even, near, far)
        return u

    return value


def ghost_sums(packs_ref, field=0, wide_too=False):
    left, right = beside(packs_ref)
    lane = lane_iota(HALF)
    own = packs_ref[lax.axis_index("narrow"), field, :HALF]
    lines = jnp.where(lane % 16 < 8, own, roll(own, 16, 1))
    inner = (lane >= 56) & (lane < 72)

    def value(i):
        u = jnp.where(inner, roll(lines, 56 - 16 * i, 1), 0.0)
        if wide_too and i in (0, NODES - 1):
            rows = slice(HALF, ROWS) if i == 0 else slice(ROWS, GROWS)
            u = u + facing(packs_ref[left, field, rows], packs_ref[right, field, rows])
        return u

    return value


def apply_flux(v_ref, metric_ref, ghost_ref, grad_ref, flux_ref, part_ref, with_energy=False):
    count = v_ref.shape[1]
    energy = jnp.zeros((8, LANES), jnp.float32)
    side = dot_grad(v_ref[...].reshape(NODES * count, LANES), grad_ref)
    flux_ref[0] = side[:, :LANES]
    flux_ref[1] = side[:, LANES:]
    for chunk in range(count // 8):
        rows = pl.ds(chunk * 8, 8)
        if chunk < ROWS // 8:
            geometry, there = metric_ref, rows
        else:
            geometry, there = ghost_ref, pl.ds(chunk * 8 - ROWS, 8)
        values = [v_ref[i, rows] for i in range(NODES)]
        grad_z = along_nodes(values, DERIV)
        flux_z = []
        for i in range(NODES):
            at = pl.ds(i * count + chunk * 8, 8)
            g_z, g_a, g_r = grad_z[i], flux_ref[0, at], flux_ref[1, at]
            m = [geometry[c, i, there] for c in range(6)]
            f_z = m[0] * g_z + m[3] * g_a + m[4] * g_r
            f_a = m[3] * g_z + m[1] * g_a + m[5] * g_r
            f_r = m[4] * g_z + m[5] * g_a + m[2] * g_r
            flux_z.append(f_z)
            flux_ref[0, at] = f_a
            flux_ref[1, at] = f_r
            if with_energy:
                energy = energy + (g_z * f_z + g_a * f_a + g_r * f_r)
        part_z = along_nodes(flux_z, DERIV.T)
        for i in range(NODES):
            screened = geometry[6, i, there] * values[i]
            part_ref[i, rows] = part_z[i] + screened
            if with_energy:
                energy = energy + screened * values[i]
    return energy


def whole_planes(flux_ref, part_ref, diver_ref, planes):
    count = part_ref.shape[1]

    def flux(f):
        if len(planes) == NODES:
            return flux_ref[f]
        return jnp.concatenate([flux_ref[f, i * count : (i + 1) * count] for i in planes], axis=0)

    total = dot_diver(jnp.concatenate([flux(0), flux(1)], axis=1), diver_ref)
    return [
        part_ref[i] + total[n * count : (n + 1) * count] for n, i in enumerate(planes)
    ]


def store_faces(first, last, far_ref, near_ref, field=0):
    first, last = own_assembly(first), own_assembly(last)
    even = is_even()
    near_ref[field] = jnp.where(even, last, first)
    far_ref[field] = jnp.where(even, first, last)


def store_flux_faces(flux_ref, part_ref, diver_ref, far_ref, near_ref, field=0):
    planes = whole_planes(flux_ref, part_ref, diver_ref, (0, NODES - 1))
    store_faces(*planes, far_ref, near_ref, field)


def rest_kernel(flux_ref, part_ref, diver_ref, kv_ref):
    for i, u in enumerate(whole_planes(flux_ref, part_ref, diver_ref, range(NODES))):
        kv_ref[i] = own_assembly(u)


def rest_energy_kernel(flux_ref, part_ref, diver_ref, v_ref, sums_in, kv_ref, sums_ref):
    energy = jnp.zeros((ROWS, LANES), jnp.float32)
    for i, u in enumerate(whole_planes(flux_ref, part_ref, diver_ref, range(NODES))):
        kv_ref[i] = own_assembly(u)
        energy = energy + v_ref[i] * u[:ROWS]
    sums_ref[...] = sums_in[...] + sum_row([jnp.zeros((1, LANES), jnp.float32), energy])


def rest_edges_kernel(
    step, flux_ref, part_ref, diver_ref, start_ref, inverse_ref, kv_ref, pack_ref, edges_ref
):
    for i, u in enumerate(whole_planes(flux_ref, part_ref, diver_ref, range(NODES))):
        kv_ref[i] = own_assembly(u)
    pack_ref[0] = line_pack(lambda i: kv_ref[i])
    store_edges(
        edges_ref, edges_ref, 0, 1,
        [edge(start_ref[i] - step * inverse_ref[i] * kv_ref[i]) for i in range(NODES)],
    )


def weight_plane():
    lane, row = lane_iota(ROWS), row_iota(ROWS)
    j, k, er = (lane // 8) % 8, lane % 8, row % HALF
    w_a = jnp.where((j == 0) | (j == 7), 0.5, 1.0)
    shared = ((k == 0) & (er > 0)) | ((k == 7) & (er < HALF - 1))
    return w_a * jnp.where(shared, 0.5, 1.0)


def node_weight(i):
    return 0.5 if i in (0, NODES - 1) else 1.0


def sum_row(sums):
    lane = lane_iota(1)
    row = jnp.zeros((1, LANES), jnp.float32)
    for d, value in enumerate(sums):
        row = jnp.where(lane == d, jnp.sum(value), row)
    return row


SIGMA = ((INTERVAL_HIGH + INTERVAL_LOW) / 2.0) / ((INTERVAL_HIGH - INTERVAL_LOW) / 2.0)
CENTER = (INTERVAL_HIGH + INTERVAL_LOW) / 2.0
HALF_WIDTH = (INTERVAL_HIGH - INTERVAL_LOW) / 2.0
RHO0 = 1.0 / SIGMA
RHO1 = 1.0 / (2.0 * SIGMA - RHO0)
RHO2 = 1.0 / (2.0 * SIGMA - RHO1)


STEP1 = 2.0 * RHO1 / HALF_WIDTH
STEP2 = 2.0 * RHO2 / HALF_WIDTH


def place_kernel(
    order_hbm, load_hbm, geom_hbm, abs_hbm,
    metric_ref, placed_ref, flux_ref, part_ref, far_ref, near_ref,
    order_ref, load_ref, geom_ref, abs_ref, sems,
):
    copies = [
        pltpu.make_async_copy(source, target, sems.at[c])
        for c, (source, target) in enumerate(
            [(order_hbm, order_ref), (load_hbm, load_ref), (geom_hbm, geom_ref), (abs_hbm, abs_ref)]
        )
    ]
    for copy in copies:
        copy.start()
    copies[0].wait()
    copies[1].wait()
    pick = jnp.where(
        lax.broadcasted_iota(jnp.int32, (64, 64), 0) == order_ref[...], 1.0, 0.0
    ).astype(jnp.bfloat16)
    low = lane_iota(ROWS) < 64

    def spread(placed, store):
        for b in range(4):
            piece = placed[:, b * LANES : (b + 1) * LANES]
            first, second = piece[:ROWS], piece[ROWS:]
            store(2 * b, jnp.where(low, first, roll(second, 64, 1)))
            store(2 * b + 1, jnp.where(low, roll(first, 64, 1), second))

    load = load_ref[...]
    high, rest = split(load)
    middle = (load - high.astype(jnp.float32) - rest.astype(jnp.float32)).astype(jnp.bfloat16)

    def store_load(i, value):
        placed_ref[i] = value

    spread(dot(pick, high) + (dot(pick, rest) + dot(pick, middle)), store_load)
    store_faces(placed_ref[0], placed_ref[NODES - 1], far_ref, near_ref, 0)

    copies[2].wait()
    for c in range(7):

        def store_metric(i, value, c=c):
            metric_ref[c, i] = value

        spread(dot(pick, geom_ref[c]), store_metric)

    lane = lane_iota(8)
    q_a = jnp.zeros((8, LANES), jnp.float32)
    q_r = jnp.zeros((8, LANES), jnp.float32)
    for m in range(NODES):
        q_a = jnp.where((lane // 8) % 8 == m, float(ROW_TOTAL[m]), q_a)
        q_r = jnp.where(lane % 8 == m, float(ROW_TOTAL[m]), q_r)
    for chunk in range(ROWS // 8):
        rows = pl.ds(chunk * 8, 8)
        h_z = []
        for i in range(NODES):
            at = pl.ds(i * ROWS + chunk * 8, 8)
            q_z = float(ROW_TOTAL[i])
            g = [jnp.abs(metric_ref[c, i, rows]) for c in range(6)]
            h_z.append(g[0] * q_z + g[3] * q_a + g[4] * q_r)
            flux_ref[0, at] = g[3] * q_z + g[1] * q_a + g[5] * q_r
            flux_ref[1, at] = g[4] * q_z + g[5] * q_a + g[2] * q_r
        part_z = along_nodes_plain(h_z, ABS_DERIV.T)
        for i in range(NODES):
            part_ref[i, rows] = part_z[i] + jnp.abs(metric_ref[6, i, rows])
    copies[3].wait()
    store_flux_faces(flux_ref, part_ref, abs_ref, far_ref, near_ref, 1)


def rest_place_kernel(
    metric_ref, placed_ref, flux_ref, part_ref, abs_ref, load_kv, bound_kv, pack_ref, lo_ref, hi_ref
):
    planes = whole_planes(flux_ref, part_ref, abs_ref, range(NODES))
    for i in range(NODES):
        load_kv[i] = own_assembly(placed_ref[i])
        bound_kv[i] = own_assembly(planes[i])
    for field, kv in enumerate((load_kv, bound_kv)):
        pack_ref[field] = line_pack(lambda i, kv=kv: kv[i])
        store_edges(lo_ref, hi_ref, 3 + field, 3 + field, [edge(kv[i]) for i in range(NODES)])
    for slot, c in enumerate(WHOLE):
        store_edges(lo_ref, hi_ref, slot, slot, [edge(metric_ref[c, i]) for i in range(NODES)])
    for slot, c in enumerate(LINES):
        lines = line_pack(lambda i, c=c: metric_ref[c, i])
        lo_ref[5, slot] = lines
        hi_ref[5, slot] = lines


def first_kernel(
    load_kv, bound_kv, h0, h1, h2, left_ref, right_ref, metric_ref, grad_ref, diver_ref,
    residual_ref, inverse_ref, update_ref, ghost_inverse, ghost_metric, flux_ref, part_ref, far_ref, near_ref,
    v_ref,
):
    residual = completed(load_kv, (h0, h1, h2), 0)
    bound = completed(bound_kv, (h0, h1, h2), 1)
    for i in range(NODES):
        r = residual(i)
        inverse = 1.0 / bound(i)
        update = r * inverse * (1.0 / CENTER)
        residual_ref[i] = r
        inverse_ref[i] = inverse
        update_ref[i] = update
        v_ref[i, :ROWS] = update
    residual, residual_sums = ghost_columns(left_ref[3], right_ref[3]), ghost_sums(h2, 0, True)
    bound, bound_sums = ghost_columns(left_ref[4], right_ref[4]), ghost_sums(h2, 1, True)
    for i in range(NODES):
        inverse = 1.0 / (bound[i] + bound_sums(i))
        ghost_inverse[i] = inverse
        v_ref[i, ROWS:] = (residual[i] + residual_sums(i)) * inverse * (1.0 / CENTER)
    for slot, c in enumerate(WHOLE):
        for i, value in enumerate(ghost_columns(left_ref[slot], right_ref[slot])):
            ghost_metric[c, i] = value
    for slot, c in enumerate(LINES):
        for i, value in enumerate(ghost_lines(left_ref[5, slot], right_ref[5, slot])):
            ghost_metric[c, i] = value
    apply_flux(v_ref, metric_ref, ghost_metric, grad_ref, flux_ref, part_ref)
    store_flux_faces(flux_ref, part_ref, diver_ref, far_ref, near_ref)


def second_kernel(
    kv_in, h0, h1, source_ref, inverse_ref, update_in, metric_ref, grad_ref, diver_ref,
    start_ref, flux_ref, part_ref, far_ref, near_ref, v_ref,
):
    image = completed(kv_in, (h0, h1))
    for i in range(NODES):
        old = update_in[i]
        inverse = inverse_ref[i]
        source = source_ref[i]
        update = (RHO1 * RHO0) * old + STEP1 * inverse * (source - image(i))
        result = old + update
        v_ref[i] = result
        start_ref[i] = result + (RHO2 * RHO1) * update + STEP2 * inverse * source
    apply_flux(v_ref, metric_ref, None, grad_ref, flux_ref, part_ref)
    store_flux_faces(flux_ref, part_ref, diver_ref, far_ref, near_ref)


def third_kernel(
    kv_in, h0, h1, h2, source_ref, inverse_ref, start_ref,
    ghost_inverse, ghost_metric, metric_ref, grad_ref, diver_ref,
    result_ref, flux_ref, part_ref, far_ref, near_ref, sums_ref, v_ref,
):
    image = completed(kv_in, (h0, h1, h2))
    plane = weight_plane()
    rz = jnp.zeros((ROWS, LANES), jnp.float32)
    for i in range(NODES):
        result = start_ref[i] - STEP2 * inverse_ref[i] * image(i)
        result_ref[i] = result
        v_ref[i, :ROWS] = result
        rz = rz + source_ref[i] * result * node_weight(i)
    start, sums = gathered_ghost(h2), ghost_sums(h2)
    for i in range(NODES):
        v_ref[i, ROWS:] = start[i] - STEP2 * ghost_inverse[i] * sums(i)
    apply_flux(v_ref, metric_ref, ghost_metric, grad_ref, flux_ref, part_ref)
    store_flux_faces(flux_ref, part_ref, diver_ref, far_ref, near_ref)
    sums_ref[...] = sum_row([rz * plane])


def fourth_kernel(
    kv_in, h0, h1, inverse_ref, metric_ref, grad_ref, diver_ref,
    image_ref, update_ref, start_ref, flux_ref, part_ref, far_ref, near_ref,
):
    image = completed(kv_in, (h0, h1))
    for i in range(NODES):
        value = image(i)
        image_ref[i] = value
        update = value * inverse_ref[i] * (1.0 / CENTER)
        update_ref[i] = update
        start_ref[i] = (1.0 + RHO1 * RHO0 + STEP1 * CENTER) * update
    apply_flux(update_ref, metric_ref, None, grad_ref, flux_ref, part_ref)
    store_flux_faces(flux_ref, part_ref, diver_ref, far_ref, near_ref)


def fifth_kernel(
    kv_in, h0, h1, h2, source_ref, inverse_ref, update_in,
    ghost_inverse, ghost_metric, metric_ref, grad_ref, diver_ref,
    start_ref, flux_ref, part_ref, far_ref, near_ref, v_ref,
):
    image = completed(kv_in, (h0, h1, h2))
    for i in range(NODES):
        old = update_in[i]
        inverse = inverse_ref[i]
        source = source_ref[i]
        update = (RHO1 * RHO0) * old + STEP1 * inverse * (source - image(i))
        result = old + update
        v_ref[i, :ROWS] = result
        start_ref[i] = result + (RHO2 * RHO1) * update + STEP2 * inverse * source
    start, sums = gathered_ghost(h2), ghost_sums(h2)
    for i in range(NODES):
        v_ref[i, ROWS:] = start[i] - STEP1 * ghost_inverse[i] * sums(i)
    apply_flux(v_ref, metric_ref, ghost_metric, grad_ref, flux_ref, part_ref)
    store_flux_faces(flux_ref, part_ref, diver_ref, far_ref, near_ref)


def sixth_kernel(
    kv_in, h0, h1, source_ref, inverse_ref, start_ref, residual_ref, early_ref,
    metric_ref, grad_ref,
    result_ref, flux_ref, part_ref, sums_hbm, sums_ref, sem,
):
    image = completed(kv_in, (h0, h1))
    plane = weight_plane()
    r_y = jnp.zeros((ROWS, LANES), jnp.float32)
    w_y = jnp.zeros((ROWS, LANES), jnp.float32)
    for i in range(NODES):
        result = start_ref[i] - STEP2 * inverse_ref[i] * image(i)
        result_ref[i] = result
        r_y = r_y + residual_ref[i] * result * node_weight(i)
        w_y = w_y + source_ref[i] * result * node_weight(i)
    energy = apply_flux(
        result_ref, metric_ref, None, grad_ref, flux_ref, part_ref, with_energy=True
    )
    zero = jnp.zeros((1, LANES), jnp.float32)
    late = sum_row([zero, zero, r_y * plane, w_y * plane, energy])
    sums_ref[...] = jnp.broadcast_to(early_ref[...] + late, sums_ref.shape)
    leave = pltpu.make_async_copy(sums_ref, sums_hbm, sem)
    leave.start()
    leave.wait()


def rest_faces_kernel(flux_ref, part_ref, diver_ref, kv_ref, far_ref, near_ref, pack_ref):
    planes = whole_planes(flux_ref, part_ref, diver_ref, range(NODES))
    store_assembled(kv_ref, far_ref, near_ref, is_even(), lambda i: planes[i], 0, pack_ref)


def spread_fields(order_ref, fields, out_ref, spread_ref):
    low = lane_iota(ROWS) < 64
    pick = jnp.where(
        lax.broadcasted_iota(jnp.int32, (64, 64), 1) == order_ref[...], 1.0, 0.0
    ).astype(jnp.bfloat16)
    for f, field in enumerate(fields):
        for b in range(NODES // 2):
            even, odd = field(2 * b), field(2 * b + 1)
            lanes = pl.ds(b * LANES, LANES)
            spread_ref[:ROWS, lanes] = jnp.where(low, even, roll(odd, 64, 1))
            spread_ref[ROWS:, lanes] = jnp.where(low, roll(even, 64, 1), odd)
        value = spread_ref[...]
        high, middle = split(value)
        rest = (value - high.astype(jnp.float32) - middle.astype(jnp.float32)).astype(jnp.bfloat16)
        out_ref[f] = dot(pick, high) + (dot(pick, middle) + dot(pick, rest))


def spread_early_kernel(order_ref, first_ref, residual_ref, image_ref, out_ref, spread_ref):
    refs = (first_ref, residual_ref, image_ref)
    spread_fields(order_ref, [lambda i, ref=ref: ref[i] for ref in refs], out_ref, spread_ref)


def spread_late_kernel(kv_in, h0, h1, h2, second_ref, order_ref, out_ref, spread_ref):
    fields = [lambda i: second_ref[i], completed(kv_in, (h0, h1, h2))]
    spread_fields(order_ref, fields, out_ref, spread_ref)


def half_sum_kernel(rows_ref, out_ref):
    out_ref[...] = jnp.broadcast_to(
        jnp.sum(rows_ref[...], axis=0, keepdims=True), out_ref.shape
    )


def last_kernel(sums_ref, spread_ref, late_ref, solution_ref, residual_ref):
    sums = jnp.sum(sums_ref[...], axis=0)
    lane = lane_iota(1)

    def total(d):
        return jnp.sum(jnp.where(lane == d, sums, 0.0), axis=1, keepdims=True)

    rz0, zw, ry, wy, yq = (total(d) for d in range(5))
    alpha0 = rz0 / zw
    rz1 = rz0 - alpha0 * (zw + ry) + alpha0 * alpha0 * wy
    beta = rz1 / rz0
    share = 1.0 + beta
    energy = share * share * zw - 2.0 * share * alpha0 * wy + alpha0 * alpha0 * yq
    alpha1 = rz1 / energy
    first_scale = alpha0 + alpha1 * share
    second_scale = alpha1 * alpha0
    solution_ref[...] = first_scale * spread_ref[0] - second_scale * late_ref[0]
    residual_ref[...] = (
        spread_ref[1] - first_scale * spread_ref[2] + second_scale * late_ref[1]
    )


VMEM_LIMIT = 24 * 1024 * 1024
F32 = jnp.float32


def call(kernel, outs, scratch, *operands, space=pltpu.VMEM, out_spaces=None, cost=None):
    out_spaces = out_spaces or [pltpu.VMEM] * len(outs)
    return pl.pallas_call(
        kernel,
        out_shape=[jax.ShapeDtypeStruct(s, F32) for s in outs],
        in_specs=[pl.BlockSpec(memory_space=space)] * len(operands),
        out_specs=[pl.BlockSpec(memory_space=s) for s in out_spaces],
        scratch_shapes=[pltpu.VMEM(s, F32) if isinstance(s, tuple) else s for s in scratch],
        cost_estimate=cost,
        compiler_params=pltpu.CompilerParams(vmem_limit_bytes=VMEM_LIMIT),
    )(*operands)


FLUX = (2, NODES * ROWS, LANES)
COST = pl.CostEstimate(flops=10**11, transcendentals=0, bytes_accessed=10**8)
BIG_FLUX = (2, NODES * GROWS, LANES)


def faces(fields=1):
    return [(fields, ROWS, LANES), (fields, ROWS, LANES)]


def packs(fields=1):
    return [(fields, HALF, LANES)]


def swap_far(far):
    count = lax.axis_size(WIDE)
    return lax.ppermute(
        far, WIDE, [(w, (w + 1 if w % 2 else w - 1) % count) for w in range(count)]
    )


def swap_wide(far, near):
    count = lax.axis_size(WIDE)
    return swap_far(far), lax.ppermute(near, WIDE, [(w, w ^ 1) for w in range(count)])


def swap_all(far, near, pack, rows):
    far, near = swap_wide(far, near)
    (pack,) = call(pack_kernel, [(pack.shape[0], rows, LANES)], [], pack, far, near, cost=COST)
    return far, near, lax.all_gather(pack, "narrow")


def edges(fields):
    return (fields, NODES // 2, HALF, LANES)


def swap_edged(step, inverse, far, near, pack, edges_out):
    far, near = swap_wide(far, near)
    (pack,) = call(
        functools.partial(pack_edges_kernel, step),
        [(1, HALF * (1 + NODES), LANES)],
        [],
        pack, edges_out, inverse, far, near,
    )
    return far, near, lax.all_gather(pack, "narrow")


def swap_edges(lo, hi):
    count = lax.axis_size("narrow")
    left = lax.ppermute(hi, "narrow", [(n, (n + 1) % count) for n in range(count)])
    right = lax.ppermute(lo, "narrow", [(n, (n - 1) % count) for n in range(count)])
    return left, right


def local(load, geom, element_order):
    grad = jnp.asarray(GRAD_HL)
    diver = jnp.asarray(DIVER_HL)
    absolute = jnp.asarray(ABS_HL)
    metric, *parts, far, near = call(
        place_kernel,
        [(7,) + FIELD, FIELD, FLUX, FIELD] + faces(2),
        [
            pltpu.VMEM((1, 64), jnp.int32), pltpu.VMEM(load.shape, load.dtype),
            pltpu.VMEM(geom.shape, geom.dtype), pltpu.VMEM(ABS_HL.shape, jnp.bfloat16),
            pltpu.SemaphoreType.DMA((4,)),
        ],
        *(
            pltpu.with_memory_space_constraint(x, pltpu.HBM)
            for x in (element_order.reshape(1, 64), load, geom, absolute)
        ),
        space=pltpu.HBM,
    )
    load_kv, bound_kv, pack, lo, hi = call(
        rest_place_kernel,
        [FIELD, FIELD] + packs(2) + [edges(6)] * 2,
        [],
        metric, *parts, absolute,
    )
    sides = swap_edges(lo, hi)
    halo = swap_all(far, near, pack, GROWS)
    residual, inverse, update, ghost_inverse, ghost_metric, *parts, far, near = call(
        first_kernel,
        [FIELD, FIELD, FIELD, GHOST, (7,) + GHOST, BIG_FLUX, BIG] + faces(),
        [BIG],
        load_kv, bound_kv, *halo, *sides, metric, grad, diver,
    )
    (kv,) = call(rest_kernel, [FIELD], [], *parts, diver)
    halo = swap_wide(far, near)
    start, *parts, far, near = call(
        second_kernel,
        [FIELD, FLUX, FIELD] + faces(),
        [FIELD],
        kv, *halo, residual, inverse, update, metric, grad, diver,
    )
    kv, *side = call(
        functools.partial(rest_edges_kernel, STEP2),
        [FIELD] + packs() + [edges(2)],
        [],
        *parts, diver, start, inverse,
    )
    halo = swap_edged(STEP2, inverse, far, near, *side)
    first, *parts, far, near, early = call(
        third_kernel,
        [FIELD, BIG_FLUX, BIG] + faces() + [(1, LANES)],
        [BIG],
        kv, *halo, residual, inverse, start, ghost_inverse, ghost_metric, metric, grad, diver,
    )
    kv, early = call(rest_energy_kernel, [FIELD, (1, LANES)], [], *parts, diver, first, early)
    halo = swap_wide(far, near)
    image, update, start, *parts, far, near = call(
        fourth_kernel,
        [FIELD, FIELD, FIELD, FLUX, FIELD] + faces(),
        [],
        kv, *halo, inverse, metric, grad, diver,
    )
    kv, *side = call(
        functools.partial(rest_edges_kernel, STEP1),
        [FIELD] + packs() + [edges(2)],
        [],
        *parts, diver, start, inverse,
    )
    halo = swap_edged(STEP1, inverse, far, near, *side)
    start, *parts, far, near = call(
        fifth_kernel,
        [FIELD, BIG_FLUX, BIG] + faces(),
        [BIG],
        kv, *halo, image, inverse, update, ghost_inverse, ghost_metric, metric, grad, diver,
    )
    (kv,) = call(rest_kernel, [FIELD], [], *parts, diver)
    halo = swap_wide(far, near)
    order = element_order.reshape(64, 1)
    (spread,) = call(
        spread_early_kernel, [(3, 64, 512)], [(64, 512)], order, first, residual, image
    )
    kv, spread = lax.optimization_barrier((kv, spread))
    sums_shape = (lax.axis_size(REST), LANES)
    second, *parts, sums = call(
        sixth_kernel,
        [FIELD, FLUX, FIELD, sums_shape],
        [sums_shape, pltpu.SemaphoreType.DMA(())],
        kv, *halo, image, inverse, start, residual, early, metric, grad,
        out_spaces=[pltpu.VMEM] * 3 + [pltpu.HBM],
    )
    sums = lax.all_to_all(sums[:, None], REST, 0, 0)
    kv, far, near, pack = call(
        rest_faces_kernel, [FIELD] + faces() + packs(), [], *parts, diver
    )
    far = swap_far(far)
    ring = lax.axis_size("ring")
    (sums,) = call(half_sum_kernel, [(ring, 1, LANES)], [], sums)
    near, sums = lax.optimization_barrier((near, sums))
    sums = lax.all_to_all(sums, "ring", 0, 0)
    near = lax.all_gather(
        near, "ring", axis_index_groups=[[v, v + 1] for v in range(0, ring, 2)]
    )
    (pack,) = call(pack_kernel, [pack.shape], [], pack, far, near)
    halo = far, near, lax.all_gather(pack, "narrow")
    (late,) = call(spread_late_kernel, [(2, 64, 512)], [(64, 512)], kv, *halo, second, order)
    return tuple(call(last_kernel, [(64, 512), (64, 512)], [], sums, spread, late))


def solution(mesh):
    wide, narrow = mesh.devices.shape
    ring = 12 if wide % 12 == 0 else 2
    fine = jax.sharding.Mesh(
        mesh.devices.reshape(wide // ring, ring, narrow), ("outer", "ring", "narrow")
    )
    rows = ("outer", "ring", "narrow")
    return jax.shard_map(
        local,
        mesh=fine,
        in_specs=(P(rows, None), P(None, rows, None), P(WIDE, "narrow", None)),
        out_specs=(P(rows, None), P(rows, None)),
        check_vma=False,
    )
```

```python
import functools

import jax
import jax.numpy as jnp
import ml_dtypes
import numpy as np
from jax import lax
from jax.experimental import pallas as pl
from jax.experimental.pallas import tpu as pltpu
from jax.sharding import PartitionSpec as P

NODES = 8
ROWS = 32
LANES = 128
HALF = 16
GROWS = ROWS + HALF
INTERVAL_LOW = 0.03
INTERVAL_HIGH = 1.0
FIELD = (NODES, ROWS, LANES)
GHOST = (NODES, HALF, LANES)
BIG = (NODES, GROWS, LANES)
WIDE = ("outer", "ring")
REST = ("outer", "narrow")


def legendre_seven(point):
    before = 1.0
    current = point
    for degree in range(1, 7):
        after = ((2.0 * degree + 1.0) * point * current - degree * before) / (degree + 1.0)
        before = current
        current = after
    return current


def gll_derivative():
    points = 8
    inner_nodes = [
        -0.8717401485096066,
        -0.5917001814331423,
        -0.2092992179024789,
        0.2092992179024789,
        0.5917001814331423,
        0.8717401485096066,
    ]
    nodes = [-1.0] + inner_nodes + [1.0]
    values_at = [legendre_seven(node) for node in nodes]
    matrix = np.zeros((points, points))
    for source in range(points):
        for target in range(points):
            if source != target:
                matrix[source, target] = values_at[source] / (
                    values_at[target] * (nodes[source] - nodes[target])
                )
    matrix[0, 0] = -(points - 1) * points / 4.0
    matrix[points - 1, points - 1] = (points - 1) * points / 4.0
    return matrix


DERIV = gll_derivative().astype(np.float32)
ABS_DERIV = np.abs(DERIV)
ROW_TOTAL = ABS_DERIV.sum(axis=1)
EYE8 = np.eye(8, dtype=np.float32)


def cycle_matrix(small):
    return np.kron(np.eye(2, dtype=np.float32), np.kron(small, EYE8))


def radial_matrix(small):
    return np.kron(np.eye(16, dtype=np.float32), small)


def split_const(matrix):
    high = matrix.astype(ml_dtypes.bfloat16)
    low = (matrix - high.astype(np.float32)).astype(ml_dtypes.bfloat16)
    return high, low


GRAD = np.concatenate([cycle_matrix(DERIV.T), radial_matrix(DERIV.T)], axis=1)
DIVER = np.concatenate([cycle_matrix(DERIV), radial_matrix(DERIV)], axis=0)
GRAD_PARTS = split_const(GRAD)
GRAD_HL = np.concatenate([GRAD_PARTS[0], GRAD_PARTS[0], GRAD_PARTS[1]], axis=0)
DIVER_HL = np.concatenate(split_const(DIVER), axis=1)
ABS_HL = np.stack(split_const(np.abs(DIVER)))


def split(value):
    high = value.astype(jnp.bfloat16)
    return high, (value - high.astype(jnp.float32)).astype(jnp.bfloat16)


def dot(left, right):
    return lax.dot_general(
        left, right, (((1,), (0,)), ((), ())), preferred_element_type=jnp.float32
    )


def dot_split(value, matrix_ref):
    high, low = split(value)
    return dot(high, matrix_ref[0]) + (dot(low, matrix_ref[0]) + dot(high, matrix_ref[1]))


def dot_grad(value, grad_ref):
    high, low = split(value)
    both = jnp.concatenate([high, low], axis=1)
    return dot(both, grad_ref[: 2 * LANES]) + dot(high, grad_ref[2 * LANES :])


def dot_diver(value, diver_ref):
    high, low = split(value)
    both = dot(high, diver_ref[...])
    return both[:, :LANES] + (both[:, LANES:] + dot(low, diver_ref[:, :LANES]))


def lane_iota(rows):
    return lax.broadcasted_iota(jnp.int32, (rows, LANES), 1)


def row_iota(rows):
    return lax.broadcasted_iota(jnp.int32, (rows, LANES), 0)


def roll(value, shift, axis):
    size = value.shape[axis]
    return pltpu.roll(value, shift % size, axis)


def along_nodes(values, small):
    half = NODES // 2
    even = [values[i] + values[NODES - 1 - i] for i in range(half)]
    odd = [values[i] - values[NODES - 1 - i] for i in range(half)]
    out = [None] * NODES
    for m in range(half):
        from_even, from_odd = None, None
        for i in range(half):
            near, far = float(small[m][i]), float(small[m][NODES - 1 - i])
            one = even[i] * (0.5 * (near + far))
            two = odd[i] * (0.5 * (near - far))
            from_even = one if from_even is None else from_even + one
            from_odd = two if from_odd is None else from_odd + two
        out[m] = from_odd + from_even
        out[NODES - 1 - m] = from_odd - from_even
    return out


def along_nodes_plain(values, small):
    out = []
    for m in range(NODES):
        total = None
        for i in range(NODES):
            term = values[i] * float(small[m][i])
            total = term if total is None else total + term
        out.append(total)
    return out


def edge(value):
    return jnp.where(lane_iota(HALF) < 64, value[:HALF], value[HALF:])


def packed_edges(even, odd):
    low = lane_iota(HALF) < 64
    return jnp.where(low, even, roll(odd, 64, 1)), jnp.where(low, roll(even, 64, 1), odd)


def store_edges(lo_ref, hi_ref, lo_at, hi_at, values):
    for b in range(NODES // 2):
        lo_ref[lo_at, b], hi_ref[hi_at, b] = packed_edges(values[2 * b], values[2 * b + 1])


def ghost_columns(lefts, rights):
    low = lane_iota(HALF) < 64
    out = []
    for b in range(NODES // 2):
        left, right = lefts[b], rights[b]
        out.append(jnp.where(low, left, roll(right, 64, 1)))
        out.append(jnp.where(low, roll(left, 64, 1), right))
    return out


def gathered_ghost(packs_ref):
    left, right = beside(packs_ref)
    half = range(NODES // 2)
    return ghost_columns(
        [packs_ref[left, 0, HALF * (5 + b) : HALF * (6 + b)] for b in half],
        [packs_ref[right, 0, HALF * (1 + b) : HALF * (2 + b)] for b in half],
    )


def facing(left, right):
    return roll(jnp.where(lane_iota(HALF) < 64, right, left), 64, 1)


def own_assembly(u):
    count = u.shape[0]
    k = lane_iota(count) % 8
    er = row_iota(count) % HALF
    up = roll(roll(u, -1, 0), 7, 1)
    down = roll(roll(u, 1, 0), -7, 1)
    u = (
        u
        + jnp.where((k == 7) & (er < HALF - 1), up, 0.0)
        + jnp.where((k == 0) & (er > 0), down, 0.0)
    )
    top, bottom = u[:HALF], u[HALF:ROWS]
    lane = lane_iota(HALF)
    j = (lane // 8) % 8
    block = lane // 64
    new_top = (
        top
        + jnp.where(j == 7, roll(bottom, 56, 1), 0.0)
        + jnp.where((j == 0) & (block == 1), roll(bottom, 8, 1), 0.0)
    )
    new_bottom = (
        bottom
        + jnp.where(j == 0, roll(top, -56, 1), 0.0)
        + jnp.where((j == 7) & (block == 0), roll(top, -8, 1), 0.0)
    )
    if count == GROWS:
        ghost = u[ROWS:]
        new_top = new_top + jnp.where(lane < 8, roll(ghost, -56, 1), 0.0)
        new_bottom = new_bottom + jnp.where(lane >= 120, roll(ghost, 56, 1), 0.0)
    return jnp.concatenate([new_top, new_bottom], axis=0)


def ends(value):
    lane = lane_iota(HALF)
    return jnp.where(lane < 8, value[:HALF], jnp.where(lane >= 120, value[HALF:], 0.0))


def store_assembled(kv_ref, far_ref, near_ref, even, source, field=0, pack_ref=None):
    pack = None
    for i in range(NODES):
        value = own_assembly(source(i))
        kv_ref[i] = value
        if i == 0:
            first = value
        last = value
        if pack_ref is not None:
            piece = ends(value)
            if i:
                piece = roll(piece, 16 * i, 1)
            pack = piece if pack is None else pack + piece
    near_ref[field] = jnp.where(even, last, first)
    far_ref[field] = jnp.where(even, first, last)
    if pack_ref is not None:
        pack_ref[field] = pack


def is_even():
    return lax.broadcast_in_dim(lax.rem(lax.axis_index("ring"), 2), (ROWS, LANES), ()) == 0


def near_face(near_ref, field, even):
    if near_ref.ndim == 4:
        return jnp.where(even, near_ref[1, field], near_ref[0, field])
    return near_ref[field]


def pack_kernel(pack_in, far_ref, near_ref, pack_ref):
    even = is_even()
    for field in range(pack_ref.shape[0]):
        near, far = near_face(near_ref, field, even), far_ref[field]
        first = jnp.where(even, far, near)
        last = jnp.where(even, near, far)
        pack_ref[field, :HALF] = (
            pack_in[field] + ends(first) + roll(ends(last), 16 * (NODES - 1), 1)
        )
        if pack_ref.shape[1] > HALF:
            pack_ref[field, HALF:ROWS] = edge(first)
            pack_ref[field, ROWS:] = edge(last)


def pack_edges_kernel(step, pack_in, edges_in, inverse_ref, far_ref, near_ref, pack_ref):
    even = is_even()
    near, far = near_ref[0], far_ref[0]
    first = jnp.where(even, far, near)
    last = jnp.where(even, near, far)
    pack_ref[0, :HALF] = pack_in[0] + ends(first) + roll(ends(last), 16 * (NODES - 1), 1)
    zero = jnp.zeros((HALF, LANES), jnp.float32)
    for b in range(NODES // 2):
        lo, hi = edges_in[0, b], edges_in[1, b]
        if b == 0:
            add = packed_edges(edge(-step * inverse_ref[0] * first), zero)
            lo, hi = lo + add[0], hi + add[1]
        if b == NODES // 2 - 1:
            add = packed_edges(zero, edge(-step * inverse_ref[NODES - 1] * last))
            lo, hi = lo + add[0], hi + add[1]
        pack_ref[0, HALF * (1 + b) : HALF * (2 + b)] = lo
        pack_ref[0, HALF * (5 + b) : HALF * (6 + b)] = hi


WHOLE = (1, 3, 5)
LINES = (0, 2, 4, 6)


def line_pack(field):
    pack = None
    for i in range(NODES):
        piece = ends(field(i))
        if i:
            piece = roll(piece, 16 * i, 1)
        pack = piece if pack is None else pack + piece
    return pack


def ghost_lines(left, right):
    lane = lane_iota(HALF)
    both = jnp.where(lane % 16 >= 8, left, right)
    inner = (lane >= 56) & (lane < 72)
    return [jnp.where(inner, roll(both, 64 - 16 * i, 1), 0.0) for i in range(NODES)]


def beside(packs_ref):
    count = packs_ref.shape[0]
    here = lax.axis_index("narrow")
    return lax.rem(here + count - 1, count), lax.rem(here + 1, count)


def completed(kv, halo, field=0):
    far_ref, near_ref = halo[:2]
    even = is_even()
    near, far = near_face(near_ref, field, even), far_ref[field]
    lane = lane_iota(HALF)
    if len(halo) > 2:
        left, right = beside(halo[2])
        side = jnp.where(
            lane % 16 < 8,
            roll(halo[2][left, field, :HALF], 8, 1),
            roll(halo[2][right, field, :HALF], -8, 1),
        )

    def value(i):
        u = kv[i]
        if len(halo) > 2:
            piece = roll(side, -16 * i, 1) if i else side
            u = u + jnp.concatenate(
                [jnp.where(lane < 8, piece, 0.0), jnp.where(lane >= 120, piece, 0.0)], axis=0
            )
        if i == 0:
            u = u + jnp.where(even, far, near)
        if i == NODES - 1:
            u = u + jnp.where(even, near, far)
        return u

    return value


def ghost_sums(packs_ref, field=0, wide_too=False):
    left, right = beside(packs_ref)
    lane = lane_iota(HALF)
    own = packs_ref[lax.axis_index("narrow"), field, :HALF]
    lines = jnp.where(lane % 16 < 8, own, roll(own, 16, 1))
    inner = (lane >= 56) & (lane < 72)

    def value(i):
        u = jnp.where(inner, roll(lines, 56 - 16 * i, 1), 0.0)
        if wide_too and i in (0, NODES - 1):
            rows = slice(HALF, ROWS) if i == 0 else slice(ROWS, GROWS)
            u = u + facing(packs_ref[left, field, rows], packs_ref[right, field, rows])
        return u

    return value


def apply_flux(v_ref, metric_ref, ghost_ref, grad_ref, flux_ref, part_ref, with_energy=False):
    count = v_ref.shape[1]
    energy = jnp.zeros((8, LANES), jnp.float32)
    side = dot_grad(v_ref[...].reshape(NODES * count, LANES), grad_ref)
    flux_ref[0] = side[:, :LANES]
    flux_ref[1] = side[:, LANES:]
    for chunk in range(count // 8):
        rows = pl.ds(chunk * 8, 8)
        if chunk < ROWS // 8:
            geometry, there = metric_ref, rows
        else:
            geometry, there = ghost_ref, pl.ds(chunk * 8 - ROWS, 8)
        values = [v_ref[i, rows] for i in range(NODES)]
        grad_z = along_nodes(values, DERIV)
        flux_z = []
        for i in range(NODES):
            at = pl.ds(i * count + chunk * 8, 8)
            g_z, g_a, g_r = grad_z[i], flux_ref[0, at], flux_ref[1, at]
            m = [geometry[c, i, there] for c in range(6)]
            f_z = m[0] * g_z + m[3] * g_a + m[4] * g_r
            f_a = m[3] * g_z + m[1] * g_a + m[5] * g_r
            f_r = m[4] * g_z + m[5] * g_a + m[2] * g_r
            flux_z.append(f_z)
            flux_ref[0, at] = f_a
            flux_ref[1, at] = f_r
            if with_energy:
                energy = energy + (g_z * f_z + g_a * f_a + g_r * f_r)
        part_z = along_nodes(flux_z, DERIV.T)
        for i in range(NODES):
            screened = geometry[6, i, there] * values[i]
            part_ref[i, rows] = part_z[i] + screened
            if with_energy:
                energy = energy + screened * values[i]
    return energy


def whole_planes(flux_ref, part_ref, diver_ref, planes):
    count = part_ref.shape[1]

    def flux(f):
        if len(planes) == NODES:
            return flux_ref[f]
        return jnp.concatenate([flux_ref[f, i * count : (i + 1) * count] for i in planes], axis=0)

    total = dot_diver(jnp.concatenate([flux(0), flux(1)], axis=1), diver_ref)
    return [
        part_ref[i] + total[n * count : (n + 1) * count] for n, i in enumerate(planes)
    ]


def store_faces(flux_ref, part_ref, diver_ref, far_ref, near_ref):
    first, last = (
        own_assembly(u) for u in whole_planes(flux_ref, part_ref, diver_ref, (0, NODES - 1))
    )
    even = is_even()
    near_ref[0] = jnp.where(even, last, first)
    far_ref[0] = jnp.where(even, first, last)


def rest_kernel(flux_ref, part_ref, diver_ref, kv_ref):
    for i, u in enumerate(whole_planes(flux_ref, part_ref, diver_ref, range(NODES))):
        kv_ref[i] = own_assembly(u)


def rest_energy_kernel(flux_ref, part_ref, diver_ref, v_ref, sums_in, kv_ref, sums_ref):
    energy = jnp.zeros((ROWS, LANES), jnp.float32)
    for i, u in enumerate(whole_planes(flux_ref, part_ref, diver_ref, range(NODES))):
        kv_ref[i] = own_assembly(u)
        energy = energy + v_ref[i] * u[:ROWS]
    sums_ref[...] = sums_in[...] + sum_row([jnp.zeros((1, LANES), jnp.float32), energy])


def rest_edges_kernel(
    step, flux_ref, part_ref, diver_ref, start_ref, inverse_ref, kv_ref, pack_ref, edges_ref
):
    for i, u in enumerate(whole_planes(flux_ref, part_ref, diver_ref, range(NODES))):
        kv_ref[i] = own_assembly(u)
    pack_ref[0] = line_pack(lambda i: kv_ref[i])
    store_edges(
        edges_ref, edges_ref, 0, 1,
        [edge(start_ref[i] - step * inverse_ref[i] * kv_ref[i]) for i in range(NODES)],
    )


def weight_plane():
    lane, row = lane_iota(ROWS), row_iota(ROWS)
    j, k, er = (lane // 8) % 8, lane % 8, row % HALF
    w_a = jnp.where((j == 0) | (j == 7), 0.5, 1.0)
    shared = ((k == 0) & (er > 0)) | ((k == 7) & (er < HALF - 1))
    return w_a * jnp.where(shared, 0.5, 1.0)


def node_weight(i):
    return 0.5 if i in (0, NODES - 1) else 1.0


def sum_row(sums):
    lane = lane_iota(1)
    row = jnp.zeros((1, LANES), jnp.float32)
    for d, value in enumerate(sums):
        row = jnp.where(lane == d, jnp.sum(value), row)
    return row


SIGMA = ((INTERVAL_HIGH + INTERVAL_LOW) / 2.0) / ((INTERVAL_HIGH - INTERVAL_LOW) / 2.0)
CENTER = (INTERVAL_HIGH + INTERVAL_LOW) / 2.0
HALF_WIDTH = (INTERVAL_HIGH - INTERVAL_LOW) / 2.0
RHO0 = 1.0 / SIGMA
RHO1 = 1.0 / (2.0 * SIGMA - RHO0)
RHO2 = 1.0 / (2.0 * SIGMA - RHO1)


STEP1 = 2.0 * RHO1 / HALF_WIDTH
STEP2 = 2.0 * RHO2 / HALF_WIDTH


def place_kernel(
    order_hbm, load_hbm, geom_hbm, abs_hbm,
    metric_ref, load_kv, bound_kv, far_ref, near_ref, pack_ref, lo_ref, hi_ref,
    flux_ref, work_ref, order_ref, load_ref, geom_ref, abs_ref, sems,
):
    copies = [
        pltpu.make_async_copy(source, target, sems.at[c])
        for c, (source, target) in enumerate(
            [(order_hbm, order_ref), (load_hbm, load_ref), (geom_hbm, geom_ref), (abs_hbm, abs_ref)]
        )
    ]
    for copy in copies:
        copy.start()
    copies[0].wait()
    copies[1].wait()
    pick = jnp.where(
        lax.broadcasted_iota(jnp.int32, (64, 64), 0) == order_ref[...], 1.0, 0.0
    ).astype(jnp.bfloat16)
    low = lane_iota(ROWS) < 64

    def spread(placed, store):
        for b in range(4):
            piece = placed[:, b * LANES : (b + 1) * LANES]
            first, second = piece[:ROWS], piece[ROWS:]
            store(2 * b, jnp.where(low, first, roll(second, 64, 1)))
            store(2 * b + 1, jnp.where(low, roll(first, 64, 1), second))

    load = load_ref[...]
    high, rest = split(load)
    middle = (load - high.astype(jnp.float32) - rest.astype(jnp.float32)).astype(jnp.bfloat16)

    def store_load(i, value):
        work_ref[i] = value

    spread(dot(pick, high) + (dot(pick, rest) + dot(pick, middle)), store_load)
    even = is_even()
    store_assembled(
        load_kv, far_ref, near_ref, even, lambda i: work_ref[i], 0, pack_ref
    )
    store_edges(lo_ref, hi_ref, 3, 3, [edge(load_kv[i]) for i in range(NODES)])

    copies[2].wait()
    for c in range(7):

        def store_metric(i, value, c=c):
            metric_ref[c, i] = value

        spread(dot(pick, geom_ref[c]), store_metric)
    for slot, c in enumerate(WHOLE):
        store_edges(lo_ref, hi_ref, slot, slot, [edge(metric_ref[c, i]) for i in range(NODES)])
    for slot, c in enumerate(LINES):
        lines = line_pack(lambda i, c=c: metric_ref[c, i])
        lo_ref[5, slot] = lines
        hi_ref[5, slot] = lines

    lane = lane_iota(8)
    q_a = jnp.zeros((8, LANES), jnp.float32)
    q_r = jnp.zeros((8, LANES), jnp.float32)
    for m in range(NODES):
        q_a = jnp.where((lane // 8) % 8 == m, float(ROW_TOTAL[m]), q_a)
        q_r = jnp.where(lane % 8 == m, float(ROW_TOTAL[m]), q_r)
    for chunk in range(ROWS // 8):
        rows = pl.ds(chunk * 8, 8)
        h_z = []
        for i in range(NODES):
            at = pl.ds(i * ROWS + chunk * 8, 8)
            q_z = float(ROW_TOTAL[i])
            g = [jnp.abs(metric_ref[c, i, rows]) for c in range(6)]
            h_z.append(g[0] * q_z + g[3] * q_a + g[4] * q_r)
            flux_ref[0, at] = g[3] * q_z + g[1] * q_a + g[5] * q_r
            flux_ref[1, at] = g[4] * q_z + g[5] * q_a + g[2] * q_r
        part_z = along_nodes_plain(h_z, ABS_DERIV.T)
        for i in range(NODES):
            work_ref[i, rows] = part_z[i] + jnp.abs(metric_ref[6, i, rows])
    flux = jnp.concatenate([flux_ref[0], flux_ref[1]], axis=1)
    copies[3].wait()
    work_ref[...] += dot_split(flux, abs_ref).reshape(FIELD)
    store_assembled(
        bound_kv, far_ref, near_ref, even, lambda i: work_ref[i], 1, pack_ref
    )
    store_edges(lo_ref, hi_ref, 4, 4, [edge(bound_kv[i]) for i in range(NODES)])


def first_kernel(
    load_kv, bound_kv, h0, h1, h2, left_ref, right_ref, metric_ref, grad_ref, diver_ref,
    residual_ref, inverse_ref, update_ref, ghost_inverse, ghost_metric, flux_ref, part_ref, far_ref, near_ref,
    v_ref,
):
    residual = completed(load_kv, (h0, h1, h2), 0)
    bound = completed(bound_kv, (h0, h1, h2), 1)
    for i in range(NODES):
        r = residual(i)
        inverse = 1.0 / bound(i)
        update = r * inverse * (1.0 / CENTER)
        residual_ref[i] = r
        inverse_ref[i] = inverse
        update_ref[i] = update
        v_ref[i, :ROWS] = update
    residual, residual_sums = ghost_columns(left_ref[3], right_ref[3]), ghost_sums(h2, 0, True)
    bound, bound_sums = ghost_columns(left_ref[4], right_ref[4]), ghost_sums(h2, 1, True)
    for i in range(NODES):
        inverse = 1.0 / (bound[i] + bound_sums(i))
        ghost_inverse[i] = inverse
        v_ref[i, ROWS:] = (residual[i] + residual_sums(i)) * inverse * (1.0 / CENTER)
    for slot, c in enumerate(WHOLE):
        for i, value in enumerate(ghost_columns(left_ref[slot], right_ref[slot])):
            ghost_metric[c, i] = value
    for slot, c in enumerate(LINES):
        for i, value in enumerate(ghost_lines(left_ref[5, slot], right_ref[5, slot])):
            ghost_metric[c, i] = value
    apply_flux(v_ref, metric_ref, ghost_metric, grad_ref, flux_ref, part_ref)
    store_faces(flux_ref, part_ref, diver_ref, far_ref, near_ref)


def second_kernel(
    kv_in, h0, h1, source_ref, inverse_ref, update_in, metric_ref, grad_ref, diver_ref,
    start_ref, flux_ref, part_ref, far_ref, near_ref, v_ref,
):
    image = completed(kv_in, (h0, h1))
    for i in range(NODES):
        old = update_in[i]
        inverse = inverse_ref[i]
        source = source_ref[i]
        update = (RHO1 * RHO0) * old + STEP1 * inverse * (source - image(i))
        result = old + update
        v_ref[i] = result
        start_ref[i] = result + (RHO2 * RHO1) * update + STEP2 * inverse * source
    apply_flux(v_ref, metric_ref, None, grad_ref, flux_ref, part_ref)
    store_faces(flux_ref, part_ref, diver_ref, far_ref, near_ref)


def third_kernel(
    kv_in, h0, h1, h2, source_ref, inverse_ref, start_ref,
    ghost_inverse, ghost_metric, metric_ref, grad_ref, diver_ref,
    result_ref, flux_ref, part_ref, far_ref, near_ref, sums_ref, v_ref,
):
    image = completed(kv_in, (h0, h1, h2))
    plane = weight_plane()
    rz = jnp.zeros((ROWS, LANES), jnp.float32)
    for i in range(NODES):
        result = start_ref[i] - STEP2 * inverse_ref[i] * image(i)
        result_ref[i] = result
        v_ref[i, :ROWS] = result
        rz = rz + source_ref[i] * result * node_weight(i)
    start, sums = gathered_ghost(h2), ghost_sums(h2)
    for i in range(NODES):
        v_ref[i, ROWS:] = start[i] - STEP2 * ghost_inverse[i] * sums(i)
    apply_flux(v_ref, metric_ref, ghost_metric, grad_ref, flux_ref, part_ref)
    store_faces(flux_ref, part_ref, diver_ref, far_ref, near_ref)
    sums_ref[...] = sum_row([rz * plane])


def fourth_kernel(
    kv_in, h0, h1, inverse_ref, metric_ref, grad_ref, diver_ref,
    image_ref, update_ref, start_ref, flux_ref, part_ref, far_ref, near_ref,
):
    image = completed(kv_in, (h0, h1))
    for i in range(NODES):
        value = image(i)
        image_ref[i] = value
        update = value * inverse_ref[i] * (1.0 / CENTER)
        update_ref[i] = update
        start_ref[i] = (1.0 + RHO1 * RHO0 + STEP1 * CENTER) * update
    apply_flux(update_ref, metric_ref, None, grad_ref, flux_ref, part_ref)
    store_faces(flux_ref, part_ref, diver_ref, far_ref, near_ref)


def fifth_kernel(
    kv_in, h0, h1, h2, source_ref, inverse_ref, update_in,
    ghost_inverse, ghost_metric, metric_ref, grad_ref, diver_ref,
    start_ref, flux_ref, part_ref, far_ref, near_ref, v_ref,
):
    image = completed(kv_in, (h0, h1, h2))
    for i in range(NODES):
        old = update_in[i]
        inverse = inverse_ref[i]
        source = source_ref[i]
        update = (RHO1 * RHO0) * old + STEP1 * inverse * (source - image(i))
        result = old + update
        v_ref[i, :ROWS] = result
        start_ref[i] = result + (RHO2 * RHO1) * update + STEP2 * inverse * source
    start, sums = gathered_ghost(h2), ghost_sums(h2)
    for i in range(NODES):
        v_ref[i, ROWS:] = start[i] - STEP1 * ghost_inverse[i] * sums(i)
    apply_flux(v_ref, metric_ref, ghost_metric, grad_ref, flux_ref, part_ref)
    store_faces(flux_ref, part_ref, diver_ref, far_ref, near_ref)


def sixth_kernel(
    kv_in, h0, h1, source_ref, inverse_ref, start_ref, residual_ref, early_ref,
    metric_ref, grad_ref,
    result_ref, flux_ref, part_ref, sums_hbm, sums_ref, sem,
):
    image = completed(kv_in, (h0, h1))
    plane = weight_plane()
    r_y = jnp.zeros((ROWS, LANES), jnp.float32)
    w_y = jnp.zeros((ROWS, LANES), jnp.float32)
    for i in range(NODES):
        result = start_ref[i] - STEP2 * inverse_ref[i] * image(i)
        result_ref[i] = result
        r_y = r_y + residual_ref[i] * result * node_weight(i)
        w_y = w_y + source_ref[i] * result * node_weight(i)
    energy = apply_flux(
        result_ref, metric_ref, None, grad_ref, flux_ref, part_ref, with_energy=True
    )
    zero = jnp.zeros((1, LANES), jnp.float32)
    late = sum_row([zero, zero, r_y * plane, w_y * plane, energy])
    sums_ref[...] = jnp.broadcast_to(early_ref[...] + late, sums_ref.shape)
    leave = pltpu.make_async_copy(sums_ref, sums_hbm, sem)
    leave.start()
    leave.wait()


def rest_faces_kernel(flux_ref, part_ref, diver_ref, kv_ref, far_ref, near_ref, pack_ref):
    planes = whole_planes(flux_ref, part_ref, diver_ref, range(NODES))
    store_assembled(kv_ref, far_ref, near_ref, is_even(), lambda i: planes[i], 0, pack_ref)


def spread_fields(order_ref, fields, out_ref, spread_ref):
    low = lane_iota(ROWS) < 64
    pick = jnp.where(
        lax.broadcasted_iota(jnp.int32, (64, 64), 1) == order_ref[...], 1.0, 0.0
    ).astype(jnp.bfloat16)
    for f, field in enumerate(fields):
        for b in range(NODES // 2):
            even, odd = field(2 * b), field(2 * b + 1)
            lanes = pl.ds(b * LANES, LANES)
            spread_ref[:ROWS, lanes] = jnp.where(low, even, roll(odd, 64, 1))
            spread_ref[ROWS:, lanes] = jnp.where(low, roll(even, 64, 1), odd)
        value = spread_ref[...]
        high, middle = split(value)
        rest = (value - high.astype(jnp.float32) - middle.astype(jnp.float32)).astype(jnp.bfloat16)
        out_ref[f] = dot(pick, high) + (dot(pick, middle) + dot(pick, rest))


def spread_early_kernel(order_ref, first_ref, residual_ref, image_ref, out_ref, spread_ref):
    refs = (first_ref, residual_ref, image_ref)
    spread_fields(order_ref, [lambda i, ref=ref: ref[i] for ref in refs], out_ref, spread_ref)


def spread_late_kernel(kv_in, h0, h1, h2, second_ref, order_ref, out_ref, spread_ref):
    fields = [lambda i: second_ref[i], completed(kv_in, (h0, h1, h2))]
    spread_fields(order_ref, fields, out_ref, spread_ref)


def half_sum_kernel(rows_ref, out_ref):
    out_ref[...] = jnp.broadcast_to(
        jnp.sum(rows_ref[...], axis=0, keepdims=True), out_ref.shape
    )


def last_kernel(sums_ref, spread_ref, late_ref, solution_ref, residual_ref):
    sums = jnp.sum(sums_ref[...], axis=0)
    lane = lane_iota(1)

    def total(d):
        return jnp.sum(jnp.where(lane == d, sums, 0.0), axis=1, keepdims=True)

    rz0, zw, ry, wy, yq = (total(d) for d in range(5))
    alpha0 = rz0 / zw
    rz1 = rz0 - alpha0 * (zw + ry) + alpha0 * alpha0 * wy
    beta = rz1 / rz0
    share = 1.0 + beta
    energy = share * share * zw - 2.0 * share * alpha0 * wy + alpha0 * alpha0 * yq
    alpha1 = rz1 / energy
    first_scale = alpha0 + alpha1 * share
    second_scale = alpha1 * alpha0
    solution_ref[...] = first_scale * spread_ref[0] - second_scale * late_ref[0]
    residual_ref[...] = (
        spread_ref[1] - first_scale * spread_ref[2] + second_scale * late_ref[1]
    )


VMEM_LIMIT = 24 * 1024 * 1024
F32 = jnp.float32


def call(kernel, outs, scratch, *operands, space=pltpu.VMEM, out_spaces=None, cost=None):
    out_spaces = out_spaces or [pltpu.VMEM] * len(outs)
    return pl.pallas_call(
        kernel,
        out_shape=[jax.ShapeDtypeStruct(s, F32) for s in outs],
        in_specs=[pl.BlockSpec(memory_space=space)] * len(operands),
        out_specs=[pl.BlockSpec(memory_space=s) for s in out_spaces],
        scratch_shapes=[pltpu.VMEM(s, F32) if isinstance(s, tuple) else s for s in scratch],
        cost_estimate=cost,
        compiler_params=pltpu.CompilerParams(vmem_limit_bytes=VMEM_LIMIT),
    )(*operands)


FLUX = (2, NODES * ROWS, LANES)
COST = pl.CostEstimate(flops=10**11, transcendentals=0, bytes_accessed=10**8)
BIG_FLUX = (2, NODES * GROWS, LANES)


def faces(fields=1):
    return [(fields, ROWS, LANES), (fields, ROWS, LANES)]


def packs(fields=1):
    return [(fields, HALF, LANES)]


def swap_far(far):
    count = lax.axis_size(WIDE)
    return lax.ppermute(
        far, WIDE, [(w, (w + 1 if w % 2 else w - 1) % count) for w in range(count)]
    )


def swap_wide(far, near):
    count = lax.axis_size(WIDE)
    return swap_far(far), lax.ppermute(near, WIDE, [(w, w ^ 1) for w in range(count)])


def swap_all(far, near, pack, rows):
    far, near = swap_wide(far, near)
    (pack,) = call(pack_kernel, [(pack.shape[0], rows, LANES)], [], pack, far, near, cost=COST)
    return far, near, lax.all_gather(pack, "narrow")


def edges(fields):
    return (fields, NODES // 2, HALF, LANES)


def swap_edged(step, inverse, far, near, pack, edges_out):
    far, near = swap_wide(far, near)
    (pack,) = call(
        functools.partial(pack_edges_kernel, step),
        [(1, HALF * (1 + NODES), LANES)],
        [],
        pack, edges_out, inverse, far, near,
    )
    return far, near, lax.all_gather(pack, "narrow")


def swap_edges(lo, hi):
    count = lax.axis_size("narrow")
    left = lax.ppermute(hi, "narrow", [(n, (n + 1) % count) for n in range(count)])
    right = lax.ppermute(lo, "narrow", [(n, (n - 1) % count) for n in range(count)])
    return left, right


def local(load, geom, element_order):
    grad = jnp.asarray(GRAD_HL)
    diver = jnp.asarray(DIVER_HL)
    metric, load_kv, bound_kv, *face, lo, hi = call(
        place_kernel,
        [(7,) + FIELD, FIELD, FIELD] + faces(2) + packs(2) + [edges(6)] * 2,
        [
            FLUX, FIELD,
            pltpu.VMEM((1, 64), jnp.int32), pltpu.VMEM(load.shape, load.dtype),
            pltpu.VMEM(geom.shape, geom.dtype), pltpu.VMEM(ABS_HL.shape, jnp.bfloat16),
            pltpu.SemaphoreType.DMA((4,)),
        ],
        *(pltpu.with_memory_space_constraint(x, pltpu.HBM) for x in (element_order.reshape(1, 64), load, geom, jnp.asarray(ABS_HL))),
        space=pltpu.HBM,
    )
    sides = swap_edges(lo, hi)
    halo = swap_all(*face, GROWS)
    residual, inverse, update, ghost_inverse, ghost_metric, *parts, far, near = call(
        first_kernel,
        [FIELD, FIELD, FIELD, GHOST, (7,) + GHOST, BIG_FLUX, BIG] + faces(),
        [BIG],
        load_kv, bound_kv, *halo, *sides, metric, grad, diver,
    )
    (kv,) = call(rest_kernel, [FIELD], [], *parts, diver)
    halo = swap_wide(far, near)
    start, *parts, far, near = call(
        second_kernel,
        [FIELD, FLUX, FIELD] + faces(),
        [FIELD],
        kv, *halo, residual, inverse, update, metric, grad, diver,
    )
    kv, *side = call(
        functools.partial(rest_edges_kernel, STEP2),
        [FIELD] + packs() + [edges(2)],
        [],
        *parts, diver, start, inverse,
    )
    halo = swap_edged(STEP2, inverse, far, near, *side)
    first, *parts, far, near, early = call(
        third_kernel,
        [FIELD, BIG_FLUX, BIG] + faces() + [(1, LANES)],
        [BIG],
        kv, *halo, residual, inverse, start, ghost_inverse, ghost_metric, metric, grad, diver,
    )
    kv, early = call(rest_energy_kernel, [FIELD, (1, LANES)], [], *parts, diver, first, early)
    halo = swap_wide(far, near)
    image, update, start, *parts, far, near = call(
        fourth_kernel,
        [FIELD, FIELD, FIELD, FLUX, FIELD] + faces(),
        [],
        kv, *halo, inverse, metric, grad, diver,
    )
    kv, *side = call(
        functools.partial(rest_edges_kernel, STEP1),
        [FIELD] + packs() + [edges(2)],
        [],
        *parts, diver, start, inverse,
    )
    halo = swap_edged(STEP1, inverse, far, near, *side)
    start, *parts, far, near = call(
        fifth_kernel,
        [FIELD, BIG_FLUX, BIG] + faces(),
        [BIG],
        kv, *halo, image, inverse, update, ghost_inverse, ghost_metric, metric, grad, diver,
    )
    (kv,) = call(rest_kernel, [FIELD], [], *parts, diver)
    halo = swap_wide(far, near)
    order = element_order.reshape(64, 1)
    (spread,) = call(
        spread_early_kernel, [(3, 64, 512)], [(64, 512)], order, first, residual, image
    )
    kv, spread = lax.optimization_barrier((kv, spread))
    sums_shape = (lax.axis_size("ring"), LANES)
    second, *parts, sums = call(
        sixth_kernel,
        [FIELD, FLUX, FIELD, sums_shape],
        [sums_shape, pltpu.SemaphoreType.DMA(())],
        kv, *halo, image, inverse, start, residual, early, metric, grad,
        out_spaces=[pltpu.VMEM] * 3 + [pltpu.HBM],
    )
    sums = lax.all_to_all(sums[:, None], "ring", 0, 0)
    kv, far, near, pack = call(
        rest_faces_kernel, [FIELD] + faces() + packs(), [], *parts, diver
    )
    far = swap_far(far)
    ring = lax.axis_size("ring")
    (sums,) = call(half_sum_kernel, [(lax.axis_size(REST), 1, LANES)], [], sums)
    near, sums = lax.optimization_barrier((near, sums))
    sums = lax.all_to_all(sums, REST, 0, 0)
    near = lax.all_gather(
        near, "ring", axis_index_groups=[[v, v + 1] for v in range(0, ring, 2)]
    )
    (pack,) = call(pack_kernel, [pack.shape], [], pack, far, near)
    halo = far, near, lax.all_gather(pack, "narrow")
    (late,) = call(spread_late_kernel, [(2, 64, 512)], [(64, 512)], kv, *halo, second, order)
    return tuple(call(last_kernel, [(64, 512), (64, 512)], [], sums, spread, late))


def solution(mesh):
    wide, narrow = mesh.devices.shape
    ring = 12 if wide % 12 == 0 else 2
    fine = jax.sharding.Mesh(
        mesh.devices.reshape(wide // ring, ring, narrow), ("outer", "ring", "narrow")
    )
    rows = ("outer", "ring", "narrow")
    return jax.shard_map(
        local,
        mesh=fine,
        in_specs=(P(rows, None), P(None, rows, None), P(WIDE, "narrow", None)),
        out_specs=(P(rows, None), P(rows, None)),
        check_vma=False,
    )
```
